32 devices in a mesh: section: 2 (over core), dp: 16 (over z, y, x).
Axes of the slice: x: 2, y: 2, z: 4, core: 2. Of those that a mesh axis runs over, the one named last changes fastest.
Arguments:
- layer_input: bfloat16 [2, 2, 16, 512, 512], P('section', None, 'dp'), may hold values from -6 to 6
- cotangent: bfloat16 [2, 16, 512, 512], P(None, 'dp'), may hold values from -6 to 6
- lengths: int32 [2, 2, 16, 4], P(None, None, 'dp'), may hold values from 1 to 256, 512 in all within a row
- attn_qkv: bfloat16 [2, 512, 1536], P('section', 'dp'), may hold values from -0.25 to 0.25
- attn_out: bfloat16 [2, 512, 512], P('section', 'dp'), may hold values from -0.5 to 0.5
- cross_proj: bfloat16 [2, 512, 1024], P('section', 'dp'), may hold values from -0.25 to 0.25
- ffn_in: bfloat16 [2, 512, 2048], P('section', None, 'dp'), may hold values from -0.25 to 0.25
- ffn_out: bfloat16 [2, 2048, 512], P('section', 'dp'), may hold values from -0.125 to 0.125
- gains: bfloat16 [2, 3, 512], P('section', None, 'dp'), may hold values from 0.5 to 1.5
- alpha_raw: float32 [3, 8], replicated, may hold values from -3 to 3
Outputs:
- layer_output: bfloat16 [2, 2, 16, 512, 512], P('section', None, 'dp')
- input_grad: float32 [2, 2, 16, 512, 512], P('section', None, 'dp')
- qkv_grad: float32 [2, 512, 1536], P('section', 'dp')
- out_grad: float32 [2, 512, 512], P('section', 'dp')
- cross_grad: float32 [2, 512, 1024], P('section', 'dp')
- ffn_in_grad: float32 [2, 512, 2048], P('section', None, 'dp')
- ffn_out_grad: float32 [2, 2048, 512], P('section', 'dp')
- gain_grad: float32 [2, 3, 512], P('section', None, 'dp')
- alpha_grad: float32 [3, 8], replicated
The draws below stay inside these ranges and needn't reach their ends.
Inputs may be any that keep to these rules, and one draw needn't show every extreme that they name: In every row the largest of the 4 document lengths is 256.
All inputs are finite; a program needn't handle non-finite values.
Results may differ from the reference program's by a relative error of at most 0.03.
Values may be sent and summed in bfloat16 or wider, within the bound.
No kernel may reach another device: no remote copies, remote signals or barrier semaphores. Data moves between devices by JAX's collectives and lax.ppermute only.
A program may use at most 384 MiB of HBM per device.

```python
import math
import jax
import jax.numpy as jnp
import numpy as np
from jax import lax

D = 512
H = 8
HD = 64
FF = 2048
ROW = 512
MICRO = 2
DOCS = 4
NBIS = 24
ROWS = 16


def spiked(drawn, stream_key, source, target, blocks, factor):
    def block_of(position):
        return (jnp.arange(drawn.shape[position]) // (drawn.shape[position] // blocks)).reshape((-1,) + (1,) * (drawn.ndim - 1 - position))

    near = jax.random.permutation(stream_key, blocks)[block_of(target)]
    other_side = (block_of(target) + blocks // 2) % blocks
    return jnp.where((block_of(source) == near) | (block_of(source) == other_side), factor * drawn, drawn)


def block_levels(rng, extent, cuts, low, largest):
    def one(dim, parts):
        heights = jax.random.uniform(jax.random.fold_in(jax.random.fold_in(rng, 6), dim), (parts,), jnp.float32, low / len(cuts), largest / len(cuts))
        return jnp.repeat(jnp.exp(heights), extent[dim] // parts).reshape((-1,) + (1,) * (len(extent) - dim - 1))

    level = one(*cuts[0])
    for cut in cuts[1:]:
        level = level * one(*cut)
    return level


def profile(amount, total, bound, slope):
    weights = [(1 << 20) // math.isqrt(standing ** slope) + 1 for standing in range(2, amount + 1)]
    surplus, holding = total - bound - (amount - 1), [1] * (amount - 1)
    while surplus > 0:
        candidates = [i for i in range(amount - 1) if holding[i] < bound]
        whole, remaining = sum([weights[i] for i in candidates]), surplus
        for i in candidates:
            addition = min(bound - holding[i], max(1, remaining * weights[i] // whole), surplus)
            holding[i] = holding[i] + addition
            surplus = surplus - addition
    return np.array([bound] + holding)


def ragged(own_key, amount, total, bound, slope):
    if amount == 2:
        one = jax.random.randint(own_key, (), max(1, total - bound), min(bound, total - 1) + 1)
        return jnp.stack([one, total - one])
    sizes = jnp.asarray(profile(amount, total, bound, slope), jnp.int32)
    couples = (amount - 1) // 2
    giver, taker = sizes[1:1 + 2 * couples:2], sizes[2:2 + 2 * couples:2]
    room = jnp.minimum(giver - 1, bound - taker)
    moved = jax.random.randint(jax.random.fold_in(own_key, 1), (couples,), 0, 1 << 20) % (room + 1)
    sizes = sizes.at[1:1 + 2 * couples:2].set(giver - moved).at[2:2 + 2 * couples:2].set(taker + moved)
    return sizes[jax.random.permutation(jax.random.fold_in(own_key, 2), amount)]


def centred(own_key, shape, scale, bound, pieces=(), kind=jnp.bfloat16):
    values = jax.random.normal(own_key, shape, jnp.float32) * scale
    if len(pieces) > 0:
        values = block_levels(own_key, shape, pieces, -0.22, 0.18) * values
    return jnp.clip(values, min=-bound, max=bound).astype(kind)


def bell_draw_with(stream_key, extent, width, limit, cuts, heavy, kind=jnp.bfloat16):
    array = width * jax.random.normal(stream_key, extent, jnp.float32)
    if cuts:
        array = array * block_levels(stream_key, extent, cuts, -0.22, 0.18)
    return jnp.clip(spiked(array, jax.random.fold_in(stream_key, 3), *heavy), -limit, limit).astype(kind)


def setup_inputs(seed: int = 0) -> dict:
    key_of = jax.random.split(jax.random.key(seed), 11)
    return {
        "layer_input": bell_draw_with(key_of[0], (2, MICRO, ROWS, ROW, D), 1.0, 6.0, ((0, 2), (2, 16)), (2, 4, 16, 2.0)),
        "cotangent": centred(key_of[1], (MICRO, ROWS, ROW, D), 1.0, 6.0, ((1, 16),)),
        "lengths": jax.vmap(lambda own: ragged(own, DOCS, ROW, ROW // 2, 2))(jax.random.split(key_of[2], 2 * MICRO * ROWS)).reshape((2, MICRO, ROWS, DOCS)).astype(jnp.int32),
        "attn_qkv": centred(key_of[3], (2, D, 3 * D), D ** -0.5, 0.25, ((0, 2), (1, 16))),
        "attn_out": centred(key_of[4], (2, D, D), (D // 4) ** -0.5, 0.5, ((0, 2), (1, 16))),
        "cross_proj": centred(key_of[5], (2, D, 2 * D), D ** -0.5, 0.25, ((0, 2), (1, 16))),
        "ffn_in": centred(key_of[6], (2, D, FF), D ** -0.5, 0.25, ((0, 2), (2, 16))),
        "ffn_out": centred(key_of[7], (2, FF, D), FF ** -0.5, 0.125, ((0, 2), (1, 16))),
        "gains": jnp.clip(1.0 + 0.1 * jax.random.normal(key_of[8], (2, 3, D), jnp.float32), 0.5, 1.5).astype(jnp.bfloat16),
        "alpha_raw": jnp.clip(jax.random.uniform(key_of[9], (3, H), jnp.float32, -3.0, 3.0), -3.0, 3.0),
    }


@jax.custom_vjp
def low(v):
    return lax.optimization_barrier(v.astype(jnp.bfloat16)).astype(jnp.float32)

@jax.custom_vjp
def low_back(v):
    return v

def low_keep(v):
    return (low(v), None)

def low_pass(kept, grad):
    return (grad,)

def back_keep(v):
    return (v, None)

def back_low(kept, grad):
    return (low(grad),)
low.defvjp(low_keep, low_pass)
low_back.defvjp(back_keep, back_low)
SHARP = 0.0625
NEG = -1000000000.0
EPS = 1e-05
HIGH = lax.Precision.HIGHEST

def product(left, right):
    return jnp.dot(left, right, precision=HIGH, preferred_element_type=jnp.float32)

def layer_norm(stream, gain):
    center = lax.optimization_barrier(jnp.mean(stream, axis=-1, keepdims=True))
    shifted = stream - center
    spread_sq = lax.optimization_barrier(jnp.mean(shifted * shifted, axis=-1, keepdims=True))
    return shifted * lax.rsqrt(spread_sq + EPS) * gain

def doc_ids(row_lengths, count):
    ends = jnp.cumsum(row_lengths).astype(jnp.int32)
    places = jnp.arange(count, dtype=jnp.int32)
    return lax.optimization_barrier(jnp.sum((places[:, None] >= ends[None, :]).astype(jnp.int32), axis=1)).astype(jnp.int32)

def spread(gap, exponent, visible):
    positive = jnp.logical_and(visible, gap > 0)
    gap_safe = jnp.where(positive, gap, 1.0)
    return jnp.where(positive, gap_safe ** exponent, 0.0)

def entmax_attend(query_rows, key_rows, value_rows, visible, shrink):
    head_count = shrink.shape[0]
    row_count = query_rows.shape[0]
    key_count = key_rows.shape[0]
    query_h = query_rows.reshape(row_count, head_count, HD)
    key_h = key_rows.reshape(key_count, head_count, HD)
    value_h = value_rows.reshape(key_count, head_count, HD)
    scores = low_back(jnp.einsum('rhe,che->hrc', query_h, key_h, precision=HIGH) / math.sqrt(HD))
    slope_gate = shrink[:, None, None]
    exponent = 1.0 / slope_gate
    logits = jnp.where(visible[None], slope_gate * scores, NEG)
    peak = lax.optimization_barrier(jnp.max(logits, axis=2, keepdims=True))
    smooth_top = peak + SHARP * jnp.log(lax.optimization_barrier(jnp.sum(jnp.exp((logits - peak) / SHARP), axis=2, keepdims=True)))
    allowed = lax.optimization_barrier(jnp.sum(visible.astype(jnp.float32), axis=1))[None, :, None]
    bracket = 1.0 + SHARP * jnp.log(allowed)
    threshold = smooth_top - bracket
    for iteration in range(NBIS):
        bracket = bracket * 0.5
        candidate = threshold + bracket
        mass_sum = lax.optimization_barrier(jnp.sum(spread(logits - candidate, exponent, visible[None]), axis=2, keepdims=True))
        threshold = jnp.where(mass_sum >= 1.0, candidate, threshold)
    raw_weights = spread(logits - threshold, exponent, visible[None])
    weights = raw_weights / lax.optimization_barrier(jnp.sum(raw_weights, axis=2, keepdims=True))
    result = jnp.einsum('hrc,che->rhe', low(weights), value_h, precision=HIGH)
    return result.reshape(row_count, head_count * HD)

def encoder(stream, row_lengths, gain_rows, w_qkv, w_out, w_cross, w_in, w_down, shrink):
    token_docs = doc_ids(row_lengths, ROW)
    visible = token_docs[:, None] == token_docs[None, :]
    normed = low(layer_norm(stream, gain_rows[0]))
    projected = low(low_back(product(normed, w_qkv)))
    attended = low(low_back(entmax_attend(projected[:, :D], projected[:, D:2 * D], projected[:, 2 * D:], visible, shrink)))
    middle = stream + low_back(product(attended, w_out))
    hidden = low_back(product(low(layer_norm(middle, gain_rows[1])), w_in))
    activated = low(jax.nn.gelu(hidden, approximate=False))
    ending = middle + low_back(product(activated, w_down))
    memory = low(layer_norm(ending, gain_rows[2]))
    memory_pair = low(low_back(product(memory, w_cross)))
    return (memory, memory_pair)

def decoder(stream, row_lengths, source_lengths, memory_pair, gain_rows, w_qkv, w_out, w_cross, w_in, w_down, shrink_self, shrink_cross):
    token_docs = doc_ids(row_lengths, ROW)
    source_docs = doc_ids(source_lengths, ROW)
    places = jnp.arange(ROW, dtype=jnp.int32)
    visible = jnp.logical_and(token_docs[:, None] == token_docs[None, :], places[:, None] >= places[None, :])
    normed = low(layer_norm(stream, gain_rows[0]))
    projected = low(low_back(product(normed, w_qkv)))
    attended = low(low_back(entmax_attend(projected[:, :D], projected[:, D:2 * D], projected[:, 2 * D:], visible, shrink_self)))
    middle = stream + low_back(product(attended, w_out))
    cross_query = low(low_back(product(low(layer_norm(middle, gain_rows[1])), w_cross[:, :D])))
    cross_visible = token_docs[:, None] == source_docs[None, :]
    crossed = low(low_back(entmax_attend(cross_query, memory_pair[:, :D], memory_pair[:, D:], cross_visible, shrink_cross)))
    second = middle + low_back(product(crossed, w_cross[:, D:]))
    hidden = low_back(product(low(layer_norm(second, gain_rows[2])), w_in))
    activated = low(jax.nn.gelu(hidden, approximate=False))
    return second + low_back(product(activated, w_down))

def reference(layer_input, cotangent, lengths, attn_qkv, attn_out, cross_proj, ffn_in, ffn_out, gains, alpha_raw):
    row_total = MICRO * ROWS
    inputs = layer_input.astype(jnp.float32)
    weights = tuple((item.astype(jnp.float32) for item in (attn_qkv, attn_out, cross_proj, ffn_in, ffn_out, gains)))
    row_lengths = lengths.reshape(2, row_total, DOCS)

    def forward(streams, w_qkv, w_out, w_cross, w_in, w_down, w_gain, raw_alpha):
        shrink = 0.25 + 0.25 * jax.nn.sigmoid(raw_alpha)
        source = streams[0].reshape(row_total, ROW, D)
        target = streams[1].reshape(row_total, ROW, D)

        def one_row(running, row_item):
            source_row, target_row, source_len, target_len = row_item
            memory, memory_pair = encoder(source_row, source_len, w_gain[0], w_qkv[0], w_out[0], w_cross[0], w_in[0], w_down[0], shrink[0])
            result = decoder(target_row, target_len, source_len, memory_pair, w_gain[1], w_qkv[1], w_out[1], w_cross[1], w_in[1], w_down[1], shrink[1], shrink[2])
            return (running, (memory, result))
        running, (memories, results) = lax.scan(jax.checkpoint(one_row), jnp.zeros((), jnp.float32), (source, target, row_lengths[0], row_lengths[1]))
        return jnp.stack([memories, results]).reshape(2, MICRO, ROWS, ROW, D)
    outputs, pull_back = jax.vjp(forward, inputs, *weights, alpha_raw)
    seed_grad = jnp.stack([jnp.zeros(cotangent.shape, jnp.float32), cotangent.astype(jnp.float32)])
    gradients = pull_back(seed_grad)
    return (outputs.astype(jnp.bfloat16), gradients[0], gradients[1], gradients[2], gradients[3], gradients[4], gradients[5], gradients[6], gradients[7])
```

```python
import functools
import math

import jax
import jax.numpy as jnp
import numpy as np
from jax import lax
from jax.experimental import pallas as pl
from jax.experimental.pallas import tpu as pltpu
from jax.sharding import PartitionSpec as P

SHARP = 0.0625
NEG = -1e9
EPS = 1e-5
TINY = 1e-37
LOG2E = 1.4426950408889634
NEWTON = 7
CHUNK = 64
TILE = 128
BLOCKS = 16
MB = 1 << 20
F32, BF16 = jnp.float32, jnp.bfloat16
WHOLE = pl.BlockSpec(memory_space=pltpu.VMEM)
TABLE = pl.BlockSpec(memory_space=pltpu.SMEM)
AWAY = pl.BlockSpec(memory_space=pl.ANY)


def mm(a, b):
    return jnp.dot(a, b, preferred_element_type=F32)


def mm_nt(a, b):
    return lax.dot_general(a, b, (((1,), (1,)), ((), ())), preferred_element_type=F32)


def mm_tn(a, b):
    return lax.dot_general(a, b, (((0,), (0,)), ((), ())), preferred_element_type=F32)


def low(v):
    return v.astype(BF16)


def fold(block):
    return jnp.sum(block.reshape(block.shape[0] // 8, 8, block.shape[1]), axis=0)


def fold_max(block):
    return jnp.max(block.reshape(block.shape[0] // 8, 8, block.shape[1]), axis=0)


def rows_of(parts, op):
    return jnp.concatenate([op(part, axis=0, keepdims=True) for part in parts], axis=0)


def per_head(coef, which, heads):
    place = lax.broadcasted_iota(jnp.int32, (heads, TILE), 0)
    out = jnp.zeros((heads, TILE), F32)
    for h in range(heads):
        out = jnp.where(place == h, coef[which, h], out)
    return out


def bias_of(lo, hi, start):
    place = lax.broadcasted_iota(jnp.int32, (CHUNK, TILE), 0) + start
    return jnp.where(jnp.logical_and(place >= lo, place < hi), 0.0, NEG)


def pair_of(h, width):
    return slice(h // 2 * 2 * width, (h // 2 + 1) * 2 * width)


def split_pairs(dst, turned, heads, width):
    for h in range(heads):
        block = turned[pair_of(h, width), :]
        mine = lax.broadcasted_iota(jnp.int32, block.shape, 0) // width == h % 2
        dst[h] = jnp.where(mine, block, jnp.zeros_like(block))


def attend_kernel(
    span, coef, lo_ref, hi_ref, q_ref, k_ref, v_ref, o_ref, tau_ref, top_ref, inv_ref, v_t, zs, ps, qz
):
    heads, keys = zs.shape[0], zs.shape[1]
    width = q_ref.shape[1] // heads
    tile = pl.program_id(0)

    @pl.when(tile == 0)
    def _():
        v_t[...] = v_ref[...].T

    split_pairs(qz, q_ref[...].T, heads, width)
    lo, hi = lo_ref[...], hi_ref[...]
    first, last = span[0, tile], span[1, tile]

    def scores(c, tops):
        start = pl.multiple_of(c * CHUNK, CHUNK)
        bias = bias_of(lo, hi, start)
        out = []
        for h in range(heads):
            z = mm(k_ref[pl.ds(start, CHUNK), pair_of(h, width)], qz[h]) * coef[0, h] + bias
            zs[h, pl.ds(start, CHUNK), :] = z
            out.append(jnp.maximum(tops[h], fold_max(z)))
        return tuple(out)

    tops = lax.fori_loop(
        first, last, scores, tuple(jnp.full((8, TILE), -3e38, F32) for _ in range(heads))
    )
    peak = rows_of(tops, jnp.max)
    power = 1.0 - per_head(coef, 1, heads)
    zero = tuple(jnp.zeros((8, TILE), F32) for _ in range(2 * heads))

    def newton(_, tau):
        def body(c, sums):
            start = pl.multiple_of(c * CHUNK, CHUNK)
            out = []
            for h in range(heads):
                u = jnp.maximum(zs[h, pl.ds(start, CHUNK), :] - tau[h : h + 1, :], TINY)
                lower = jnp.exp2(jnp.log2(u) * coef[2, h])
                out += [sums[2 * h] + fold(lower * u), sums[2 * h + 1] + fold(lower)]
            return tuple(out)

        sums = lax.fori_loop(first, last, body, zero)
        mass, slope = rows_of(sums[0::2], jnp.sum), rows_of(sums[1::2], jnp.sum)
        return tau + (mass - jnp.exp2(power * jnp.log2(mass))) / slope

    tau = lax.fori_loop(0, NEWTON, newton, peak - 1.0)

    def blank(c, carry):
        start = pl.multiple_of(c * CHUNK, CHUNK)
        for h in range(heads):
            ps[h, pl.ds(start, CHUNK), :] = jnp.zeros((CHUNK, TILE), BF16)
        return carry

    lax.fori_loop(0, first, blank, 0)
    lax.fori_loop(last, keys // CHUNK, blank, 0)

    def final(c, sums):
        start = pl.multiple_of(c * CHUNK, CHUNK)
        out = []
        for h in range(heads):
            z = zs[h, pl.ds(start, CHUNK), :]
            u = jnp.maximum(z - tau[h : h + 1, :], TINY)
            p = jnp.exp2(jnp.log2(u) * coef[2, h]) * u
            ps[h, pl.ds(start, CHUNK), :] = low(p)
            soft = jnp.exp2((z - peak[h : h + 1, :]) * (LOG2E / SHARP))
            out += [sums[2 * h] + fold(p), sums[2 * h + 1] + fold(soft)]
        return tuple(out)

    sums = lax.fori_loop(first, last, final, zero)
    inv = 1.0 / rows_of(sums[0::2], jnp.sum)
    tau_ref[...] = tau
    top_ref[...] = peak + SHARP * jnp.log(rows_of(sums[1::2], jnp.sum))
    inv_ref[...] = inv
    for h in range(0, heads, 2):
        got = [
            mm(v_t[i * width : (i + 1) * width, :], ps[i]) * inv[i : i + 1, :] for i in (h, h + 1)
        ]
        o_ref[:, pair_of(h, width)] = low(jnp.concatenate(got, axis=0).T)


def attend(q, k, v, marks, coef):
    lo, hi, span = marks
    rows, width = q.shape
    keys, heads = k.shape[0], coef.shape[1]
    line = pl.BlockSpec((1, TILE), lambda t, *_: (0, t))
    tile = pl.BlockSpec((TILE, width), lambda t, *_: (t, 0))
    stat = pl.BlockSpec((heads, TILE), lambda t, *_: (0, t))
    full = pl.BlockSpec((keys, width), lambda t, *_: (0, 0))
    return pl.pallas_call(
        attend_kernel,
        grid_spec=pltpu.PrefetchScalarGridSpec(
            num_scalar_prefetch=2,
            grid=(rows // TILE,),
            in_specs=[line, line, tile, full, full],
            out_specs=[tile, stat, stat, stat],
            scratch_shapes=[
                pltpu.VMEM((width, keys), BF16),
                pltpu.VMEM((heads, keys, TILE), F32),
                pltpu.VMEM((heads, keys, TILE), BF16),
                pltpu.VMEM((heads, 2 * width // heads, TILE), BF16),
            ],
        ),
        out_shape=[jax.ShapeDtypeStruct((rows, width), BF16)]
        + [jax.ShapeDtypeStruct((heads, rows), F32)] * 3,
        compiler_params=pltpu.CompilerParams(vmem_limit_bytes=24 * MB),
        cost_estimate=pl.CostEstimate(
            flops=4 * rows * keys * width, bytes_accessed=4 * MB, transcendentals=heads * rows * keys * 8
        ),
        name="attend",
    )(span, coef, lo, hi, q, k, v)


def attend_back_kernel(
    span, coef, lo_ref, hi_ref, q_ref, go_ref, tau_ref, top_ref, inv_ref, q_all, go_all, k_ref, v_ref,
    dq_ref, dk_ref, dv_ref, ds_ref, k_t, zs, gs, ls, qz, gz, g_all, p_all,
):
    heads, keys = zs.shape[0], zs.shape[1]
    width = q_ref.shape[1] // heads
    scale = 1.0 / math.sqrt(width)
    tile = pl.program_id(0)
    at = pl.multiple_of(tile * TILE, TILE)

    @pl.when(tile == 0)
    def _():
        k_t[...] = k_ref[...].T
        ds_ref[...] = jnp.zeros_like(ds_ref)

    split_pairs(qz, q_ref[...].T, heads, width)
    split_pairs(gz, go_ref[...].T, heads, width)
    lo, hi = lo_ref[...], hi_ref[...]
    tau, top, inv = tau_ref[...], top_ref[...], inv_ref[...]
    first, last = span[0, tile], span[1, tile]
    kinds = 5
    zero = tuple(jnp.zeros((8, TILE), F32) for _ in range(kinds * heads))

    def gather(c, sums):
        start = pl.multiple_of(c * CHUNK, CHUNK)
        here = pl.ds(start, CHUNK)
        bias = bias_of(lo, hi, start)
        out = []
        for h in range(heads):
            z = mm(k_ref[here, pair_of(h, width)], qz[h]) * coef[0, h] + bias
            g = mm(v_ref[here, pair_of(h, width)], gz[h])
            u = jnp.maximum(z - tau[h : h + 1, :], TINY)
            log_u = jnp.log2(u)
            lower = jnp.exp2(log_u * coef[2, h])
            p = lower * u
            p_log = p * log_u
            zs[h, here, :] = z
            gs[h, here, :] = g
            ls[h, here, :] = lower
            new = (g * p, g * lower, lower, g * p_log, p_log)
            out += [sums[kinds * h + i] + fold(new[i]) for i in range(kinds)]
        return tuple(out)

    sums = lax.fori_loop(first, last, gather, zero)
    gp, gl, ll, gpl, pl_sum = (rows_of(sums[i::kinds], jnp.sum) for i in range(kinds))
    shrink = per_head(coef, 1, heads)
    inv_k = per_head(coef, 3, heads) * inv
    mean = gp * inv
    drop = inv_k * (gl - mean * ll)
    grad_k = inv * (gpl - mean * pl_sum) * (1.0 / LOG2E)

    def blank(c, carry):
        start = pl.multiple_of(c * CHUNK, CHUNK)
        for h in range(heads):
            g_all[h, pl.ds(start, CHUNK), pl.ds(at, TILE)] = jnp.zeros((CHUNK, TILE), BF16)
            p_all[h, pl.ds(start, CHUNK), pl.ds(at, TILE)] = jnp.zeros((CHUNK, TILE), BF16)
        return carry

    lax.fori_loop(0, first, blank, 0)
    lax.fori_loop(last, keys // CHUNK, blank, 0)

    def final(c, sums):
        here = pl.ds(pl.multiple_of(c * CHUNK, CHUNK), CHUNK)
        out = []
        for h in range(heads):
            one = slice(h, h + 1)
            z, lower = zs[h, here, :], ls[h, here, :]
            p = lower * jnp.maximum(z - tau[one], TINY)
            r = (gs[h, here, :] - mean[one]) * lower * inv_k[one]
            g_z = r - drop[one] * jnp.exp2((z - top[one]) * (LOG2E / SHARP))
            g_all[h, here, pl.ds(at, TILE)] = low(g_z * coef[1, h])
            p_all[h, here, pl.ds(at, TILE)] = low(p * inv[one])
            out.append(sums[h] + fold(g_z * z))
        return tuple(out)

    sums = lax.fori_loop(first, last, final, zero[:heads])
    ds_ref[...] += rows_of(sums, jnp.sum) / shrink - grad_k / (shrink * shrink)
    for h in range(0, heads, 2):
        got = [
            mm(k_t[i * width : (i + 1) * width, :], g_all[i, :, pl.ds(at, TILE)]) for i in (h, h + 1)
        ]
        dq_ref[:, pair_of(h, width)] = low(jnp.concatenate(got, axis=0).T * scale)

    @pl.when(tile == pl.num_programs(0) - 1)
    def _():
        rows = q_all.shape[0]
        lane = lax.broadcasted_iota(jnp.int32, (rows, 2 * width), 1) // width
        blank_rows = jnp.zeros((rows, 2 * width), BF16)
        for h in range(0, heads, 2):
            cols = pair_of(h, width)
            dk, dv = 0.0, 0.0
            for i in (h, h + 1):
                dk += mm(g_all[i], jnp.where(lane == i % 2, q_all[:, cols], blank_rows))
                dv += mm(p_all[i], jnp.where(lane == i % 2, go_all[:, cols], blank_rows))
            dk_ref[:, cols] = low(dk * scale)
            dv_ref[:, cols] = low(dv)


def attend_back(q, k, v, go, stats, marks, coef):
    lo, hi, span = marks
    rows, width = q.shape
    keys, heads = k.shape[0], coef.shape[1]
    line = pl.BlockSpec((1, TILE), lambda t, *_: (0, t))
    tile = pl.BlockSpec((TILE, width), lambda t, *_: (t, 0))
    stat = pl.BlockSpec((heads, TILE), lambda t, *_: (0, t))
    q_full = pl.BlockSpec((rows, width), lambda t, *_: (0, 0))
    k_full = pl.BlockSpec((keys, width), lambda t, *_: (0, 0))
    return pl.pallas_call(
        attend_back_kernel,
        grid_spec=pltpu.PrefetchScalarGridSpec(
            num_scalar_prefetch=2,
            grid=(rows // TILE,),
            in_specs=[line, line, tile, tile, stat, stat, stat, q_full, q_full, k_full, k_full],
            out_specs=[tile, k_full, k_full, pl.BlockSpec((heads, TILE), lambda t, *_: (0, 0))],
            scratch_shapes=[pltpu.VMEM((width, keys), BF16)]
            + [pltpu.VMEM((heads, keys, TILE), F32)] * 3
            + [pltpu.VMEM((heads, 2 * width // heads, TILE), BF16)] * 2
            + [pltpu.VMEM((heads, keys, rows), BF16)] * 2,
        ),
        out_shape=[
            jax.ShapeDtypeStruct((rows, width), BF16),
            jax.ShapeDtypeStruct((keys, width), BF16),
            jax.ShapeDtypeStruct((keys, width), BF16),
            jax.ShapeDtypeStruct((heads, TILE), F32),
        ],
        compiler_params=pltpu.CompilerParams(vmem_limit_bytes=32 * MB),
        cost_estimate=pl.CostEstimate(
            flops=10 * rows * keys * width, bytes_accessed=6 * MB, transcendentals=heads * rows * keys * 3
        ),
        name="attend_back",
    )(span, coef, lo, hi, q, go, *stats, q, go, k, v)


def marks_of(q_lengths, k_lengths, rows, causal):
    q_end, k_end = jnp.cumsum(q_lengths), jnp.cumsum(k_lengths)
    places = jnp.arange(rows, dtype=jnp.int32)
    doc = jnp.sum((places[:, None] >= q_end[None, :]).astype(jnp.int32), axis=1)
    pick = doc[:, None] == jnp.arange(q_lengths.shape[0])[None, :]
    hi = jnp.sum(jnp.where(pick, k_end[None, :], 0), axis=1)
    lo = jnp.sum(jnp.where(pick, (k_end - k_lengths)[None, :], 0), axis=1)
    if causal:
        hi = jnp.minimum(hi, places + 1)
    first = jnp.min(lo.reshape(-1, TILE), axis=1) // CHUNK
    last = (jnp.max(hi.reshape(-1, TILE), axis=1) + CHUNK - 1) // CHUNK
    return (lo[None], hi[None], jnp.stack([first, last]))


def coefs_of(shrink, width):
    exponent = 1.0 / shrink
    return jnp.stack([shrink / math.sqrt(width), shrink, exponent - 1.0, exponent])


OUT, CROSS, DOWN, IN, SECOND = 0, 32, 96, 224, 352
QKV, GAIN, FIRST = 0, 96, 112


def pack_first(qkv, gains_rows):
    width = qkv.shape[-1] // 3
    parts = [qkv[:, i * width : (i + 1) * width] for i in range(3)]
    return jnp.concatenate(parts + [gains_rows], axis=0)


def pack_second(out, cross, down, inner):
    width = out.shape[-1]
    quarter = inner.shape[0] // 4
    turned = inner.reshape(4, quarter, inner.shape[1]).transpose(1, 0, 2).reshape(quarter, -1)
    return jnp.concatenate([out, cross[:, :width], cross[:, width:], down, turned], axis=0)


def rows_at(block, rows):
    return pl.ds(pl.multiple_of(block * rows, rows), rows)


def start_rows(src, block_of, dst, dst_block, rows, offset, cols, sem):
    pltpu.make_async_copy(
        src.at[block_of, pl.ds(offset, rows), :], dst.at[rows_at(dst_block, rows), cols], sem
    ).start()


def start_inner(src, block, dst, sem):
    cols = rows_at(block, 128)
    for i in range(4):
        pltpu.make_async_copy(
            src.at[block, pl.ds(IN, 128), pl.ds(128 * i, 128)], dst.at[pl.ds(128 * i, 128), cols], sem
        ).start()


def wait_for(ref, sem):
    pltpu.make_async_copy(ref, ref, sem).wait()


def fetch_out(src, dst, sem):
    @pl.loop(0, BLOCKS)
    def _(j):
        start_rows(src, j, dst, j, 32, OUT, slice(None), sem)


def fetch_cross(src, dst, sem, which):
    @pl.loop(0, BLOCKS)
    def _(j):
        for n, i in enumerate(which):
            start_rows(src, j, dst, j, 32, CROSS + 32 * i, pl.ds(512 * n, 512), sem)


def fetch_ffn(src, inner, down, sems):
    @pl.loop(0, BLOCKS)
    def _(j):
        start_inner(src, j, inner, sems.at[0])

    @pl.loop(0, BLOCKS)
    def _(j):
        start_rows(src, j, down, j, 128, DOWN, slice(None), sems.at[1])


def stage_rows(stage, offset, grad):
    for j in range(BLOCKS):
        for h in range(2):
            stage[h, j, offset : offset + 16, :] = grad[32 * j + 16 * h : 32 * j + 16 * h + 16, :]


def stage_down(stage, offset, c, grad):
    for j in range(4):
        for h in range(2):
            at = 128 * j + 64 * h
            stage[h, 4 * c + j, offset : offset + 64, :] = grad[at : at + 64, :]


def stage_inner(stage, offset, c, grad):
    for j in range(4):
        for h in range(2):
            for i in range(4):
                at = 256 * h + 64 * i
                stage[h, 4 * c + j, offset : offset + 64, 128 * i : 128 * (i + 1)] = grad[
                    at : at + 64, 128 * j : 128 * (j + 1)
                ]


def send_stage(stage, dst, place, sem):
    for h in range(2):

        @pl.loop(0, BLOCKS)
        def _(j):
            pltpu.make_async_copy(stage.at[h, j], dst.at[place[2, h], place[h, j]], sem).start()


STEP = 64


def each_rows(rows, body):
    @pl.loop(0, rows // STEP)
    def _(i):
        body(pl.ds(pl.multiple_of(i * STEP, STEP), STEP))


def centred(v):
    shifted = v - jnp.mean(v, axis=-1, keepdims=True)
    rate = lax.rsqrt(jnp.mean(shifted * shifted, axis=-1, keepdims=True) + EPS)
    return shifted * rate, rate


def norm_back(v, gain, grad):
    unit, rate = centred(v)
    e = grad * gain
    back = e - jnp.mean(e, axis=-1, keepdims=True) - unit * jnp.mean(e * unit, axis=-1, keepdims=True)
    return back * rate, fold(grad * unit)


def gelu_parts(u):
    phi = 0.5 + 0.5 * lax.erf(u * (1.0 / math.sqrt(2.0)))
    bell = jnp.exp2(u * u * (-0.5 * LOG2E)) * (1.0 / math.sqrt(2.0 * math.pi))
    return u * phi, phi + u * bell


def front_kernel(
    table, x_e, x_d, own, other, n_e, q_e, k_e, v_e, n_d, q_d, k_d, v_d, g_e, g_d, w, gs, prod, sems
):
    for which, src in enumerate((own, other)):
        section = table[2, 0] if which == 0 else 1 - table[2, 0]

        @pl.loop(0, BLOCKS)
        def _(p):
            j = table[which, p]
            for i in range(3):
                start_rows(src, p, w.at[section], j, 32, 32 * i, pl.ds(512 * i, 512), sems.at[section])
            pltpu.make_async_copy(src.at[p, pl.ds(GAIN, 16), :], gs.at[section, p], sems.at[section]).start()

    for section, (x, g, n, q, k, v) in enumerate(
        ((x_e, g_e, n_e, q_e, k_e, v_e), (x_d, g_d, n_d, q_d, k_d, v_d))
    ):
        wait_for(w.at[section], sems.at[section])
        wait_for(gs.at[section], sems.at[section])
        gains = jnp.sum(gs[section].astype(F32), axis=0)[0:8]
        g[...] = gains

        def body(rows, x=x, n=n, gain=gains[0:1]):
            n[rows, :] = low(centred(x[rows, :].astype(F32))[0] * gain)

        each_rows(x.shape[0], body)
        for i, out in enumerate((q, k, v)):
            prod[...] = mm(n[...], w[section, :, 512 * i : 512 * (i + 1)])

            def keep(rows, out=out):
                out[rows, :] = low(prod[rows, :])

            each_rows(x.shape[0], keep)


def front(table, x_e, x_d, own, other):
    rows, width = x_e.shape
    row16 = jax.ShapeDtypeStruct((rows, width), BF16)
    gain = jax.ShapeDtypeStruct((8, width), F32)
    return pl.pallas_call(
        front_kernel,
        in_specs=[TABLE, WHOLE, WHOLE, AWAY, AWAY],
        out_specs=[WHOLE] * 10,
        out_shape=[row16] * 8 + [gain] * 2,
        scratch_shapes=[
            pltpu.VMEM((2, width, 3 * width), BF16),
            pltpu.VMEM((2, BLOCKS, 16, width), BF16),
            pltpu.VMEM((rows, width), F32),
            pltpu.SemaphoreType.DMA((2,)),
        ],
        compiler_params=pltpu.CompilerParams(vmem_limit_bytes=24 * MB),
        cost_estimate=pl.CostEstimate(flops=12 * rows * width * width, bytes_accessed=8 * MB, transcendentals=0),
        name="front",
    )(table, x_e, x_d, own, other)


def mid_kernel(
    a_e, a_d, x_e, x_d, g_e, g_d, pack,
    m_e, n_e, act, slope, end, memory, mem_k, mem_v, m_d, n_d, query,
    w_out, w_in, w_down, w_cross, w_query, prod, total, sems,
):
    enc, dec = pack.at[0], pack.at[1]
    fetch_out(enc, w_out.at[0], sems.at[0])
    fetch_ffn(enc, w_in, w_down, sems.at[pl.ds(1, 2)])
    fetch_out(dec, w_out.at[1], sems.at[3])
    fetch_cross(enc, w_cross, sems.at[4], (0, 1))
    fetch_cross(dec, w_query, sems.at[5], (0,))
    count = x_e.shape[0]

    def attended(a, x, g, m, n, section, sem):
        wait_for(w_out.at[section], sem)
        prod[...] = mm(a[...], w_out[section])
        gain = g[1:2, :]

        def body(rows):
            middle = x[rows, :].astype(F32) + prod[rows, :]
            m[rows, :] = middle
            n[rows, :] = low(centred(middle)[0] * gain)

        each_rows(count, body)

    attended(a_e, x_e, g_e, m_e, n_e, 0, sems.at[0])
    wait_for(w_in, sems.at[1])
    wait_for(w_down, sems.at[2])
    total[...] = m_e[...]

    @pl.loop(0, 4)
    def _(c):
        cols = rows_at(c, 512)
        prod[...] = mm(n_e[...], w_in[:, cols])

        def body(rows):
            value, rate = gelu_parts(prod[rows, :])
            act[rows, cols] = low(value)
            slope[rows, cols] = low(rate)

        each_rows(count, body)
        total[...] += mm(act[:, cols], w_down[cols, :])

    gain = g_e[2:3, :]

    def body(rows):
        ending = total[rows, :]
        end[rows, :] = ending
        memory[rows, :] = low(centred(ending)[0] * gain)

    each_rows(count, body)
    wait_for(w_cross, sems.at[4])
    mem_k[...] = low(mm(memory[...], w_cross[:, 0:512]))
    mem_v[...] = low(mm(memory[...], w_cross[:, 512:1024]))
    attended(a_d, x_d, g_d, m_d, n_d, 1, sems.at[3])
    wait_for(w_query, sems.at[5])
    query[...] = low(mm(n_d[...], w_query[...]))


def mid(a_e, a_d, x_e, x_d, g_e, g_d, pack):
    rows, width = x_e.shape
    row16 = jax.ShapeDtypeStruct((rows, width), BF16)
    row32 = jax.ShapeDtypeStruct((rows, width), F32)
    wide = jax.ShapeDtypeStruct((rows, 4 * width), BF16)
    return pl.pallas_call(
        mid_kernel,
        in_specs=[WHOLE] * 6 + [AWAY],
        out_specs=[WHOLE] * 11,
        out_shape=[row32, row16, wide, wide, row32, row16, row16, row16, row32, row16, row16],
        scratch_shapes=[
            pltpu.VMEM((2, width, width), BF16),
            pltpu.VMEM((width, 4 * width), BF16),
            pltpu.VMEM((4 * width, width), BF16),
            pltpu.VMEM((width, 2 * width), BF16),
            pltpu.VMEM((width, width), BF16),
            pltpu.VMEM((rows, width), F32),
            pltpu.VMEM((rows, width), F32),
            pltpu.SemaphoreType.DMA((6,)),
        ],
        compiler_params=pltpu.CompilerParams(vmem_limit_bytes=40 * MB),
        cost_estimate=pl.CostEstimate(flops=26 * rows * width * width, bytes_accessed=20 * MB, transcendentals=0),
        name="mid",
    )(a_e, a_d, x_e, x_d, g_e, g_d, pack)


def tail_kernel(
    place, crossed, m_d, ct, g_d, pack,
    out, second_grad, crossed_grad, gain_grad, packed,
    w_out, w_in, w_down, second, n, unit_grad, prod, act, hidden, total, stage, sems,
):
    dec = pack.at[1]
    fetch_cross(dec, w_out, sems.at[0], (1,))
    fetch_ffn(dec, w_in, w_down, sems.at[pl.ds(1, 2)])
    count = m_d.shape[0]
    wait_for(w_out, sems.at[0])
    prod[...] = mm(crossed[...], w_out[...])
    gain = g_d[2:3, :]

    def body(rows):
        value = m_d[rows, :] + prod[rows, :]
        second[rows, :] = value
        total[rows, :] = value
        n[rows, :] = low(centred(value)[0] * gain)
        unit_grad[rows, :] = jnp.zeros((STEP, value.shape[1]), F32)

    each_rows(count, body)
    wait_for(w_in, sems.at[1])
    wait_for(w_down, sems.at[2])

    @pl.loop(0, 4)
    def _(c):
        cols = rows_at(c, 512)
        prod[...] = mm(n[...], w_in[:, cols])
        hidden[...] = mm_nt(ct[...], w_down[cols, :])

        def body(rows):
            value, rate = gelu_parts(prod[rows, :])
            act[rows, :] = low(value)
            hidden[rows, :] = hidden[rows, :] * rate

        each_rows(count, body)
        total[...] += mm(act[...], w_down[cols, :])
        stage_down(stage, 0, c, low(mm_tn(act[...], ct[...])))
        grad = low(hidden[...])
        stage_inner(stage, 64, c, low(mm_tn(n[...], grad)))
        unit_grad[...] += mm_nt(grad, w_in[:, cols])

    gain_grad[...] = jnp.zeros_like(gain_grad)

    def back(rows):
        out[rows, :] = low(total[rows, :])
        part, gained = norm_back(second[rows, :], gain, unit_grad[rows, :])
        gain_grad[...] += gained
        whole = ct[rows, :].astype(F32) + part
        second_grad[rows, :] = whole
        n[rows, :] = low(whole)

    each_rows(count, back)
    stage_rows(stage, 128, low(mm_tn(crossed[...], n[...])))
    send_stage(stage, packed, place, sems.at[3])
    crossed_grad[...] = low(mm_nt(n[...], w_out[...]))
    wait_for(stage, sems.at[3])


def tail(place, crossed, m_d, ct, g_d, pack):
    rows, width = m_d.shape
    row16 = jax.ShapeDtypeStruct((rows, width), BF16)
    row32 = jax.ShapeDtypeStruct((rows, width), F32)
    return pl.pallas_call(
        tail_kernel,
        in_specs=[TABLE] + [WHOLE] * 4 + [AWAY],
        out_specs=[WHOLE] * 4 + [AWAY],
        out_shape=[row16, row32, row16, jax.ShapeDtypeStruct((8, width), F32),
                   jax.ShapeDtypeStruct((2, BLOCKS, 144, width), BF16)],
        scratch_shapes=[
            pltpu.VMEM((width, width), BF16),
            pltpu.VMEM((width, 4 * width), BF16),
            pltpu.VMEM((4 * width, width), BF16),
            pltpu.VMEM((rows, width), F32),
            pltpu.VMEM((rows, width), BF16),
            pltpu.VMEM((rows, width), F32),
            pltpu.VMEM((rows, width), F32),
            pltpu.VMEM((rows, width), BF16),
            pltpu.VMEM((rows, width), F32),
            pltpu.VMEM((rows, width), F32),
            pltpu.VMEM((2, BLOCKS, 144, width), BF16),
            pltpu.SemaphoreType.DMA((4,)),
        ],
        compiler_params=pltpu.CompilerParams(vmem_limit_bytes=40 * MB),
        cost_estimate=pl.CostEstimate(flops=54 * rows * width * width, bytes_accessed=16 * MB, transcendentals=0),
        name="tail",
    )(place, crossed, m_d, ct, g_d, pack)


def mid_back_kernel(
    place, dq, dk, dv, n_d, m_d, second_grad, a_d, memory, end, act, slope, n_e, m_e, a_e, g_e, g_d, pack,
    md_grad, ad_grad, me_grad, ae_grad, gd_grad, ge_grad, packed,
    w_out, w_in, w_down, w_cross, w_query, prod, total, small, stage, sems,
):
    enc, dec = pack.at[0], pack.at[1]
    fetch_cross(dec, w_query, sems.at[5], (0,))
    fetch_out(dec, w_out.at[1], sems.at[3])
    fetch_cross(enc, w_cross, sems.at[4], (0, 1))
    fetch_ffn(enc, w_in, w_down, sems.at[pl.ds(1, 2)])
    fetch_out(enc, w_out.at[0], sems.at[0])
    count = m_d.shape[0]
    ge_grad[...] = jnp.zeros_like(ge_grad)
    gd_grad[...] = jnp.zeros_like(gd_grad)

    def through_out(a, grad, result, section, offset):
        stage_rows(stage, offset, low(mm_tn(a[...], small[...])))
        result[...] = low(mm_nt(small[...], w_out[section]))

    stage_rows(stage, 176, low(mm_tn(n_d[...], dq[...])))
    wait_for(w_query, sems.at[5])
    prod[...] = mm_nt(dq[...], w_query[...])
    gain_d = g_d[1:2, :]

    def decoder(rows):
        part, gained = norm_back(m_d[rows, :], gain_d, prod[rows, :])
        gd_grad[...] += gained
        whole = second_grad[rows, :] + part
        md_grad[rows, :] = whole
        small[rows, :] = low(whole)

    each_rows(count, decoder)
    wait_for(w_out.at[1], sems.at[3])
    through_out(a_d, md_grad, ad_grad, 1, 192)

    stage_rows(stage, 0, low(mm_tn(memory[...], dk[...])))
    stage_rows(stage, 16, low(mm_tn(memory[...], dv[...])))
    wait_for(w_cross, sems.at[4])
    prod[...] = mm_nt(dk[...], w_cross[:, 0:512])
    prod[...] += mm_nt(dv[...], w_cross[:, 512:1024])
    gain_two = g_e[2:3, :]

    def ending(rows):
        part, gained = norm_back(end[rows, :], gain_two, prod[rows, :])
        ge_grad[8:16, :] += gained
        me_grad[rows, :] = part
        small[rows, :] = low(part)
        total[rows, :] = jnp.zeros_like(part)

    each_rows(count, ending)
    wait_for(w_in, sems.at[1])
    wait_for(w_down, sems.at[2])

    @pl.loop(0, 4)
    def _(c):
        cols = rows_at(c, 512)
        stage_down(stage, 32, c, low(mm_tn(act[:, cols], small[...])))
        prod[...] = mm_nt(small[...], w_down[cols, :])

        def body(rows):
            prod[rows, :] = prod[rows, :] * slope[rows, cols].astype(F32)

        each_rows(count, body)
        grad = low(prod[...])
        stage_inner(stage, 96, c, low(mm_tn(n_e[...], grad)))
        total[...] += mm_nt(grad, w_in[:, cols])

    gain_one = g_e[1:2, :]

    def encoder(rows):
        part, gained = norm_back(m_e[rows, :], gain_one, total[rows, :])
        ge_grad[0:8, :] += gained
        whole = me_grad[rows, :] + part
        me_grad[rows, :] = whole
        small[rows, :] = low(whole)

    each_rows(count, encoder)
    wait_for(w_out.at[0], sems.at[0])
    through_out(a_e, me_grad, ae_grad, 0, 160)
    send_stage(stage, packed, place, sems.at[6])
    wait_for(stage, sems.at[6])


def mid_back(place, dq, dk, dv, n_d, m_d, second_grad, a_d, memory, end, act, slope, n_e, m_e, a_e, g_e, g_d, pack):
    rows, width = m_d.shape
    row16 = jax.ShapeDtypeStruct((rows, width), BF16)
    row32 = jax.ShapeDtypeStruct((rows, width), F32)
    return pl.pallas_call(
        mid_back_kernel,
        in_specs=[TABLE] + [WHOLE] * 16 + [AWAY],
        out_specs=[WHOLE] * 6 + [AWAY],
        out_shape=[row32, row16, row32, row16, jax.ShapeDtypeStruct((8, width), F32),
                   jax.ShapeDtypeStruct((16, width), F32),
                   jax.ShapeDtypeStruct((2, BLOCKS, 208, width), BF16)],
        scratch_shapes=[
            pltpu.VMEM((2, width, width), BF16),
            pltpu.VMEM((width, 4 * width), BF16),
            pltpu.VMEM((4 * width, width), BF16),
            pltpu.VMEM((width, 2 * width), BF16),
            pltpu.VMEM((width, width), BF16),
            pltpu.VMEM((rows, width), F32),
            pltpu.VMEM((rows, width), F32),
            pltpu.VMEM((rows, width), BF16),
            pltpu.VMEM((2, BLOCKS, 208, width), BF16),
            pltpu.SemaphoreType.DMA((7,)),
        ],
        compiler_params=pltpu.CompilerParams(vmem_limit_bytes=50 * MB),
        cost_estimate=pl.CostEstimate(flops=52 * rows * width * width, bytes_accessed=30 * MB, transcendentals=0),
        name="mid_back",
    )(place, dq, dk, dv, n_d, m_d, second_grad, a_d, memory, end, act, slope, n_e, m_e, a_e, g_e, g_d, pack)


def front_back_kernel(
    table, place, qe, ke, ve, qd, kd, vd, n_e, n_d, x_e, x_d, me_grad, md_grad, g_e, g_d,
    ge_parts, gd_two, gd_one, ds_e, ds_d, ds_c, own, other,
    xe_grad, xd_grad, packed, w, prod, gained, stage, sems,
):
    for which, src in enumerate((own, other)):
        section = table[2, 0] if which == 0 else 1 - table[2, 0]

        @pl.loop(0, BLOCKS)
        def _(p):
            j = table[which, p]
            for i in range(3):
                start_rows(src, p, w.at[section], j, 32, 32 * i, pl.ds(512 * i, 512), sems.at[section])

    count = x_e.shape[0]
    gained[...] = jnp.zeros_like(gained)
    for section, (grads, n, x, m_grad, g, x_grad) in enumerate(
        (((qe, ke, ve), n_e, x_e, me_grad, g_e, xe_grad), ((qd, kd, vd), n_d, x_d, md_grad, g_d, xd_grad))
    ):
        for i in range(3):
            stage_rows(stage, 48 * section + 16 * i, low(mm_tn(n[...], grads[i][...])))
        wait_for(w.at[section], sems.at[section])
        prod[...] = mm_nt(grads[0][...], w[section, :, 0:512])
        for i in (1, 2):
            prod[...] += mm_nt(grads[i][...], w[section, :, 512 * i : 512 * (i + 1)])
        gain = g[0:1, :]

        def body(rows, x=x, m_grad=m_grad, x_grad=x_grad, gain=gain, section=section):
            part, more = norm_back(x[rows, :].astype(F32), gain, prod[rows, :])
            gained[8 * section : 8 * section + 8, :] += more
            x_grad[rows, :] = m_grad[rows, :] + part

        each_rows(count, body)

    def line(block):
        return jnp.sum(block, axis=0, keepdims=True)

    lane = lax.broadcasted_iota(jnp.int32, (8, x_e.shape[1]), 1)
    heads = jnp.zeros((8, x_e.shape[1]), F32)
    for i, ds in enumerate((ds_e, ds_d, ds_c)):
        heads = jnp.where(lane == i, jnp.sum(ds[...], axis=1, keepdims=True), heads)
    extra = low(jnp.concatenate([
        line(gained[0:8, :]), line(ge_parts[0:8, :]), line(ge_parts[8:16, :]),
        line(gained[8:16, :]), line(gd_one[...]), line(gd_two[...]),
        jnp.zeros((2, x_e.shape[1]), F32), heads,
    ], axis=0))
    for j in range(BLOCKS):
        for h in range(2):
            stage[h, j, 96:112, :] = extra
    send_stage(stage, packed, place, sems.at[2])
    wait_for(stage, sems.at[2])


def front_back(table, place, grads_e, grads_d, n_e, n_d, x_e, x_d, me_grad, md_grad, g_e, g_d, ge_parts, gd_two, gd_one, ds, own, other):
    rows, width = x_e.shape
    row32 = jax.ShapeDtypeStruct((rows, width), F32)
    return pl.pallas_call(
        front_back_kernel,
        in_specs=[TABLE, TABLE] + [WHOLE] * 20 + [AWAY] * 2,
        out_specs=[WHOLE] * 2 + [AWAY],
        out_shape=[row32, row32, jax.ShapeDtypeStruct((2, BLOCKS, 112, width), BF16)],
        scratch_shapes=[
            pltpu.VMEM((2, width, 3 * width), BF16),
            pltpu.VMEM((rows, width), F32),
            pltpu.VMEM((16, width), F32),
            pltpu.VMEM((2, BLOCKS, 112, width), BF16),
            pltpu.SemaphoreType.DMA((3,)),
        ],
        compiler_params=pltpu.CompilerParams(vmem_limit_bytes=40 * MB),
        cost_estimate=pl.CostEstimate(flops=24 * rows * width * width, bytes_accessed=16 * MB, transcendentals=0),
        name="front_back",
    )(table, place, *grads_e, *grads_d, n_e, n_d, x_e, x_d, me_grad, md_grad, g_e, g_d, ge_parts, gd_two, gd_one, *ds, own, other)


ORDER = ((4, 8, 1, 2), (4, 8, 2, 1))
SHIFT = np.array(
    [[functools.reduce(lambda a, b: a ^ b, [m for b, m in enumerate(order) if p >> b & 1], 0) for p in range(BLOCKS)] for order in ORDER],
    np.int32,
)
WHERE = np.argsort(SHIFT, axis=1).astype(np.int32)
SWAP = [(0, 1), (1, 0)]


def swap(value):
    return lax.ppermute(value, "section", SWAP)


def hop(value, bit):
    pairs = [
        (BLOCKS * s + i, BLOCKS * s + (i ^ ORDER[s][bit])) for s in range(2) for i in range(BLOCKS)
    ]
    return lax.ppermute(value, ("section", "dp"), pairs)


def add(kept, came):
    return low(kept.astype(F32) + came.astype(F32))


def reduce_blocks(packed):
    kept = add(packed[0], swap(packed[1]))
    for bit in reversed(range(len(ORDER[0]))):
        half = kept.shape[0] // 2
        kept = add(kept[:half], hop(kept[half:], bit))
    return kept[0]


def inner_of(halves):
    quarter, width = halves[0].shape
    rows = [h.reshape(quarter, 4, width // 4).transpose(1, 0, 2).reshape(4 * quarter, width // 4) for h in halves]
    return jnp.concatenate(rows, axis=0)


def weights_near(attn_qkv, attn_out, cross_proj, ffn_in, ffn_out, gains):
    me, section = lax.axis_index("dp"), lax.axis_index("section")
    columns = gains.shape[2]
    spread_gains = lax.dynamic_update_slice(
        jnp.zeros((16, columns * BLOCKS), BF16), gains[0], (0, me * columns)
    )
    own = pack_first(attn_qkv[0], spread_gains)[None]
    for bit in range(len(ORDER[0])):
        own = jnp.concatenate([own, hop(own, bit)], axis=0)
    other = swap(own)
    second = pack_second(attn_out[0], cross_proj[0], ffn_out[0], ffn_in[0])
    pack = lax.all_gather(second, ("section", "dp"), axis=0, tiled=False)
    shift = jnp.asarray(SHIFT)
    table = jnp.stack([shift[section] ^ me, shift[1 - section] ^ me, jnp.full((BLOCKS,), section, jnp.int32)])
    where = jnp.asarray(WHERE)[:, jnp.arange(BLOCKS, dtype=jnp.int32) ^ me]
    halves = jnp.where(jnp.arange(BLOCKS) == section, 0, 1).astype(jnp.int32)
    return own, other, pack.reshape((2, BLOCKS) + second.shape), table, jnp.concatenate([where, halves[None]])


def weights_far(attn_qkv, attn_out, cross_proj, ffn_in, ffn_out, gains):
    def whole(shard, axis):
        return lax.all_gather(shard[0], "dp", axis=axis, tiled=True)

    qkv, out, cross, inner, down, gain = (
        whole(w, a) for w, a in ((attn_qkv, 0), (attn_out, 0), (cross_proj, 0), (ffn_in, 1), (ffn_out, 0), (gains, 1))
    )
    width = out.shape[1]
    gain_rows = jnp.zeros((BLOCKS, 16, width), BF16).at[0, : gain.shape[0]].set(gain)
    own = jax.vmap(pack_first)(qkv.reshape(BLOCKS, -1, 3 * width), gain_rows)
    second = jax.vmap(pack_second)(
        out.reshape(BLOCKS, -1, width),
        cross.reshape(BLOCKS, -1, 2 * width),
        down.reshape(BLOCKS, -1, width),
        inner.reshape(width, BLOCKS, -1).transpose(1, 0, 2),
    )
    other, second_other = swap(own), swap(second)
    section = lax.axis_index("section")
    pack = jnp.where(section == 0, jnp.stack([second, second_other]), jnp.stack([second_other, second]))
    plain = jnp.arange(BLOCKS, dtype=jnp.int32)
    table = jnp.stack([plain, plain, jnp.full((BLOCKS,), section, jnp.int32)])
    return own, other, pack, table, jnp.stack([plain, plain, plain])


def near_shards(tail_pack, mid_pack, front_pack):
    section = lax.axis_index("section")
    dec_a, both, last = reduce_blocks(tail_pack), reduce_blocks(mid_pack), reduce_blocks(front_pack)

    def meet(enc, dec):
        pairs = (lax.ppermute(enc, "section", [(1, 0)]), lax.ppermute(dec, "section", [(0, 1)]))
        return (enc, pairs[0]), (pairs[1], dec)

    enc_halves, dec_halves = meet(
        jnp.concatenate([both[0:176], last[0:48]], axis=0),
        jnp.concatenate([dec_a, both[176:208], last[48:96]], axis=0),
    )
    e, d = enc_halves, dec_halves

    def rows(halves, start, count):
        return jnp.concatenate([h[start : start + count] for h in halves], axis=0)

    def side(*starts_of):
        return jnp.concatenate(starts_of, axis=1)

    enc = (
        side(*(rows(e, 176 + 16 * i, 16) for i in range(3))),
        rows(e, 160, 16),
        side(rows(e, 0, 16), rows(e, 16, 16)),
        inner_of([h[96:160] for h in e]),
        rows(e, 32, 64),
    )
    dec = (
        side(*(rows(d, 176 + 16 * i, 16) for i in range(3))),
        rows(d, 160, 16),
        side(rows(d, 144, 16), rows(d, 128, 16)),
        inner_of([h[64:128] for h in d]),
        rows(d, 0, 64),
    )
    grads = tuple(jnp.where(section == 0, a, b).astype(F32) for a, b in zip(enc, dec))
    extra = last[96:112].astype(F32)
    mine = lax.dynamic_slice_in_dim(extra, 3 * section, 3, axis=0)
    columns = extra.shape[1] // BLOCKS
    gain = lax.dynamic_slice_in_dim(mine, lax.axis_index("dp") * columns, columns, axis=1)
    return grads + (gain,), extra[8:16, 0:3].T


def far_shards(tail_pack, mid_pack, front_pack):
    def rows(pack, start, count):
        part = pack[:, :, start : start + count]
        return part.transpose(1, 0, 2, 3).reshape(-1, part.shape[-1])

    def inner(pack, start):
        blocks = jax.vmap(lambda a, b: inner_of([a, b]))(pack[0, :, start : start + 64], pack[1, :, start : start + 64])
        return blocks.transpose(1, 0, 2).reshape(blocks.shape[1], -1)

    def side(pack, *starts):
        return jnp.concatenate([rows(pack, s, 16) for s in starts], axis=1)

    enc = (side(front_pack, 0, 16, 32), rows(mid_pack, 160, 16), side(mid_pack, 0, 16), inner(mid_pack, 96), rows(mid_pack, 32, 64))
    cross_d = jnp.concatenate([rows(mid_pack, 176, 16), rows(tail_pack, 128, 16)], axis=1)
    dec = (side(front_pack, 48, 64, 80), rows(mid_pack, 192, 16), cross_d, inner(tail_pack, 64), rows(tail_pack, 0, 64))
    section = lax.axis_index("section")
    grads = []
    for a, b, axis in zip(enc, dec, (0, 0, 0, 1, 0)):
        mine = jnp.where(section == 0, a, b).astype(F32) + swap(jnp.where(section == 0, b, a)).astype(F32)
        grads.append(lax.psum_scatter(mine, "dp", scatter_dimension=axis, tiled=True))
    extra = lax.psum(front_pack[0, 0, 96:112].astype(F32), ("section", "dp"))
    mine = lax.dynamic_slice_in_dim(extra, 3 * section, 3, axis=0)
    columns = extra.shape[1] // lax.axis_size("dp")
    gain = lax.dynamic_slice_in_dim(mine, lax.axis_index("dp") * columns, columns, axis=1)
    return tuple(grads) + (gain,), extra[8:16, 0:3].T


def local(
    layer_input, cotangent, lengths, attn_qkv, attn_out, cross_proj, ffn_in, ffn_out, gains, alpha_raw
):
    section = lax.axis_index("section")
    near = lax.axis_size("dp") == BLOCKS
    weights = weights_near if near else weights_far
    own, other, pack, table, place = weights(attn_qkv, attn_out, cross_proj, ffn_in, ffn_out, gains)
    rows, width = layer_input.shape[3:]
    inputs = layer_input[0, :, 0]
    mine = lax.dynamic_index_in_dim(inputs, section, 0, keepdims=False)
    came = swap(lax.dynamic_index_in_dim(inputs, 1 - section, 0, keepdims=False))
    first = section == 0
    x_e, x_d = jnp.where(first, mine, came), jnp.where(first, came, mine)
    ct = lax.dynamic_index_in_dim(cotangent[:, 0], section, 0, keepdims=False)
    own_lengths = lax.dynamic_index_in_dim(lengths[:, :, 0], section, 1, keepdims=False)
    head_width = width // alpha_raw.shape[1]
    gate = jax.nn.sigmoid(alpha_raw)
    coef = [coefs_of(0.25 + 0.25 * gate[i], head_width) for i in range(3)]
    marks_e = marks_of(own_lengths[0], own_lengths[0], rows, False)
    marks_d = marks_of(own_lengths[1], own_lengths[1], rows, True)
    marks_c = marks_of(own_lengths[1], own_lengths[0], rows, False)

    n_e, q_e, k_e, v_e, n_d, q_d, k_d, v_d, g_e, g_d = front(table, x_e, x_d, own, other)
    a_e, *stats_e = attend(q_e, k_e, v_e, marks_e, coef[0])
    a_d, *stats_d = attend(q_d, k_d, v_d, marks_d, coef[1])
    m_e, n1_e, act, slope, end, memory, mem_k, mem_v, m_d, n1_d, query = mid(a_e, a_d, x_e, x_d, g_e, g_d, pack)
    crossed, *stats_c = attend(query, mem_k, mem_v, marks_c, coef[2])
    result, second_grad, crossed_grad, gd_two, tail_pack = tail(place, crossed, m_d, ct, g_d, pack)
    query_grad, mk_grad, mv_grad, ds_c = attend_back(query, mem_k, mem_v, crossed_grad, stats_c, marks_c, coef[2])
    md_grad, ad_grad, me_grad, ae_grad, gd_one, ge_parts, mid_pack = mid_back(
        place, query_grad, mk_grad, mv_grad, n1_d, m_d, second_grad, a_d, memory, end, act, slope, n1_e, m_e, a_e, g_e, g_d, pack
    )
    *grads_e, ds_e = attend_back(q_e, k_e, v_e, ae_grad, stats_e, marks_e, coef[0])
    *grads_d, ds_d = attend_back(q_d, k_d, v_d, ad_grad, stats_d, marks_d, coef[1])
    xe_grad, xd_grad, front_pack = front_back(
        table, place, grads_e, grads_d, n_e, n_d, x_e, x_d, me_grad, md_grad, g_e, g_d, ge_parts, gd_two, gd_one,
        (ds_e, ds_d, ds_c), own, other,
    )
    grads, ds = (near_shards if near else far_shards)(tail_pack, mid_pack, front_pack)

    def settle(enc, dec):
        kept, came = jnp.where(first, enc, dec), swap(jnp.where(first, dec, enc))
        return jnp.stack([jnp.where(first, kept, came), jnp.where(first, came, kept)])[None, :, None]

    alpha_grad = ds * 0.25 * gate * (1.0 - gate)
    return (settle(memory, result), settle(xe_grad, xd_grad)) + tuple(g[None] for g in grads) + (alpha_grad,)


def solution(mesh):
    return jax.shard_map(
        local,
        mesh=mesh,
        in_specs=(
            P("section", None, "dp", None, None),
            P(None, "dp", None, None),
            P(None, None, "dp", None),
            P("section", "dp", None),
            P("section", "dp", None),
            P("section", "dp", None),
            P("section", None, "dp"),
            P("section", "dp", None),
            P("section", None, "dp"),
            P(),
        ),
        out_specs=(
            P("section", None, "dp", None, None),
            P("section", None, "dp", None, None),
            P("section", "dp", None),
            P("section", "dp", None),
            P("section", "dp", None),
            P("section", None, "dp"),
            P("section", "dp", None),
            P("section", None, "dp"),
            P(),
        ),
        check_vma=False,
    )
```

```python
import functools
import math

import jax
import jax.numpy as jnp
import numpy as np
from jax import lax
from jax.experimental import pallas as pl
from jax.experimental.pallas import tpu as pltpu
from jax.sharding import PartitionSpec as P

SHARP = 0.0625
NEG = -1e9
EPS = 1e-5
TINY = 1e-37
LOG2E = 1.4426950408889634
PART = 256
CHUNK = 128
TILE = 128
BLOCKS = 16
MB = 1 << 20
F32, BF16 = jnp.float32, jnp.bfloat16
WHOLE = pl.BlockSpec(memory_space=pltpu.VMEM)
TABLE = pl.BlockSpec(memory_space=pltpu.SMEM)
AWAY = pl.BlockSpec(memory_space=pl.ANY)


def mm(a, b):
    return jnp.dot(a, b, preferred_element_type=F32)


def mm_nt(a, b):
    return lax.dot_general(a, b, (((1,), (1,)), ((), ())), preferred_element_type=F32)


def mm_tn(a, b):
    return lax.dot_general(a, b, (((0,), (0,)), ((), ())), preferred_element_type=F32)


def low(v):
    return v.astype(BF16)


def fold(block):
    return jnp.sum(block.reshape(block.shape[0] // 8, 8, block.shape[1]), axis=0)


def fold_max(block):
    return jnp.max(block.reshape(block.shape[0] // 8, 8, block.shape[1]), axis=0)


def rows_of(parts, op):
    return jnp.concatenate([op(part, axis=0, keepdims=True) for part in parts], axis=0)


def per_head(coef, which, heads):
    place = lax.broadcasted_iota(jnp.int32, (heads, TILE), 0)
    out = jnp.zeros((heads, TILE), F32)
    for h in range(heads):
        out = jnp.where(place == h, coef[which, h], out)
    return out


def bias_of(lo, hi, start):
    place = lax.broadcasted_iota(jnp.int32, (CHUNK, TILE), 0) + start
    return jnp.where(jnp.logical_and(place >= lo, place < hi), 0.0, NEG)


def pair_of(h, width):
    return slice(h // 2 * 2 * width, (h // 2 + 1) * 2 * width)


def split_pairs(dst, turned, heads, width):
    for h in range(heads):
        block = turned[pair_of(h, width), :]
        mine = lax.broadcasted_iota(jnp.int32, block.shape, 0) // width == h % 2
        dst[h] = jnp.where(mine, block, jnp.zeros_like(block))


def fold(block):
    return jnp.sum(block.reshape(block.shape[0] // 8, 8, block.shape[1]), axis=0)


def fold_max(block):
    return jnp.max(block.reshape(block.shape[0] // 8, 8, block.shape[1]), axis=0)


def rows_of(parts, op):
    return jnp.concatenate([op(part, axis=0, keepdims=True) for part in parts], axis=0)


def per_head(coef, which, heads):
    place = lax.broadcasted_iota(jnp.int32, (heads, TILE), 0)
    out = jnp.zeros((heads, TILE), F32)
    for h in range(heads):
        out = jnp.where(place == h, coef[which, h], out)
    return out


def bias_of(lo, hi, start):
    place = lax.broadcasted_iota(jnp.int32, (CHUNK, TILE), 0) + start
    return jnp.where(jnp.logical_and(place >= lo, place < hi), 0.0, NEG)


def pair_of(h, width):
    return slice(h // 2 * 2 * width, (h // 2 + 1) * 2 * width)


def chunk_at(c):
    return pl.ds(pl.multiple_of(c * CHUNK, CHUNK), CHUNK)


def split_pairs(dst, turned, heads, width):
    for h in range(heads):
        block = turned[pair_of(h, width), :]
        mine = lax.broadcasted_iota(jnp.int32, block.shape, 0) // width == h % 2
        dst[h] = jnp.where(mine, block, jnp.zeros_like(block))


def clear_outside(first, last, keys, refs, cols):
    def blank(c, carry):
        for ref in refs:
            for h in range(ref.shape[0]):
                ref[h, chunk_at(c), cols] = jnp.zeros((CHUNK, TILE), BF16)
        return carry

    lax.fori_loop(0, first, blank, 0)
    lax.fori_loop(last, keys // CHUNK, blank, 0)


def meets(first, last, half):
    per = PART // CHUNK
    return jnp.logical_and(first < (half + 1) * per, last > half * per)


def attend_kernel(
    span, coef, lo_ref, hi_ref, q_ref, k_ref, v_ref, o_ref, tau_ref, top_ref, inv_ref, v_t, zs, ps, qz, o_t
):
    heads, keys = zs.shape[0], zs.shape[1]
    width = q_ref.shape[1] // heads
    tile = pl.program_id(0)

    @pl.when(tile == 0)
    def _():
        v_t[...] = v_ref[...].T

    split_pairs(qz, q_ref[...].T, heads, width)
    lo, hi = lo_ref[...], hi_ref[...]
    first, last = span[0, tile], span[1, tile]

    def scores(c, tops):
        here = chunk_at(c)
        bias = bias_of(lo, hi, c * CHUNK)
        out = []
        for h in range(heads):
            z = mm(k_ref[here, pair_of(h, width)], qz[h]) * coef[0, h] + bias
            zs[h, here, :] = z
            out.append(jnp.maximum(tops[h], fold_max(z)))
        return tuple(out)

    tops = lax.fori_loop(
        first, last, scores, tuple(jnp.full((8, TILE), -3e38, F32) for _ in range(heads))
    )
    peak = rows_of(tops, jnp.max)
    shrink, exponent = per_head(coef, 1, heads), per_head(coef, 4, heads)
    least = peak - 1.0
    most = peak - jnp.exp2(-shrink * jnp.log2((hi - lo).astype(F32)))
    close = 4e-6 + 5e-7 * jnp.abs(peak)
    zero = tuple(jnp.zeros((8, TILE), F32) for _ in range(3 * heads))

    def search(state):
        turn, tau, _ = state

        def body(c, sums):
            here = chunk_at(c)
            out = []
            for h in range(heads):
                u = jnp.maximum(zs[h, here, :] - tau[h : h + 1, :], TINY)
                curve = jnp.exp2(jnp.log2(u) * coef[3, h])
                slope = curve * u
                out += [sums[3 * h] + fold(slope * u), sums[3 * h + 1] + fold(slope), sums[3 * h + 2] + fold(curve)]
            return tuple(out)

        sums = lax.fori_loop(first, last, body, zero)
        mass, slope, curve = (rows_of(sums[i::3], jnp.sum) for i in range(3))
        bend = jnp.clip(1.0 - (exponent - 1.0) * curve * mass / (exponent * slope * slope), 0.0, 1.0)
        bend = jnp.where(turn < 5, bend, shrink)
        log_mass = jnp.log(mass)
        x = bend * log_mass
        rise = jnp.where(
            jnp.abs(x) < 0.1,
            log_mass * (1.0 - x * (0.5 - x * (1.0 / 6.0))),
            (1.0 - jnp.exp(-x)) / jnp.maximum(bend, 1e-6),
        )
        new = jnp.clip(tau + mass / (exponent * slope) * rise, least, most)
        return turn + 1, new, jnp.max(jnp.abs(new - tau))

    def finish(state):
        turn, tau, _, _, _ = state
        turn, tau, _ = lax.while_loop(
            lambda s: jnp.logical_and(s[2] > 6e-3, s[0] < 40), search, (turn, tau, jnp.float32(1.0))
        )

        def final(c, sums):
            here = chunk_at(c)
            out = []
            for h in range(heads):
                z = zs[h, here, :]
                u = jnp.maximum(z - tau[h : h + 1, :], TINY)
                slope = jnp.exp2(jnp.log2(u) * coef[2, h])
                p = slope * u
                ps[h, here, :] = low(p)
                soft = jnp.exp2((z - peak[h : h + 1, :]) * (LOG2E / SHARP))
                out += [sums[3 * h] + fold(p), sums[3 * h + 1] + fold(slope), sums[3 * h + 2] + fold(soft)]
            return tuple(out)

        sums = lax.fori_loop(first, last, final, zero)
        mass, slope, soft = (rows_of(sums[i::3], jnp.sum) for i in range(3))
        off = (mass - 1.0) / (exponent * slope)
        open_ = jnp.max(jnp.where(jnp.abs(off) > close, 1.0, 0.0))
        return turn, jnp.where(open_ > 0.0, jnp.clip(tau + off, least, most), tau), open_, mass, soft

    blank = jnp.ones((heads, TILE), F32)
    _, tau, _, mass, soft = lax.while_loop(
        lambda s: jnp.logical_and(s[2] > 0.0, s[0] < 40), finish, (0, least, jnp.float32(1.0), blank, blank)
    )
    inv = 1.0 / mass
    tau_ref[...] = tau
    top_ref[...] = peak + SHARP * jnp.log(soft)
    inv_ref[...] = inv
    clear_outside(first, last, keys, (ps,), slice(None))
    o_t[...] = jnp.zeros_like(o_t)
    for half in range(keys // PART):
        cols = slice(half * PART, (half + 1) * PART)

        @pl.when(meets(first, last, half))
        def _():
            for h in range(heads):
                rows = slice(h * width, (h + 1) * width)
                o_t[rows, :] += mm(v_t[rows, cols], ps[h, cols, :])

    for h in range(0, heads, 2):
        got = [o_t[i * width : (i + 1) * width, :] * inv[i : i + 1, :] for i in (h, h + 1)]
        o_ref[:, pair_of(h, width)] = low(jnp.concatenate(got, axis=0).T)


def attend(q, k, v, marks, coef):
    lo, hi, span = marks
    rows, width = q.shape
    keys, heads = k.shape[0], coef.shape[1]
    line = pl.BlockSpec((1, TILE), lambda t, *_: (0, t))
    tile = pl.BlockSpec((TILE, width), lambda t, *_: (t, 0))
    stat = pl.BlockSpec((heads, TILE), lambda t, *_: (0, t))
    full = pl.BlockSpec((keys, width), lambda t, *_: (0, 0))
    return pl.pallas_call(
        attend_kernel,
        grid_spec=pltpu.PrefetchScalarGridSpec(
            num_scalar_prefetch=2,
            grid=(rows // TILE,),
            in_specs=[line, line, tile, full, full],
            out_specs=[tile, stat, stat, stat],
            scratch_shapes=[
                pltpu.VMEM((width, keys), BF16),
                pltpu.VMEM((heads, keys, TILE), F32),
                pltpu.VMEM((heads, keys, TILE), BF16),
                pltpu.VMEM((heads, 2 * width // heads, TILE), BF16),
                pltpu.VMEM((width, TILE), F32),
            ],
        ),
        out_shape=[jax.ShapeDtypeStruct((rows, width), BF16)]
        + [jax.ShapeDtypeStruct((heads, rows), F32)] * 3,
        compiler_params=pltpu.CompilerParams(vmem_limit_bytes=24 * MB),
        cost_estimate=pl.CostEstimate(
            flops=4 * rows * keys * width, bytes_accessed=4 * MB, transcendentals=heads * rows * keys * 8
        ),
        name="attend",
    )(span, coef, lo, hi, q, k, v)


def attend_back_kernel(
    span, coef, lo_ref, hi_ref, q_ref, go_ref, tau_ref, top_ref, inv_ref, q_all, go_all, k_ref, v_ref,
    dq_ref, dk_ref, dv_ref, ds_ref, k_t, zs, gs, ls, qz, gz, g_all, p_all, dq_t, dk_sum, dv_sum,
):
    heads, keys = zs.shape[0], zs.shape[1]
    width = q_ref.shape[1] // heads
    scale = 1.0 / math.sqrt(width)
    tile = pl.program_id(0)
    at = pl.ds(pl.multiple_of(tile * TILE, TILE), TILE)

    @pl.when(tile == 0)
    def _():
        k_t[...] = k_ref[...].T
        ds_ref[...] = jnp.zeros_like(ds_ref)

    split_pairs(qz, q_ref[...].T, heads, width)
    split_pairs(gz, go_ref[...].T, heads, width)
    lo, hi = lo_ref[...], hi_ref[...]
    tau, top, inv = tau_ref[...], top_ref[...], inv_ref[...]
    first, last = span[0, tile], span[1, tile]
    kinds = 5
    zero = tuple(jnp.zeros((8, TILE), F32) for _ in range(kinds * heads))

    def gather(c, sums):
        here = chunk_at(c)
        bias = bias_of(lo, hi, c * CHUNK)
        out = []
        for h in range(heads):
            z = mm(k_ref[here, pair_of(h, width)], qz[h]) * coef[0, h] + bias
            g = mm(v_ref[here, pair_of(h, width)], gz[h])
            u = jnp.maximum(z - tau[h : h + 1, :], TINY)
            log_u = jnp.log2(u)
            slope = jnp.exp2(log_u * coef[2, h])
            p = slope * u
            p_log = p * log_u
            zs[h, here, :] = z
            gs[h, here, :] = g
            ls[h, here, :] = slope
            new = (g * p, g * slope, slope, g * p_log, p_log)
            out += [sums[kinds * h + i] + fold(new[i]) for i in range(kinds)]
        return tuple(out)

    sums = lax.fori_loop(first, last, gather, zero)
    gp, gl, ll, gpl, pl_sum = (rows_of(sums[i::kinds], jnp.sum) for i in range(kinds))
    shrink = per_head(coef, 1, heads)
    inv_k = per_head(coef, 4, heads) * inv
    mean = gp * inv
    drop = inv_k * (gl - mean * ll)
    grad_k = inv * (gpl - mean * pl_sum) * (1.0 / LOG2E)
    clear_outside(first, last, keys, (g_all, p_all), at)

    def final(c, sums):
        here = chunk_at(c)
        out = []
        for h in range(heads):
            one = slice(h, h + 1)
            z, slope = zs[h, here, :], ls[h, here, :]
            p = slope * jnp.maximum(z - tau[one], TINY)
            r = (gs[h, here, :] - mean[one]) * slope * inv_k[one]
            g_z = r - drop[one] * jnp.exp2((z - top[one]) * (LOG2E / SHARP))
            g_all[h, here, at] = low(g_z * coef[1, h])
            p_all[h, here, at] = low(p * inv[one])
            out.append(sums[h] + fold(g_z * z))
        return tuple(out)

    sums = lax.fori_loop(first, last, final, zero[:heads])
    ds_ref[...] += rows_of(sums, jnp.sum) / shrink - grad_k / (shrink * shrink)
    dq_t[...] = jnp.zeros_like(dq_t)
    for half in range(keys // PART):
        cols = slice(half * PART, (half + 1) * PART)

        @pl.when(meets(first, last, half))
        def _():
            for h in range(heads):
                rows = slice(h * width, (h + 1) * width)
                dq_t[rows, :] += mm(k_t[rows, cols], g_all[h, cols, at])

    for h in range(0, heads, 2):
        dq_ref[:, pair_of(h, width)] = low(dq_t[pair_of(h, width), :].T * scale)

    @pl.when(tile == pl.num_programs(0) - 1)
    def _():
        dk_sum[...] = jnp.zeros_like(dk_sum)
        dv_sum[...] = jnp.zeros_like(dv_sum)
        tiles = PART // TILE
        lane = lax.broadcasted_iota(jnp.int32, (PART, 2 * width), 1) // width
        blank_rows = jnp.zeros((PART, 2 * width), BF16)
        for q_half in range(q_all.shape[0] // PART):
            rows = slice(q_half * PART, (q_half + 1) * PART)
            for half in range(keys // PART):
                cols = slice(half * PART, (half + 1) * PART)
                reach = [
                    meets(span[0, t], span[1, t], half) for t in range(q_half * tiles, (q_half + 1) * tiles)
                ]

                @pl.when(functools.reduce(jnp.logical_or, reach))
                def _():
                    for h in range(0, heads, 2):
                        pair = pair_of(h, width)
                        for i in (h, h + 1):
                            mine = lane == i % 2
                            dk_sum[cols, pair] += mm(g_all[i, cols, rows], jnp.where(mine, q_all[rows, pair], blank_rows))
                            dv_sum[cols, pair] += mm(p_all[i, cols, rows], jnp.where(mine, go_all[rows, pair], blank_rows))

        dk_ref[...] = low(dk_sum[...] * scale)
        dv_ref[...] = low(dv_sum[...])


def attend_back(q, k, v, go, stats, marks, coef):
    lo, hi, span = marks
    rows, width = q.shape
    keys, heads = k.shape[0], coef.shape[1]
    line = pl.BlockSpec((1, TILE), lambda t, *_: (0, t))
    tile = pl.BlockSpec((TILE, width), lambda t, *_: (t, 0))
    stat = pl.BlockSpec((heads, TILE), lambda t, *_: (0, t))
    q_full = pl.BlockSpec((rows, width), lambda t, *_: (0, 0))
    k_full = pl.BlockSpec((keys, width), lambda t, *_: (0, 0))
    return pl.pallas_call(
        attend_back_kernel,
        grid_spec=pltpu.PrefetchScalarGridSpec(
            num_scalar_prefetch=2,
            grid=(rows // TILE,),
            in_specs=[line, line, tile, tile, stat, stat, stat, q_full, q_full, k_full, k_full],
            out_specs=[tile, k_full, k_full, pl.BlockSpec((heads, TILE), lambda t, *_: (0, 0))],
            scratch_shapes=[pltpu.VMEM((width, keys), BF16)]
            + [pltpu.VMEM((heads, keys, TILE), F32)] * 3
            + [pltpu.VMEM((heads, 2 * width // heads, TILE), BF16)] * 2
            + [pltpu.VMEM((heads, keys, rows), BF16)] * 2
            + [pltpu.VMEM((width, TILE), F32)]
            + [pltpu.VMEM((keys, width), F32)] * 2,
        ),
        out_shape=[
            jax.ShapeDtypeStruct((rows, width), BF16),
            jax.ShapeDtypeStruct((keys, width), BF16),
            jax.ShapeDtypeStruct((keys, width), BF16),
            jax.ShapeDtypeStruct((heads, TILE), F32),
        ],
        compiler_params=pltpu.CompilerParams(vmem_limit_bytes=36 * MB),
        cost_estimate=pl.CostEstimate(
            flops=10 * rows * keys * width, bytes_accessed=6 * MB, transcendentals=heads * rows * keys * 3
        ),
        name="attend_back",
    )(span, coef, lo, hi, q, go, *stats, q, go, k, v)


def starts_of(lengths, rank):
    number = jnp.arange(lengths.shape[0])
    before = rank[None, :] < rank[:, None]
    before |= (rank[None, :] == rank[:, None]) & (number[None, :] < number[:, None])
    return jnp.sum(jnp.where(before, lengths[None, :], 0), axis=1)


def marks_of(q_starts, q_lengths, k_starts, k_lengths, rows, causal):
    places = jnp.arange(rows, dtype=jnp.int32)
    pick = (places[:, None] >= q_starts[None, :]) & (places[:, None] < (q_starts + q_lengths)[None, :])
    lo = jnp.sum(jnp.where(pick, k_starts[None, :], 0), axis=1)
    hi = jnp.sum(jnp.where(pick, (k_starts + k_lengths)[None, :], 0), axis=1)
    if causal:
        hi = jnp.minimum(hi, places + 1)
    first = jnp.min(lo.reshape(-1, TILE), axis=1) // CHUNK
    last = (jnp.max(hi.reshape(-1, TILE), axis=1) + CHUNK - 1) // CHUNK
    return (lo[None], hi[None], jnp.stack([first, last]))


def coefs_of(shrink, width):
    exponent = 1.0 / shrink
    return jnp.stack([shrink / math.sqrt(width), shrink, exponent - 1.0, exponent - 2.0, exponent])


OUT, CROSS, DOWN, IN, SECOND = 0, 32, 96, 224, 352
GAIN, FIRST = 48, 64


def pack_first(qkv, gain_rows):
    width = qkv.shape[-1] // 3
    parts = [qkv[:, i * width : (i + 1) * width] for i in range(3)]
    tails = (gain_rows, jnp.zeros_like(gain_rows))
    return [
        jnp.concatenate([p[16 * h : 16 * h + 16] for p in parts] + [tails[h]], axis=0) for h in range(2)
    ]


def pack_second(out, cross, down, inner):
    width = out.shape[-1]
    quarter = inner.shape[0] // 4
    turned = inner.reshape(4, quarter, inner.shape[1]).transpose(1, 0, 2).reshape(quarter, -1)
    return jnp.concatenate([out, cross[:, :width], cross[:, width:], down, turned], axis=0)


def pack_kernel(me, qkv, out, cross, inner, down, gains, kept, sent, second):
    width = out.shape[1]
    columns = gains.shape[1]
    spot = lax.broadcasted_iota(jnp.int32, (columns, width), 1) - me[0] * columns
    here = spot == lax.broadcasted_iota(jnp.int32, (columns, width), 0)
    spread = low(mm(gains[...], jnp.where(here, 1.0, 0.0).astype(BF16)))
    for h in range(2):
        for mine, dst in ((True, kept), (False, sent)):

            @pl.when((me[1] == h) == mine)
            def _():
                for i in range(3):
                    dst[16 * i : 16 * i + 16, :] = qkv[16 * h : 16 * h + 16, width * i : width * (i + 1)]
                dst[GAIN : GAIN + 16, :] = spread if h == 0 else jnp.zeros_like(spread)

    second[OUT : OUT + 32, :] = out[...]
    for i in range(2):
        second[CROSS + 32 * i : CROSS + 32 * i + 32, :] = cross[:, width * i : width * (i + 1)]
    second[DOWN : DOWN + 128, :] = down[...]
    for i in range(4):
        second[IN : IN + 128, 128 * i : 128 * (i + 1)] = inner[128 * i : 128 * (i + 1), :]


def pack_shards(me, qkv, out, cross, inner, down, gains):
    width = out.shape[1]
    half = jax.ShapeDtypeStruct((FIRST, width), BF16)
    return pl.pallas_call(
        pack_kernel,
        in_specs=[TABLE] + [WHOLE] * 6,
        out_specs=[WHOLE] * 3,
        out_shape=[half, half, jax.ShapeDtypeStruct((SECOND, width), BF16)],
        name="pack_shards",
    )(me, qkv, out, cross, inner, down, gains)


def rows_at(block, rows):
    return pl.ds(pl.multiple_of(block * rows, rows), rows)


def start_rows(src, block_of, dst, dst_block, rows, offset, cols, sem):
    pltpu.make_async_copy(
        src.at[block_of, pl.ds(offset, rows), :], dst.at[rows_at(dst_block, rows), cols], sem
    ).start()


def start_inner(src, block, dst, sem):
    cols = rows_at(block, 128)
    for i in range(4):
        pltpu.make_async_copy(
            src.at[block, pl.ds(IN, 128), pl.ds(128 * i, 128)], dst.at[pl.ds(128 * i, 128), cols], sem
        ).start()


def wait_for(ref, sem):
    pltpu.make_async_copy(ref, ref, sem).wait()


def fetch_out(src, dst, sem):
    @pl.loop(0, BLOCKS)
    def _(j):
        start_rows(src, j, dst, j, 32, OUT, slice(None), sem)


def fetch_cross(src, dst, sem, which):
    @pl.loop(0, BLOCKS)
    def _(j):
        for n, i in enumerate(which):
            start_rows(src, j, dst, j, 32, CROSS + 32 * i, pl.ds(512 * n, 512), sem)


def fetch_ffn(src, inner, down, sems):
    @pl.loop(0, BLOCKS)
    def _(j):
        start_inner(src, j, inner, sems.at[0])

    @pl.loop(0, BLOCKS)
    def _(j):
        start_rows(src, j, down, j, 128, DOWN, slice(None), sems.at[1])


def pack_pair(rows, width):
    return [jax.ShapeDtypeStruct((BLOCKS, rows, width), BF16)] * 2


def stage_rows(stage, offset, grad):
    for j in range(BLOCKS):
        for h in range(2):
            stage[h, j, offset : offset + 16, :] = grad[32 * j + 16 * h : 32 * j + 16 * h + 16, :]


def stage_down(stage, offset, c, grad):
    for j in range(4):
        for h in range(2):
            at = 128 * j + 64 * h
            stage[h, 4 * c + j, offset : offset + 64, :] = grad[at : at + 64, :]


def stage_inner(stage, offset, c, grad):
    for j in range(4):
        for h in range(2):
            for i in range(4):
                at = 256 * h + 64 * i
                stage[h, 4 * c + j, offset : offset + 64, 128 * i : 128 * (i + 1)] = grad[
                    at : at + 64, 128 * j : 128 * (j + 1)
                ]


def send_stage(stage, kept, sent, place, sem):
    for h in range(2):
        for which, dst in enumerate((kept, sent)):

            @pl.when(place[2, h] == which)
            def _():
                @pl.loop(0, BLOCKS)
                def _(j):
                    pltpu.make_async_copy(stage.at[h, j], dst.at[place[h, j]], sem).start()


STEP = 64


def each_rows(rows, body):
    @pl.loop(0, rows // STEP)
    def _(i):
        body(pl.ds(pl.multiple_of(i * STEP, STEP), STEP))


def centred(v):
    shifted = v - jnp.mean(v, axis=-1, keepdims=True)
    rate = lax.rsqrt(jnp.mean(shifted * shifted, axis=-1, keepdims=True) + EPS)
    return shifted * rate, rate


def norm_back(v, gain, grad):
    unit, rate = centred(v)
    e = grad * gain
    back = e - jnp.mean(e, axis=-1, keepdims=True) - unit * jnp.mean(e * unit, axis=-1, keepdims=True)
    return back * rate, grad * unit


def gelu_parts(u):
    phi = 0.5 + 0.5 * lax.erf(u * (1.0 / math.sqrt(2.0)))
    bell = jnp.exp2(u * u * (-0.5 * LOG2E)) * (1.0 / math.sqrt(2.0 * math.pi))
    return u * phi, phi + u * bell


def places_of(dest):
    rows = dest.shape[1]
    return jnp.where(lax.broadcasted_iota(jnp.int32, (rows, rows), 0) == dest[...], 1.0, 0.0).astype(BF16)


def sort_kernel(section, inputs, came, cotangent, dest_e, dest_d, x_e, x_d, ct):
    s = section[0]
    place_e, place_d = places_of(dest_e), places_of(dest_d)
    for owner, dst, place in ((0, x_e, place_e), (1, x_d, place_d)):

        @pl.when(s == owner)
        def _():
            dst[...] = low(mm(place, inputs[s]))

        @pl.when(s != owner)
        def _():
            dst[...] = low(mm(place, came[...]))

    ct[...] = low(mm(place_d, cotangent[s]))


def sort_rows(section, inputs, came, cotangent, dest_e, dest_d):
    row16 = jax.ShapeDtypeStruct(came.shape, BF16)
    return pl.pallas_call(
        sort_kernel,
        in_specs=[TABLE] + [WHOLE] * 5,
        out_specs=[WHOLE] * 3,
        out_shape=[row16] * 3,
        compiler_params=pltpu.CompilerParams(vmem_limit_bytes=24 * MB),
        name="sort_rows",
    )(section, inputs, came, cotangent, dest_e, dest_d)


def fetch_front(table, own, other, w, sem):
    for which, src in enumerate((own, other)):
        half = table[2, 0] if which == 0 else 1 - table[2, 0]

        @pl.loop(0, BLOCKS)
        def _(p):
            at = pl.ds(pl.multiple_of(32 * table[which, p] + 16 * half, 16), 16)
            for i in range(3):
                pltpu.make_async_copy(
                    src.at[p, pl.ds(16 * i, 16), :], w.at[at, pl.ds(512 * i, 512)], sem
                ).start()


def front_kernel(table, x, own, other, n, q, k, v, g, w, gs, prod, sems):
    for which, src in enumerate((own, other)):

        @pl.loop(0, BLOCKS)
        def _(p):
            pltpu.make_async_copy(src.at[p, pl.ds(GAIN, 16), :], gs.at[which, p], sems.at[1]).start()

    fetch_front(table, own, other, w, sems.at[0])
    wait_for(gs, sems.at[1])
    gains = jnp.sum(gs[...].astype(F32), axis=(0, 1))[0:8]
    g[...] = gains
    gain = gains[0:1]

    def body(rows):
        n[rows, :] = low(centred(x[rows, :].astype(F32))[0] * gain)

    each_rows(x.shape[0], body)
    wait_for(w, sems.at[0])
    for i, out in enumerate((q, k, v)):
        prod[...] = mm(n[...], w[:, 512 * i : 512 * (i + 1)])

        def keep(rows, out=out):
            out[rows, :] = low(prod[rows, :])

        each_rows(x.shape[0], keep)


def front(table, x, own, other):
    rows, width = x.shape
    row16 = jax.ShapeDtypeStruct((rows, width), BF16)
    gain = jax.ShapeDtypeStruct((8, width), F32)
    return pl.pallas_call(
        front_kernel,
        in_specs=[TABLE, WHOLE, AWAY, AWAY],
        out_specs=[WHOLE] * 5,
        out_shape=[row16] * 4 + [gain],
        scratch_shapes=[
            pltpu.VMEM((width, 3 * width), BF16),
            pltpu.VMEM((2, BLOCKS, 16, width), BF16),
            pltpu.VMEM((rows, width), F32),
            pltpu.SemaphoreType.DMA((2,)),
        ],
        compiler_params=pltpu.CompilerParams(vmem_limit_bytes=24 * MB),
        cost_estimate=pl.CostEstimate(flops=6 * rows * width * width, bytes_accessed=4 * MB, transcendentals=0),
        name="front",
    )(table, x, own, other)


def mid_kernel(
    a_e, a_d, x_e, x_d, g_e, g_d, dest, pack,
    m_e, n_e, act, slope, end, memory, mem_k, mem_v, m_d, n_d, query, memory_out,
    w_out, w_in, w_down, w_cross, w_query, prod, total, sems,
):
    enc, dec = pack.at[0], pack.at[1]
    fetch_out(enc, w_out.at[0], sems.at[0])
    fetch_ffn(enc, w_in, w_down, sems.at[pl.ds(1, 2)])
    fetch_out(dec, w_out.at[1], sems.at[3])
    fetch_cross(enc, w_cross, sems.at[4], (0, 1))
    fetch_cross(dec, w_query, sems.at[5], (0,))
    count = x_e.shape[0]

    def attended(a, x, g, m, n, section, sem):
        wait_for(w_out.at[section], sem)
        prod[...] = mm(a[...], w_out[section])
        gain = g[1:2, :]

        def body(rows):
            middle = x[rows, :].astype(F32) + prod[rows, :]
            m[rows, :] = middle
            n[rows, :] = low(centred(middle)[0] * gain)

        each_rows(count, body)

    attended(a_e, x_e, g_e, m_e, n_e, 0, sems.at[0])
    wait_for(w_in, sems.at[1])
    wait_for(w_down, sems.at[2])
    total[...] = m_e[...]

    @pl.loop(0, 4)
    def _(c):
        cols = rows_at(c, 512)
        prod[...] = mm(n_e[...], w_in[:, cols])

        def body(rows):
            value, rate = gelu_parts(prod[rows, :])
            act[rows, cols] = low(value)
            slope[rows, cols] = low(rate)

        each_rows(count, body)
        total[...] += mm(act[:, cols], w_down[cols, :])

    gain = g_e[2:3, :]

    def body(rows):
        ending = total[rows, :]
        end[rows, :] = ending
        memory[rows, :] = low(centred(ending)[0] * gain)

    each_rows(count, body)
    wait_for(w_cross, sems.at[4])
    mem_k[...] = low(mm(memory[...], w_cross[:, 0:512]))
    mem_v[...] = low(mm(memory[...], w_cross[:, 512:1024]))
    memory_out[...] = low(mm_tn(places_of(dest), memory[...]))
    attended(a_d, x_d, g_d, m_d, n_d, 1, sems.at[3])
    wait_for(w_query, sems.at[5])
    query[...] = low(mm(n_d[...], w_query[...]))


def mid(a_e, a_d, x_e, x_d, g_e, g_d, dest, pack):
    rows, width = x_e.shape
    row16 = jax.ShapeDtypeStruct((rows, width), BF16)
    row32 = jax.ShapeDtypeStruct((rows, width), F32)
    wide = jax.ShapeDtypeStruct((rows, 4 * width), BF16)
    return pl.pallas_call(
        mid_kernel,
        in_specs=[WHOLE] * 7 + [AWAY],
        out_specs=[WHOLE] * 12,
        out_shape=[row32, row16, wide, wide, row32, row16, row16, row16, row32, row16, row16, row16],
        scratch_shapes=[
            pltpu.VMEM((2, width, width), BF16),
            pltpu.VMEM((width, 4 * width), BF16),
            pltpu.VMEM((4 * width, width), BF16),
            pltpu.VMEM((width, 2 * width), BF16),
            pltpu.VMEM((width, width), BF16),
            pltpu.VMEM((rows, width), F32),
            pltpu.VMEM((rows, width), F32),
            pltpu.SemaphoreType.DMA((6,)),
        ],
        compiler_params=pltpu.CompilerParams(vmem_limit_bytes=56 * MB),
        cost_estimate=pl.CostEstimate(flops=26 * rows * width * width, bytes_accessed=20 * MB, transcendentals=0),
        name="mid",
    )(a_e, a_d, x_e, x_d, g_e, g_d, dest, pack)


def tail_kernel(
    place, crossed, m_d, ct, g_d, dest, pack,
    out, second_grad, crossed_grad, gain_grad, kept, sent,
    w_out, w_in, w_down, second, n, unit_grad, prod, act, hidden, total, stage, sems,
):
    dec = pack.at[1]
    fetch_cross(dec, w_out, sems.at[0], (1,))
    fetch_ffn(dec, w_in, w_down, sems.at[pl.ds(1, 2)])
    count = m_d.shape[0]
    wait_for(w_out, sems.at[0])
    prod[...] = mm(crossed[...], w_out[...])
    gain = g_d[2:3, :]

    def body(rows):
        value = m_d[rows, :] + prod[rows, :]
        second[rows, :] = value
        total[rows, :] = value
        n[rows, :] = low(centred(value)[0] * gain)
        unit_grad[rows, :] = jnp.zeros((STEP, value.shape[1]), F32)

    each_rows(count, body)
    wait_for(w_in, sems.at[1])
    wait_for(w_down, sems.at[2])

    @pl.loop(0, 4)
    def _(c):
        cols = rows_at(c, 512)
        prod[...] = mm(n[...], w_in[:, cols])
        hidden[...] = mm_nt(ct[...], w_down[cols, :])

        def body(rows):
            value, rate = gelu_parts(prod[rows, :])
            act[rows, :] = low(value)
            hidden[rows, :] = hidden[rows, :] * rate

        each_rows(count, body)
        total[...] += mm(act[...], w_down[cols, :])
        stage_down(stage, 0, c, low(mm_tn(act[...], ct[...])))
        grad = low(hidden[...])
        stage_inner(stage, 64, c, low(mm_tn(n[...], grad)))
        unit_grad[...] += mm_nt(grad, w_in[:, cols])

    gain_grad[...] = jnp.zeros_like(gain_grad)

    def back(rows):
        act[rows, :] = low(total[rows, :])
        part, gained = norm_back(second[rows, :], gain, unit_grad[rows, :])
        gain_grad[...] += fold(gained)
        whole = ct[rows, :].astype(F32) + part
        second_grad[rows, :] = whole
        n[rows, :] = low(whole)

    each_rows(count, back)
    stage_rows(stage, 128, low(mm_tn(crossed[...], n[...])))
    send_stage(stage, kept, sent, place, sems.at[3])
    crossed_grad[...] = low(mm_nt(n[...], w_out[...]))
    out[...] = low(mm_tn(places_of(dest), act[...]))
    wait_for(stage, sems.at[3])


def tail(place, crossed, m_d, ct, g_d, dest, pack):
    rows, width = m_d.shape
    row16 = jax.ShapeDtypeStruct((rows, width), BF16)
    row32 = jax.ShapeDtypeStruct((rows, width), F32)
    return pl.pallas_call(
        tail_kernel,
        in_specs=[TABLE] + [WHOLE] * 5 + [AWAY],
        out_specs=[WHOLE] * 4 + [AWAY] * 2,
        out_shape=[row16, row32, row16, jax.ShapeDtypeStruct((8, width), F32),
                   *pack_pair(144, width)],
        scratch_shapes=[
            pltpu.VMEM((width, width), BF16),
            pltpu.VMEM((width, 4 * width), BF16),
            pltpu.VMEM((4 * width, width), BF16),
            pltpu.VMEM((rows, width), F32),
            pltpu.VMEM((rows, width), BF16),
            pltpu.VMEM((rows, width), F32),
            pltpu.VMEM((rows, width), F32),
            pltpu.VMEM((rows, width), BF16),
            pltpu.VMEM((rows, width), F32),
            pltpu.VMEM((rows, width), F32),
            pltpu.VMEM((2, BLOCKS, 144, width), BF16),
            pltpu.SemaphoreType.DMA((4,)),
        ],
        compiler_params=pltpu.CompilerParams(vmem_limit_bytes=56 * MB),
        cost_estimate=pl.CostEstimate(flops=54 * rows * width * width, bytes_accessed=16 * MB, transcendentals=0),
        name="tail",
    )(place, crossed, m_d, ct, g_d, dest, pack)


def mid_back_kernel(
    place, dq, dk, dv, n_d, m_d, second_grad, a_d, memory, end, act, slope, n_e, m_e, a_e, g_e, g_d, pack,
    md_grad, ad_grad, me_grad, ae_grad, ge_grad, kept, sent,
    w_out, w_in, w_down, w_cross, w_query, prod, total, small, stage, sems,
):
    enc, dec = pack.at[0], pack.at[1]
    fetch_cross(dec, w_query, sems.at[5], (0,))
    fetch_out(dec, w_out.at[1], sems.at[3])
    fetch_cross(enc, w_cross, sems.at[4], (0, 1))
    fetch_ffn(enc, w_in, w_down, sems.at[pl.ds(1, 2)])
    fetch_out(enc, w_out.at[0], sems.at[0])
    count = m_d.shape[0]
    ge_grad[...] = jnp.zeros_like(ge_grad)

    def through_out(a, grad, result, section, offset):
        stage_rows(stage, offset, low(mm_tn(a[...], small[...])))
        result[...] = low(mm_nt(small[...], w_out[section]))

    stage_rows(stage, 176, low(mm_tn(n_d[...], dq[...])))
    wait_for(w_query, sems.at[5])
    prod[...] = mm_nt(dq[...], w_query[...])
    gain_d = g_d[1:2, :]

    def decoder(rows):
        part, _ = norm_back(m_d[rows, :], gain_d, prod[rows, :])
        whole = second_grad[rows, :] + part
        md_grad[rows, :] = whole
        small[rows, :] = low(whole)

    each_rows(count, decoder)
    wait_for(w_out.at[1], sems.at[3])
    through_out(a_d, md_grad, ad_grad, 1, 192)

    stage_rows(stage, 0, low(mm_tn(memory[...], dk[...])))
    stage_rows(stage, 16, low(mm_tn(memory[...], dv[...])))
    wait_for(w_cross, sems.at[4])
    prod[...] = mm_nt(dk[...], w_cross[:, 0:512])
    prod[...] += mm_nt(dv[...], w_cross[:, 512:1024])
    gain_two = g_e[2:3, :]

    def ending(rows):
        part, _ = norm_back(end[rows, :], gain_two, prod[rows, :])
        me_grad[rows, :] = part
        small[rows, :] = low(part)
        total[rows, :] = jnp.zeros_like(part)

    each_rows(count, ending)
    wait_for(w_in, sems.at[1])
    wait_for(w_down, sems.at[2])

    @pl.loop(0, 4)
    def _(c):
        cols = rows_at(c, 512)
        stage_down(stage, 32, c, low(mm_tn(act[:, cols], small[...])))
        prod[...] = mm_nt(small[...], w_down[cols, :])

        def body(rows):
            prod[rows, :] = prod[rows, :] * slope[rows, cols].astype(F32)

        each_rows(count, body)
        grad = low(prod[...])
        stage_inner(stage, 96, c, low(mm_tn(n_e[...], grad)))
        total[...] += mm_nt(grad, w_in[:, cols])

    gain_one = g_e[1:2, :]

    def encoder(rows):
        part, gained = norm_back(m_e[rows, :], gain_one, total[rows, :])
        ge_grad[...] += fold(gained)
        whole = me_grad[rows, :] + part
        me_grad[rows, :] = whole
        small[rows, :] = low(whole)

    each_rows(count, encoder)
    wait_for(w_out.at[0], sems.at[0])
    through_out(a_e, me_grad, ae_grad, 0, 160)
    send_stage(stage, kept, sent, place, sems.at[6])
    wait_for(stage, sems.at[6])


def mid_back(place, dq, dk, dv, n_d, m_d, second_grad, a_d, memory, end, act, slope, n_e, m_e, a_e, g_e, g_d, pack):
    rows, width = m_d.shape
    row16 = jax.ShapeDtypeStruct((rows, width), BF16)
    row32 = jax.ShapeDtypeStruct((rows, width), F32)
    return pl.pallas_call(
        mid_back_kernel,
        in_specs=[TABLE] + [WHOLE] * 16 + [AWAY],
        out_specs=[WHOLE] * 5 + [AWAY] * 2,
        out_shape=[row32, row16, row32, row16, jax.ShapeDtypeStruct((8, width), F32),
                   *pack_pair(208, width)],
        scratch_shapes=[
            pltpu.VMEM((2, width, width), BF16),
            pltpu.VMEM((width, 4 * width), BF16),
            pltpu.VMEM((4 * width, width), BF16),
            pltpu.VMEM((width, 2 * width), BF16),
            pltpu.VMEM((width, width), BF16),
            pltpu.VMEM((rows, width), F32),
            pltpu.VMEM((rows, width), F32),
            pltpu.VMEM((rows, width), BF16),
            pltpu.VMEM((2, BLOCKS, 208, width), BF16),
            pltpu.SemaphoreType.DMA((7,)),
        ],
        compiler_params=pltpu.CompilerParams(vmem_limit_bytes=56 * MB),
        cost_estimate=pl.CostEstimate(flops=52 * rows * width * width, bytes_accessed=30 * MB, transcendentals=0),
        name="mid_back",
    )(place, dq, dk, dv, n_d, m_d, second_grad, a_d, memory, end, act, slope, n_e, m_e, a_e, g_e, g_d, pack)


def front_w_kernel(place, qe, ke, ve, qd, kd, vd, n_e, n_d, ge_one, gd_two, ds_e, ds_d, ds_c, kept, sent, stage, sems):
    width = n_e.shape[1]
    for section, (grads, n) in enumerate((((qe, ke, ve), n_e), ((qd, kd, vd), n_d))):
        for i in range(3):
            grad = low(mm_tn(n[...], grads[i][...]))
            for j in range(BLOCKS):
                stage[section, j, 32 * i : 32 * i + 32, :] = grad[32 * j : 32 * j + 32, :]
    lane = lax.broadcasted_iota(jnp.int32, (8, width), 1)
    heads = jnp.zeros((8, width), F32)
    for i, ds in enumerate((ds_e, ds_d, ds_c)):
        heads = jnp.where(lane == i, jnp.sum(ds[...], axis=1, keepdims=True), heads)
    lines = [jnp.sum(g[...], axis=0, keepdims=True) for g in (ge_one, gd_two)]
    extra = low(jnp.concatenate(lines + [jnp.zeros((6, width), F32), heads], axis=0))
    for h in range(2):
        for j in range(BLOCKS):
            stage[h, j, 96:112, :] = extra
    send_stage(stage, kept, sent, place, sems.at[0])
    wait_for(stage, sems.at[0])


def front_w(place, grads_e, grads_d, n_e, n_d, ge_one, gd_two, ds):
    rows, width = n_e.shape
    return pl.pallas_call(
        front_w_kernel,
        in_specs=[TABLE] + [WHOLE] * 13,
        out_specs=[AWAY] * 2,
        out_shape=[*pack_pair(112, width)],
        scratch_shapes=[pltpu.VMEM((2, BLOCKS, 112, width), BF16), pltpu.SemaphoreType.DMA((1,))],
        compiler_params=pltpu.CompilerParams(vmem_limit_bytes=56 * MB),
        cost_estimate=pl.CostEstimate(flops=12 * rows * width * width, bytes_accessed=8 * MB, transcendentals=0),
        name="front_w",
    )(place, *grads_e, *grads_d, n_e, n_d, ge_one, gd_two, *ds)


def front_x_kernel(table, dq, dk, dv, x, m_grad, g, dest, own, other, x_grad, w, prod, high, rest, sems):
    fetch_front(table, own, other, w, sems.at[0])
    wait_for(w, sems.at[0])
    prod[...] = mm_nt(dq[...], w[:, 0:512])
    prod[...] += mm_nt(dk[...], w[:, 512:1024])
    prod[...] += mm_nt(dv[...], w[:, 1024:1536])
    gain = g[0:1, :]

    def body(rows):
        part, _ = norm_back(x[rows, :].astype(F32), gain, prod[rows, :])
        whole = m_grad[rows, :] + part
        high[rows, :] = low(whole)
        rest[rows, :] = low(whole - high[rows, :].astype(F32))

    each_rows(x.shape[0], body)
    place = places_of(dest)
    x_grad[...] = mm_tn(place, high[...])
    x_grad[...] += mm_tn(place, rest[...])


def front_x(table, grads, x, m_grad, g, dest, own, other):
    rows, width = x.shape
    return pl.pallas_call(
        front_x_kernel,
        in_specs=[TABLE] + [WHOLE] * 7 + [AWAY] * 2,
        out_specs=WHOLE,
        out_shape=jax.ShapeDtypeStruct((rows, width), F32),
        scratch_shapes=[
            pltpu.VMEM((width, 3 * width), BF16),
            pltpu.VMEM((rows, width), F32),
            pltpu.VMEM((rows, width), BF16),
            pltpu.VMEM((rows, width), BF16),
            pltpu.SemaphoreType.DMA((1,)),
        ],
        compiler_params=pltpu.CompilerParams(vmem_limit_bytes=56 * MB),
        cost_estimate=pl.CostEstimate(flops=6 * rows * width * width, bytes_accessed=6 * MB, transcendentals=0),
        name="front_x",
    )(table, *grads, x, m_grad, g, dest, own, other)


ORDER = ((4, 8, 1, 2), (4, 8, 2, 1))
SHIFT = np.array(
    [[functools.reduce(lambda a, b: a ^ b, [m for b, m in enumerate(order) if p >> b & 1], 0) for p in range(BLOCKS)] for order in ORDER],
    np.int32,
)
WHERE = np.argsort(SHIFT, axis=1).astype(np.int32)
SWAP = [(0, 1), (1, 0)]


def swap(value):
    return lax.ppermute(value, "section", SWAP)


def hop(value, bit):
    pairs = [
        (BLOCKS * s + i, BLOCKS * s + (i ^ ORDER[s][bit])) for s in range(2) for i in range(BLOCKS)
    ]
    return lax.ppermute(value, ("section", "dp"), pairs)


def jump(value, position):
    pairs = [
        (BLOCKS * s + i, BLOCKS * s + (i ^ int(SHIFT[s, position]))) for s in range(2) for i in range(BLOCKS)
    ]
    return lax.ppermute(value, ("section", "dp"), pairs)


def add(*terms):
    return low(sum(term.astype(F32) for term in terms))


def tie(value, held):
    return lax.optimization_barrier((value, held))


def halves(kept, came):
    cut = kept.shape[0] // 2
    return add(kept[:cut], came[:cut]), add(kept[cut:], came[cut:])


def plane(pair, bit):
    return halves(pair[0], hop(pair[1], bit))


def line(pair):
    parts = (pair[0][0], pair[0][1], pair[1][0], pair[1][1])
    came = [jump(parts[i], i) for i in (1, 2, 3)]
    return sum(part.astype(F32) for part in [parts[0]] + came)


def inner_of(halves):
    quarter, width = halves[0].shape
    rows = [h.reshape(quarter, 4, width // 4).transpose(1, 0, 2).reshape(4 * quarter, width // 4) for h in halves]
    return jnp.concatenate(rows, axis=0)


def spread_line(block):
    return jnp.stack([block] + [jump(block, i) for i in (1, 2, 3)])


def spread_plane(blocks, bit):
    return jnp.concatenate([blocks, hop(blocks, bit)], axis=0)


def weights_near(attn_qkv, attn_out, cross_proj, ffn_in, ffn_out, gains):
    me, section = lax.axis_index("dp"), lax.axis_index("section")
    gain_rows = jnp.pad(gains[0], ((0, 16 - gains.shape[1]), (0, 0)))
    kept, sent, second = pack_shards(
        jnp.stack([me, section]), attn_qkv[0], attn_out[0], cross_proj[0], ffn_in[0], ffn_out[0], gain_rows
    )
    came = swap(sent)
    enc, dec = jnp.where(section == 0, kept, came), jnp.where(section == 0, came, kept)
    enc = spread_line(enc)
    dec, enc = tie(dec, enc)
    enc, dec = tie(spread_plane(enc, 2), spread_line(dec))
    enc, dec = tie(spread_plane(enc, 3), spread_plane(dec, 2))
    enc = (enc, swap(enc))
    dec = spread_plane(dec, 3)
    pack = lax.all_gather(second, ("section", "dp"), axis=0, tiled=False)
    shift = jnp.asarray(SHIFT)
    table = jnp.stack([shift[section] ^ me, shift[1 - section] ^ me, jnp.full((BLOCKS,), section, jnp.int32)])
    where = jnp.asarray(WHERE)[:, jnp.arange(BLOCKS, dtype=jnp.int32) ^ me]
    halves = jnp.where(jnp.arange(BLOCKS) == section, 0, 1).astype(jnp.int32)
    return enc, dec, pack.reshape((2, BLOCKS) + second.shape), table, jnp.concatenate([where, halves[None]])


def weights_far(attn_qkv, attn_out, cross_proj, ffn_in, ffn_out, gains):
    def whole(shard, axis):
        return lax.all_gather(shard[0], "dp", axis=axis, tiled=True)

    qkv, out, cross, inner, down, gain = (
        whole(w, a) for w, a in ((attn_qkv, 0), (attn_out, 0), (cross_proj, 0), (ffn_in, 1), (ffn_out, 0), (gains, 1))
    )
    width = out.shape[1]
    gain_rows = jnp.zeros((BLOCKS, 16, width), BF16).at[0, : gain.shape[0]].set(gain)
    first = jnp.stack(jax.vmap(pack_first)(qkv.reshape(BLOCKS, -1, 3 * width), gain_rows))
    second = jax.vmap(pack_second)(
        out.reshape(BLOCKS, -1, width),
        cross.reshape(BLOCKS, -1, 2 * width),
        down.reshape(BLOCKS, -1, width),
        inner.reshape(width, BLOCKS, -1).transpose(1, 0, 2),
    )
    section = lax.axis_index("section")
    first_other, second_other = swap(first), swap(second)

    def both(mine, came):
        return jnp.where(section == 0, mine, came), jnp.where(section == 0, came, mine)

    enc, dec = both(first, first_other)
    pack = jnp.stack(both(second, second_other))
    plain = jnp.arange(BLOCKS, dtype=jnp.int32)
    table = jnp.stack([plain, plain, jnp.zeros_like(plain)])
    halves = jnp.where(plain == 0, 0, 1).astype(jnp.int32)
    return (enc[0], enc[1]), (dec[0], dec[1]), pack, table, jnp.stack([plain, plain, halves])


def meet(pack_a, pack_b):
    enc, dec = low(pack_b[0:176]), low(jnp.concatenate([pack_a, pack_b[176:208]], axis=0))
    came = lax.ppermute(enc, "section", [(1, 0)]), lax.ppermute(dec, "section", [(0, 1)])
    return (enc, came[0]), (came[1], dec)


def near_shards(met, last):
    section = lax.axis_index("section")
    e, d = met

    def rows(halves, start, count):
        return jnp.concatenate([h[start : start + count] for h in halves], axis=0)

    def side(*parts):
        return jnp.concatenate(parts, axis=1)

    enc = (
        rows(e, 160, 16),
        side(rows(e, 0, 16), rows(e, 16, 16)),
        inner_of([h[96:160] for h in e]),
        rows(e, 32, 64),
    )
    dec = (
        rows(d, 160, 16),
        side(rows(d, 144, 16), rows(d, 128, 16)),
        inner_of([h[64:128] for h in d]),
        rows(d, 0, 64),
    )
    qkv = side(*(last[32 * i : 32 * i + 32] for i in range(3)))
    rest = tuple(jnp.where(section == 0, a, b).astype(F32) for a, b in zip(enc, dec))
    return (qkv,) + rest, last[96:112]


def far_shards(tail_pack, mid_pack, front_pack):
    tail_pack, mid_pack, front_pack = (jnp.stack(p) for p in (tail_pack, mid_pack, front_pack))

    def qkv_of(pack):
        return jnp.concatenate([pack[:, 32 * i : 32 * i + 32].reshape(-1, pack.shape[2]) for i in range(3)], axis=1)
    def rows(pack, start, count):
        part = pack[:, :, start : start + count]
        return part.transpose(1, 0, 2, 3).reshape(-1, part.shape[-1])

    def inner(pack, start):
        blocks = jax.vmap(lambda a, b: inner_of([a, b]))(pack[0, :, start : start + 64], pack[1, :, start : start + 64])
        return blocks.transpose(1, 0, 2).reshape(blocks.shape[1], -1)

    def side(pack, *starts):
        return jnp.concatenate([rows(pack, s, 16) for s in starts], axis=1)

    enc = (qkv_of(front_pack[0]), rows(mid_pack, 160, 16), side(mid_pack, 0, 16), inner(mid_pack, 96), rows(mid_pack, 32, 64))
    cross_d = jnp.concatenate([rows(mid_pack, 176, 16), rows(tail_pack, 128, 16)], axis=1)
    dec = (qkv_of(front_pack[1]), rows(mid_pack, 192, 16), cross_d, inner(tail_pack, 64), rows(tail_pack, 0, 64))
    section = lax.axis_index("section")
    grads = []
    for a, b, axis in zip(enc, dec, (0, 0, 0, 1, 0)):
        mine = jnp.where(section == 0, a, b).astype(F32) + swap(jnp.where(section == 0, b, a)).astype(F32)
        grads.append(lax.psum_scatter(mine, "dp", scatter_dimension=axis, tiled=True))
    extra = lax.psum(front_pack[0, 0, 96:112].astype(F32), ("section", "dp"))
    return tuple(grads), extra


def gain_grads(weights, grads, gains, extra):
    section = lax.axis_index("section")
    qkv, cross = (w[0].astype(F32) * g for w, g in zip(weights, grads))
    gain = gains[0].astype(F32)
    columns = gain.shape[1]
    start = lax.axis_index("dp") * columns
    split = lax.dynamic_slice(extra, (section, start), (1, columns))[0]
    half = cross.shape[1] // 2
    reach = jnp.sum(cross[:, :half], axis=1)
    memory = (reach + jnp.sum(cross[:, half:], axis=1)) / gain[2]
    first = jnp.sum(qkv, axis=1) / gain[0]
    enc, dec = jnp.stack([first, split, memory]), jnp.stack([first, reach / gain[1], split])
    return jnp.where(section == 0, enc, dec)


def new_places(lengths, starts, rows):
    ends = jnp.cumsum(lengths)
    places = jnp.arange(rows, dtype=jnp.int32)
    pick = (places[:, None] >= (ends - lengths)[None, :]) & (places[:, None] < ends[None, :])
    return (places + jnp.sum(jnp.where(pick, (starts - ends + lengths)[None, :], 0), axis=1))[None]


def local(
    layer_input, cotangent, lengths, attn_qkv, attn_out, cross_proj, ffn_in, ffn_out, gains, alpha_raw
):
    section = lax.axis_index("section")
    near = lax.axis_size("dp") == BLOCKS
    weights = weights_near if near else weights_far
    first_e, first_d, pack, table, place = weights(attn_qkv, attn_out, cross_proj, ffn_in, ffn_out, gains)
    rows, width = layer_input.shape[3:]
    inputs = layer_input[0, :, 0]
    came = swap(lax.dynamic_index_in_dim(inputs, 1 - section, 0, keepdims=False))
    first = section == 0
    source, target = lax.dynamic_index_in_dim(lengths[:, :, 0], section, 1, keepdims=False)
    large_e, large_d = source == jnp.max(source), target == jnp.max(target)
    starts_e = starts_of(source, jnp.where(large_e, 0, jnp.where(large_d, 2, 1)))
    starts_d = starts_of(target, jnp.where(large_d, 0, jnp.where(large_e, 1, 2)))
    dest_e, dest_d = new_places(source, starts_e, rows), new_places(target, starts_d, rows)
    x_e, x_d, ct = sort_rows(section[None], inputs, came, cotangent[:, 0], dest_e, dest_d)
    head_width = width // alpha_raw.shape[1]
    gate = jax.nn.sigmoid(alpha_raw)
    coef = [coefs_of(0.25 + 0.25 * gate[i], head_width) for i in range(3)]
    marks_e = marks_of(starts_e, source, starts_e, source, rows, False)
    marks_d = marks_of(starts_d, target, starts_d, target, rows, True)
    marks_c = marks_of(starts_d, target, starts_e, source, rows, False)

    def settle(enc, dec):
        kept, came = jnp.where(first, enc, dec), swap(jnp.where(first, dec, enc))
        return jnp.stack([jnp.where(first, kept, came), jnp.where(first, came, kept)])[None, :, None]

    n_e, q_e, k_e, v_e, g_e = front(table, x_e, *first_e)
    if near:
        q_e, first_d = tie(q_e, first_d)
        first_d = (first_d, swap(first_d))
    a_e, *stats_e = attend(q_e, k_e, v_e, marks_e, coef[0])
    n_d, q_d, k_d, v_d, g_d = front(table, x_d, *first_d)
    a_d, *stats_d = attend(q_d, k_d, v_d, marks_d, coef[1])
    m_e, n1_e, act, slope, end, memory, mem_k, mem_v, m_d, n1_d, query, memory_out = mid(
        a_e, a_d, x_e, x_d, g_e, g_d, dest_e, pack
    )
    crossed, *stats_c = attend(query, mem_k, mem_v, marks_c, coef[2])
    result, second_grad, crossed_grad, gd_two, *pack_a = tail(place, crossed, m_d, ct, g_d, dest_d, pack)
    if near:
        came = swap(pack_a[1])
    else:
        outputs = settle(memory_out, result)
    query_grad, mk_grad, mv_grad, ds_c = attend_back(query, mem_k, mem_v, crossed_grad, stats_c, marks_c, coef[2])
    if near:
        query_grad, (pack_a, outputs) = tie(query_grad, (halves(pack_a[0], came), settle(memory_out, result)))
        pack_a = plane(pack_a, 3)
    md_grad, ad_grad, me_grad, ae_grad, ge_one, *pack_b = mid_back(
        place, query_grad, mk_grad, mv_grad, n1_d, m_d, second_grad, a_d, memory, end, act, slope, n1_e, m_e, a_e, g_e, g_d, pack
    )
    if near:
        (ad_grad, pack_b[1]), pack_a = tie((ad_grad, pack_b[1]), pack_a)
        pack_a = plane(pack_a, 2)
        came = swap(pack_b[1])
    *grads_d, ds_d = attend_back(q_d, k_d, v_d, ad_grad, stats_d, marks_d, coef[1])
    if near:
        ae_grad, (pack_a, pack_b, _) = tie(ae_grad, (pack_a, halves(pack_b[0], came), grads_d[0]))
        pack_a = line(pack_a)
        pack_b = plane(pack_b, 3)
    *grads_e, ds_e = attend_back(q_e, k_e, v_e, ae_grad, stats_e, marks_e, coef[0])
    if near:
        grads_e[0], (pack_a, pack_b) = tie(grads_e[0], (pack_a, pack_b))
        pack_b = plane(pack_b, 2)
    pack_c = list(front_w(place, grads_e, grads_d, n_e, n_d, ge_one, gd_two, (ds_e, ds_d, ds_c)))
    if near:
        came = swap(pack_c[1])
    xd_grad = front_x(table, grads_d, x_d, md_grad, g_d, dest_d, *first_d)
    if near:
        grads_e[0], (pack_c, pack_b, xd_grad) = tie(grads_e[0], (halves(pack_c[0], came), pack_b, xd_grad))
        pack_c = plane(pack_c, 3)
        pack_b = line(pack_b)
    xe_grad = front_x(table, grads_e, x_e, me_grad, g_e, dest_e, *first_e)
    if near:
        pack_c, (pack_b, xe_grad) = tie(pack_c, (pack_b, xe_grad))
        pack_c = plane(pack_c, 2)
        met = meet(pack_a, pack_b)
        input_grad = settle(xe_grad, xd_grad)
        pack_c, (met, input_grad) = tie(pack_c, (met, input_grad))
        pack_c = line(pack_c)
        grads, extra = near_shards(met, pack_c)
    else:
        input_grad = settle(xe_grad, xd_grad)
        grads, extra = far_shards(tail_pack=pack_a, mid_pack=pack_b, front_pack=pack_c)
    ds = extra[8:16, 0:3].T
    grads += (gain_grads((attn_qkv, cross_proj), (grads[0], grads[2]), gains, extra),)
    alpha_grad = ds * 0.25 * gate * (1.0 - gate)
    return (outputs, input_grad) + tuple(g[None] for g in grads) + (alpha_grad,)


def solution(mesh):
    return jax.shard_map(
        local,
        mesh=mesh,
        in_specs=(
            P("section", None, "dp", None, None),
            P(None, "dp", None, None),
            P(None, None, "dp", None),
            P("section", "dp", None),
            P("section", "dp", None),
            P("section", "dp", None),
            P("section", None, "dp"),
            P("section", "dp", None),
            P("section", None, "dp"),
            P(),
        ),
        out_specs=(
            P("section", None, "dp", None, None),
            P("section", None, "dp", None, None),
            P("section", "dp", None),
            P("section", "dp", None),
            P("section", "dp", None),
            P("section", None, "dp"),
            P("section", "dp", None),
            P("section", None, "dp"),
            P(),
        ),
        check_vma=False,
    )
```

```python
import functools
import math

import jax
import jax.numpy as jnp
import numpy as np
from jax import lax
from jax.experimental import pallas as pl
from jax.experimental.pallas import tpu as pltpu
from jax.sharding import PartitionSpec as P

SHARP = 0.0625
NEG = -1e9
EPS = 1e-5
TINY = 1e-37
LOG2E = 1.4426950408889634
PART = 256
CHUNK = 128
TILE = 128
BLOCKS = 16
MB = 1 << 20
COST = 1000
LIMIT = 52 * MB
F32, BF16 = jnp.float32, jnp.bfloat16
WHOLE = pl.BlockSpec(memory_space=pltpu.VMEM)
TABLE = pl.BlockSpec(memory_space=pltpu.SMEM)
AWAY = pl.BlockSpec(memory_space=pl.ANY)


def mm(a, b):
    return jnp.dot(a, b, preferred_element_type=F32)


def mm_nt(a, b):
    return lax.dot_general(a, b, (((1,), (1,)), ((), ())), preferred_element_type=F32)


def mm_tn(a, b):
    return lax.dot_general(a, b, (((0,), (0,)), ((), ())), preferred_element_type=F32)


def low(v):
    return v.astype(BF16)


class Moves:
    def __init__(self, pairs_in, pairs_out, sems):
        self.copies = {}
        for i, (src, dst) in enumerate(pairs_in):
            self.copies[id(dst)] = pltpu.make_async_copy(src, dst, sems.at[i])
            self.copies[id(dst)].start()
        self.outs = {
            id(src): pltpu.make_async_copy(src, dst, sems.at[len(pairs_in) + i])
            for i, (src, dst) in enumerate(pairs_out)
        }
        self.left = []

    def ready(self, *refs):
        for ref in refs:
            copy = self.copies.pop(id(ref), None)
            if copy is not None:
                copy.wait()

    def done(self, *refs):
        for ref in refs:
            copy = self.outs.pop(id(ref), None)
            if copy is not None:
                copy.start()
                self.left.append(copy)

    def finish(self):
        assert not self.copies and not self.outs
        for copy in self.left:
            copy.wait()


class Near:
    def __init__(self, array):
        self.array = array


class Both(Near):
    pass


def call_dense(body, name, us, tables, ins, far, outs, far_outs, scratch):
    near_in = [isinstance(a, Near) for a in ins]
    near_out = [isinstance(a, Near) for a in outs]
    away_out = [not isinstance(a, Near) or isinstance(a, Both) for a in outs]
    ins = [a.array if isinstance(a, Near) else a for a in ins]
    outs = [a.array if isinstance(a, Near) else a for a in outs]
    bufs_in = [a for a, near in zip(ins, near_in) if not near]
    bufs_out = [a for a, near in zip(outs, near_out) if not near]
    lone = [a for a, near in zip(outs, near_out) if near]
    sent = [a for a, away in zip(outs, away_out) if away]
    counts = [len(g) for g in (tables, ins, far, lone, sent, far_outs, bufs_in, bufs_out)]

    def kernel(*refs):
        groups, at = [], 0
        for count in counts:
            groups.append(list(refs[at : at + count]))
            at += count
        table_refs, in_refs, far_refs, lone_refs, sent_refs, far_out_refs, in_bufs, out_bufs = groups
        in_local = [ref if near else in_bufs.pop(0) for ref, near in zip(in_refs, near_in)]
        out_local = [lone_refs.pop(0) if near else out_bufs.pop(0) for near in near_out]
        pairs_in = [(ref, buf) for ref, buf, near in zip(in_refs, in_local, near_in) if not near]
        pairs_out = [(buf, sent_refs.pop(0)) for buf, away in zip(out_local, away_out) if away]
        moves = Moves(pairs_in, pairs_out, refs[at])
        body(moves, *table_refs, *in_local, *far_refs, *out_local, *far_out_refs, *refs[at + 1 :])
        moves.finish()

    got = pl.pallas_call(
        kernel,
        in_specs=[TABLE] * len(tables) + [WHOLE if near else AWAY for near in near_in] + [AWAY] * len(far),
        out_specs=[WHOLE] * len(lone) + [AWAY] * (len(sent) + len(far_outs)),
        out_shape=[*lone, *sent, *far_outs],
        scratch_shapes=[pltpu.VMEM(a.shape, a.dtype) for a in (*bufs_in, *bufs_out)]
        + [pltpu.SemaphoreType.DMA((max(1, len(bufs_in) + len(sent)),)), *scratch],
        compiler_params=pltpu.CompilerParams(vmem_limit_bytes=LIMIT),
        cost_estimate=pl.CostEstimate(flops=us * COST, transcendentals=0, bytes_accessed=us * COST // 400),
        name=name,
    )(*tables, *ins, *far)
    lone_got, sent_got = list(got[: len(lone)]), list(got[len(lone) : len(lone) + len(sent)])
    result = []
    for near, away in zip(near_out, away_out):
        pair = (lone_got.pop(0) if near else None, sent_got.pop(0) if away else None)
        result.append(pair if near and away else pair[0] if near else pair[1])
    return result + list(got[len(lone) + len(sent) :])


def fold(block):
    return jnp.sum(block.reshape(block.shape[0] // 8, 8, block.shape[1]), axis=0)


def fold_max(block):
    return jnp.max(block.reshape(block.shape[0] // 8, 8, block.shape[1]), axis=0)


def rows_of(parts, op):
    return jnp.concatenate([op(part, axis=0, keepdims=True) for part in parts], axis=0)


def per_head(coef, which, heads):
    place = lax.broadcasted_iota(jnp.int32, (heads, TILE), 0)
    out = jnp.zeros((heads, TILE), F32)
    for h in range(heads):
        out = jnp.where(place == h, coef[which, h], out)
    return out


def bias_of(lo, hi, start):
    place = lax.broadcasted_iota(jnp.int32, (CHUNK, TILE), 0) + start
    return jnp.where(jnp.logical_and(place >= lo, place < hi), 0.0, NEG)


def pair_of(h, width):
    return slice(h // 2 * 2 * width, (h // 2 + 1) * 2 * width)


def split_pairs(dst, turned, heads, width):
    for h in range(heads):
        block = turned[pair_of(h, width), :]
        mine = lax.broadcasted_iota(jnp.int32, block.shape, 0) // width == h % 2
        dst[h] = jnp.where(mine, block, jnp.zeros_like(block))


def fold(block):
    return jnp.sum(block.reshape(block.shape[0] // 8, 8, block.shape[1]), axis=0)


def fold_max(block):
    return jnp.max(block.reshape(block.shape[0] // 8, 8, block.shape[1]), axis=0)


def rows_of(parts, op):
    return jnp.concatenate([op(part, axis=0, keepdims=True) for part in parts], axis=0)


def per_head(coef, which, heads):
    place = lax.broadcasted_iota(jnp.int32, (heads, TILE), 0)
    out = jnp.zeros((heads, TILE), F32)
    for h in range(heads):
        out = jnp.where(place == h, coef[which, h], out)
    return out


def bias_of(lo, hi, start):
    place = lax.broadcasted_iota(jnp.int32, (CHUNK, TILE), 0) + start
    return jnp.where(jnp.logical_and(place >= lo, place < hi), 0.0, NEG)


def pair_of(h, width):
    return slice(h // 2 * 2 * width, (h // 2 + 1) * 2 * width)


def chunk_at(c):
    return pl.ds(pl.multiple_of(c * CHUNK, CHUNK), CHUNK)


def split_pairs(dst, turned, heads, width):
    for h in range(heads):
        block = turned[pair_of(h, width), :]
        mine = lax.broadcasted_iota(jnp.int32, block.shape, 0) // width == h % 2
        dst[h] = jnp.where(mine, block, jnp.zeros_like(block))


def clear_outside(first, last, keys, refs, cols):
    def blank(c, carry):
        for ref in refs:
            for h in range(ref.shape[0]):
                ref[h, chunk_at(c), cols] = jnp.zeros((CHUNK, TILE), BF16)
        return carry

    lax.fori_loop(0, first, blank, 0)
    lax.fori_loop(last, keys // CHUNK, blank, 0)


def meets(first, last, half):
    per = PART // CHUNK
    return jnp.logical_and(first < (half + 1) * per, last > half * per)


def attend_kernel(
    span, coef, lo_ref, hi_ref, q_ref, k_ref, v_ref, o_ref, tau_ref, top_ref, inv_ref, v_t, zs, ps, qz, o_t
):
    heads, keys = zs.shape[0], zs.shape[1]
    width = q_ref.shape[1] // heads
    tile = pl.program_id(0)

    @pl.when(tile == 0)
    def _():
        v_t[...] = v_ref[...].T

    split_pairs(qz, q_ref[...].T, heads, width)
    lo, hi = lo_ref[...], hi_ref[...]
    first, last = span[0, tile], span[1, tile]

    def scores(c, tops):
        here = chunk_at(c)
        bias = bias_of(lo, hi, c * CHUNK)
        out = []
        for h in range(heads):
            z = mm(k_ref[here, pair_of(h, width)], qz[h]) * coef[0, h] + bias
            zs[h, here, :] = z
            out.append(jnp.maximum(tops[h], fold_max(z)))
        return tuple(out)

    tops = lax.fori_loop(
        first, last, scores, tuple(jnp.full((8, TILE), -3e38, F32) for _ in range(heads))
    )
    peak = rows_of(tops, jnp.max)
    shrink, exponent = per_head(coef, 1, heads), per_head(coef, 4, heads)
    least = peak - 1.0
    most = peak - jnp.exp2(-shrink * jnp.log2((hi - lo).astype(F32)))
    close = 4e-6 + 5e-7 * jnp.abs(peak)
    zero = tuple(jnp.zeros((8, TILE), F32) for _ in range(3 * heads))

    def search(state):
        turn, tau, _ = state

        def body(c, sums):
            here = chunk_at(c)
            out = []
            for h in range(heads):
                u = jnp.maximum(zs[h, here, :] - tau[h : h + 1, :], TINY)
                curve = jnp.exp2(jnp.log2(u) * coef[3, h])
                slope = curve * u
                out += [sums[3 * h] + fold(slope * u), sums[3 * h + 1] + fold(slope), sums[3 * h + 2] + fold(curve)]
            return tuple(out)

        sums = lax.fori_loop(first, last, body, zero)
        mass, slope, curve = (rows_of(sums[i::3], jnp.sum) for i in range(3))
        bend = jnp.clip(1.0 - (exponent - 1.0) * curve * mass / (exponent * slope * slope), 0.0, 1.0)
        bend = jnp.where(turn < 5, bend, shrink)
        log_mass = jnp.log(mass)
        x = bend * log_mass
        rise = jnp.where(
            jnp.abs(x) < 0.1,
            log_mass * (1.0 - x * (0.5 - x * (1.0 / 6.0))),
            (1.0 - jnp.exp(-x)) / jnp.maximum(bend, 1e-6),
        )
        new = jnp.clip(tau + mass / (exponent * slope) * rise, least, most)
        return turn + 1, new, jnp.max(jnp.abs(new - tau))

    def finish(state):
        turn, tau, _, _, _ = state
        turn, tau, _ = lax.while_loop(
            lambda s: jnp.logical_and(s[2] > 6e-3, s[0] < 40), search, (turn, tau, jnp.float32(1.0))
        )

        def final(c, sums):
            here = chunk_at(c)
            out = []
            for h in range(heads):
                z = zs[h, here, :]
                u = jnp.maximum(z - tau[h : h + 1, :], TINY)
                slope = jnp.exp2(jnp.log2(u) * coef[2, h])
                p = slope * u
                ps[h, here, :] = low(p)
                soft = jnp.exp2((z - peak[h : h + 1, :]) * (LOG2E / SHARP))
                out += [sums[3 * h] + fold(p), sums[3 * h + 1] + fold(slope), sums[3 * h + 2] + fold(soft)]
            return tuple(out)

        sums = lax.fori_loop(first, last, final, zero)
        mass, slope, soft = (rows_of(sums[i::3], jnp.sum) for i in range(3))
        off = (mass - 1.0) / (exponent * slope)
        open_ = jnp.max(jnp.where(jnp.abs(off) > close, 1.0, 0.0))
        return turn, jnp.where(open_ > 0.0, jnp.clip(tau + off, least, most), tau), open_, mass, soft

    blank = jnp.ones((heads, TILE), F32)
    _, tau, _, mass, soft = lax.while_loop(
        lambda s: jnp.logical_and(s[2] > 0.0, s[0] < 40), finish, (0, least, jnp.float32(1.0), blank, blank)
    )
    inv = 1.0 / mass
    tau_ref[...] = tau
    top_ref[...] = peak + SHARP * jnp.log(soft)
    inv_ref[...] = inv
    clear_outside(first, last, keys, (ps,), slice(None))
    o_t[...] = jnp.zeros_like(o_t)
    for half in range(keys // PART):
        cols = slice(half * PART, (half + 1) * PART)

        @pl.when(meets(first, last, half))
        def _():
            for h in range(heads):
                rows = slice(h * width, (h + 1) * width)
                o_t[rows, :] += mm(v_t[rows, cols], ps[h, cols, :])

    for h in range(0, heads, 2):
        got = [o_t[i * width : (i + 1) * width, :] * inv[i : i + 1, :] for i in (h, h + 1)]
        o_ref[:, pair_of(h, width)] = low(jnp.concatenate(got, axis=0).T)


def attend(q, k, v, marks, coef):
    lo, hi, span = marks
    rows, width = q.shape
    keys, heads = k.shape[0], coef.shape[1]
    line = pl.BlockSpec((1, TILE), lambda t, *_: (0, t))
    tile = pl.BlockSpec((TILE, width), lambda t, *_: (t, 0))
    stat = pl.BlockSpec((heads, TILE), lambda t, *_: (0, t))
    full = pl.BlockSpec((keys, width), lambda t, *_: (0, 0))
    return pl.pallas_call(
        attend_kernel,
        grid_spec=pltpu.PrefetchScalarGridSpec(
            num_scalar_prefetch=2,
            grid=(rows // TILE,),
            in_specs=[line, line, tile, full, full],
            out_specs=[tile, stat, stat, stat],
            scratch_shapes=[
                pltpu.VMEM((width, keys), BF16),
                pltpu.VMEM((heads, keys, TILE), F32),
                pltpu.VMEM((heads, keys, TILE), BF16),
                pltpu.VMEM((heads, 2 * width // heads, TILE), BF16),
                pltpu.VMEM((width, TILE), F32),
            ],
        ),
        out_shape=[jax.ShapeDtypeStruct((rows, width), BF16)]
        + [jax.ShapeDtypeStruct((heads, rows), F32)] * 3,
        compiler_params=pltpu.CompilerParams(vmem_limit_bytes=24 * MB),
        cost_estimate=pl.CostEstimate(flops=14 * COST, transcendentals=0, bytes_accessed=14 * COST // 400),
        name="attend",
    )(span, coef, lo, hi, q, k, v)


def attend_back_kernel(
    span, coef, lo_ref, hi_ref, q_ref, go_ref, tau_ref, top_ref, inv_ref, q_all, go_all, k_ref, v_ref,
    dq_ref, dk_ref, dv_ref, ds_ref, k_t, zs, gs, ls, qz, gz, g_all, p_all, dq_t, dk_sum, dv_sum,
):
    heads, keys = zs.shape[0], zs.shape[1]
    width = q_ref.shape[1] // heads
    scale = 1.0 / math.sqrt(width)
    tile = pl.program_id(0)
    at = pl.ds(pl.multiple_of(tile * TILE, TILE), TILE)

    @pl.when(tile == 0)
    def _():
        k_t[...] = k_ref[...].T
        ds_ref[...] = jnp.zeros_like(ds_ref)

    split_pairs(qz, q_ref[...].T, heads, width)
    split_pairs(gz, go_ref[...].T, heads, width)
    lo, hi = lo_ref[...], hi_ref[...]
    tau, top, inv = tau_ref[...], top_ref[...], inv_ref[...]
    first, last = span[0, tile], span[1, tile]
    kinds = 5
    zero = tuple(jnp.zeros((8, TILE), F32) for _ in range(kinds * heads))

    def gather(c, sums):
        here = chunk_at(c)
        bias = bias_of(lo, hi, c * CHUNK)
        out = []
        for h in range(heads):
            z = mm(k_ref[here, pair_of(h, width)], qz[h]) * coef[0, h] + bias
            g = mm(v_ref[here, pair_of(h, width)], gz[h])
            u = jnp.maximum(z - tau[h : h + 1, :], TINY)
            log_u = jnp.log2(u)
            slope = jnp.exp2(log_u * coef[2, h])
            p = slope * u
            p_log = p * log_u
            zs[h, here, :] = z
            gs[h, here, :] = g
            ls[h, here, :] = slope
            new = (g * p, g * slope, slope, g * p_log, p_log)
            out += [sums[kinds * h + i] + fold(new[i]) for i in range(kinds)]
        return tuple(out)

    sums = lax.fori_loop(first, last, gather, zero)
    gp, gl, ll, gpl, pl_sum = (rows_of(sums[i::kinds], jnp.sum) for i in range(kinds))
    shrink = per_head(coef, 1, heads)
    inv_k = per_head(coef, 4, heads) * inv
    mean = gp * inv
    drop = inv_k * (gl - mean * ll)
    grad_k = inv * (gpl - mean * pl_sum) * (1.0 / LOG2E)
    clear_outside(first, last, keys, (g_all, p_all), at)

    def final(c, sums):
        here = chunk_at(c)
        out = []
        for h in range(heads):
            one = slice(h, h + 1)
            z, slope = zs[h, here, :], ls[h, here, :]
            p = slope * jnp.maximum(z - tau[one], TINY)
            r = (gs[h, here, :] - mean[one]) * slope * inv_k[one]
            g_z = r - drop[one] * jnp.exp2((z - top[one]) * (LOG2E / SHARP))
            g_all[h, here, at] = low(g_z * coef[1, h])
            p_all[h, here, at] = low(p * inv[one])
            out.append(sums[h] + fold(g_z * z))
        return tuple(out)

    sums = lax.fori_loop(first, last, final, zero[:heads])
    ds_ref[...] += rows_of(sums, jnp.sum) / shrink - grad_k / (shrink * shrink)
    dq_t[...] = jnp.zeros_like(dq_t)
    for half in range(keys // PART):
        cols = slice(half * PART, (half + 1) * PART)

        @pl.when(meets(first, last, half))
        def _():
            for h in range(heads):
                rows = slice(h * width, (h + 1) * width)
                dq_t[rows, :] += mm(k_t[rows, cols], g_all[h, cols, at])

    for h in range(0, heads, 2):
        dq_ref[:, pair_of(h, width)] = low(dq_t[pair_of(h, width), :].T * scale)

    @pl.when(tile == pl.num_programs(0) - 1)
    def _():
        dk_sum[...] = jnp.zeros_like(dk_sum)
        dv_sum[...] = jnp.zeros_like(dv_sum)
        tiles = PART // TILE
        lane = lax.broadcasted_iota(jnp.int32, (PART, 2 * width), 1) // width
        blank_rows = jnp.zeros((PART, 2 * width), BF16)
        for q_half in range(q_all.shape[0] // PART):
            rows = slice(q_half * PART, (q_half + 1) * PART)
            for half in range(keys // PART):
                cols = slice(half * PART, (half + 1) * PART)
                reach = [
                    meets(span[0, t], span[1, t], half) for t in range(q_half * tiles, (q_half + 1) * tiles)
                ]

                @pl.when(functools.reduce(jnp.logical_or, reach))
                def _():
                    for h in range(0, heads, 2):
                        pair = pair_of(h, width)
                        for i in (h, h + 1):
                            mine = lane == i % 2
                            dk_sum[cols, pair] += mm(g_all[i, cols, rows], jnp.where(mine, q_all[rows, pair], blank_rows))
                            dv_sum[cols, pair] += mm(p_all[i, cols, rows], jnp.where(mine, go_all[rows, pair], blank_rows))

        dk_ref[...] = low(dk_sum[...] * scale)
        dv_ref[...] = low(dv_sum[...])


def attend_back(q, k, v, go, stats, marks, coef):
    lo, hi, span = marks
    rows, width = q.shape
    keys, heads = k.shape[0], coef.shape[1]
    line = pl.BlockSpec((1, TILE), lambda t, *_: (0, t))
    tile = pl.BlockSpec((TILE, width), lambda t, *_: (t, 0))
    stat = pl.BlockSpec((heads, TILE), lambda t, *_: (0, t))
    q_full = pl.BlockSpec((rows, width), lambda t, *_: (0, 0))
    k_full = pl.BlockSpec((keys, width), lambda t, *_: (0, 0))
    return pl.pallas_call(
        attend_back_kernel,
        grid_spec=pltpu.PrefetchScalarGridSpec(
            num_scalar_prefetch=2,
            grid=(rows // TILE,),
            in_specs=[line, line, tile, tile, stat, stat, stat, q_full, q_full, k_full, k_full],
            out_specs=[tile, k_full, k_full, pl.BlockSpec((heads, TILE), lambda t, *_: (0, 0))],
            scratch_shapes=[pltpu.VMEM((width, keys), BF16)]
            + [pltpu.VMEM((heads, keys, TILE), F32)] * 3
            + [pltpu.VMEM((heads, 2 * width // heads, TILE), BF16)] * 2
            + [pltpu.VMEM((heads, keys, rows), BF16)] * 2
            + [pltpu.VMEM((width, TILE), F32)]
            + [pltpu.VMEM((keys, width), F32)] * 2,
        ),
        out_shape=[
            jax.ShapeDtypeStruct((rows, width), BF16),
            jax.ShapeDtypeStruct((keys, width), BF16),
            jax.ShapeDtypeStruct((keys, width), BF16),
            jax.ShapeDtypeStruct((heads, TILE), F32),
        ],
        compiler_params=pltpu.CompilerParams(vmem_limit_bytes=36 * MB),
        cost_estimate=pl.CostEstimate(flops=14 * COST, transcendentals=0, bytes_accessed=14 * COST // 400),
        name="attend_back",
    )(span, coef, lo, hi, q, go, *stats, q, go, k, v)


def starts_of(lengths, rank):
    number = jnp.arange(lengths.shape[0])
    before = rank[None, :] < rank[:, None]
    before |= (rank[None, :] == rank[:, None]) & (number[None, :] < number[:, None])
    return jnp.sum(jnp.where(before, lengths[None, :], 0), axis=1)


def marks_of(q_starts, q_lengths, k_starts, k_lengths, rows, causal):
    places = jnp.arange(rows, dtype=jnp.int32)
    pick = (places[:, None] >= q_starts[None, :]) & (places[:, None] < (q_starts + q_lengths)[None, :])
    lo = jnp.sum(jnp.where(pick, k_starts[None, :], 0), axis=1)
    hi = jnp.sum(jnp.where(pick, (k_starts + k_lengths)[None, :], 0), axis=1)
    if causal:
        hi = jnp.minimum(hi, places + 1)
    first = jnp.min(lo.reshape(-1, TILE), axis=1) // CHUNK
    last = (jnp.max(hi.reshape(-1, TILE), axis=1) + CHUNK - 1) // CHUNK
    return (lo[None], hi[None], jnp.stack([first, last]))


def coefs_of(shrink, width):
    exponent = 1.0 / shrink
    return jnp.stack([shrink / math.sqrt(width), shrink, exponent - 1.0, exponent - 2.0, exponent])


OUT, CROSS, DOWN, IN, SECOND = 0, 32, 96, 224, 352
GAIN, FIRST = 48, 64


def pack_first(qkv, gain_rows):
    width = qkv.shape[-1] // 3
    parts = [qkv[:, i * width : (i + 1) * width] for i in range(3)]
    tails = (gain_rows, jnp.zeros_like(gain_rows))
    return [
        jnp.concatenate([p[16 * h : 16 * h + 16] for p in parts] + [tails[h]], axis=0) for h in range(2)
    ]


def pack_second(out, cross, down, inner):
    width = out.shape[-1]
    quarter = inner.shape[0] // 4
    turned = inner.reshape(4, quarter, inner.shape[1]).transpose(1, 0, 2).reshape(quarter, -1)
    return jnp.concatenate([out, cross[:, :width], cross[:, width:], down, turned], axis=0)


def pack_kernel(me, qkv, out, cross, inner, down, gains, kept, sent, second):
    width = out.shape[1]
    columns = gains.shape[1]
    spot = lax.broadcasted_iota(jnp.int32, (columns, width), 1) - me[0] * columns
    here = spot == lax.broadcasted_iota(jnp.int32, (columns, width), 0)
    spread = low(mm(gains[...], jnp.where(here, 1.0, 0.0).astype(BF16)))
    for h in range(2):
        for mine, dst in ((True, kept), (False, sent)):

            @pl.when((me[1] == h) == mine)
            def _():
                for i in range(3):
                    dst[16 * i : 16 * i + 16, :] = qkv[16 * h : 16 * h + 16, width * i : width * (i + 1)]
                dst[GAIN : GAIN + 16, :] = spread if h == 0 else jnp.zeros_like(spread)

    second[OUT : OUT + 32, :] = out[...]
    for i in range(2):
        second[CROSS + 32 * i : CROSS + 32 * i + 32, :] = cross[:, width * i : width * (i + 1)]
    second[DOWN : DOWN + 128, :] = down[...]
    for i in range(4):
        second[IN : IN + 128, 128 * i : 128 * (i + 1)] = inner[128 * i : 128 * (i + 1), :]


def pack_shards(me, qkv, out, cross, inner, down, gains):
    width = out.shape[1]
    half = jax.ShapeDtypeStruct((FIRST, width), BF16)
    return pl.pallas_call(
        pack_kernel,
        in_specs=[TABLE] + [WHOLE] * 6,
        out_specs=[WHOLE] * 3,
        out_shape=[half, half, jax.ShapeDtypeStruct((SECOND, width), BF16)],
        name="pack_shards",
    )(me, qkv, out, cross, inner, down, gains)


def rows_at(block, rows):
    return pl.ds(pl.multiple_of(block * rows, rows), rows)


def start_rows(src, block_of, dst, dst_block, rows, offset, cols, sem):
    pltpu.make_async_copy(
        src.at[block_of, pl.ds(offset, rows), :], dst.at[rows_at(dst_block, rows), cols], sem
    ).start()


def start_inner(src, block, dst, sem):
    cols = rows_at(block, 128)
    for i in range(4):
        pltpu.make_async_copy(
            src.at[block, pl.ds(IN, 128), pl.ds(128 * i, 128)], dst.at[pl.ds(128 * i, 128), cols], sem
        ).start()


def wait_for(ref, sem):
    pltpu.make_async_copy(ref, ref, sem).wait()


def fetch_out(src, dst, sem):
    @pl.loop(0, BLOCKS)
    def _(j):
        start_rows(src, j, dst, j, 32, OUT, slice(None), sem)


def fetch_cross(src, dst, sem, which):
    @pl.loop(0, BLOCKS)
    def _(j):
        for n, i in enumerate(which):
            start_rows(src, j, dst, j, 32, CROSS + 32 * i, pl.ds(512 * n, 512), sem)


def fetch_ffn(src, inner, down, sems):
    @pl.loop(0, BLOCKS)
    def _(j):
        start_inner(src, j, inner, sems.at[0])

    @pl.loop(0, BLOCKS)
    def _(j):
        start_rows(src, j, down, j, 128, DOWN, slice(None), sems.at[1])


def pack_pair(rows, width):
    return [jax.ShapeDtypeStruct((BLOCKS, rows, width), BF16)] * 2


def stage_rows(stage, offset, grad):
    for j in range(BLOCKS):
        for h in range(2):
            stage[h, j, offset : offset + 16, :] = grad[32 * j + 16 * h : 32 * j + 16 * h + 16, :]


def stage_down(stage, offset, c, grad):
    for j in range(4):
        for h in range(2):
            at = 128 * j + 64 * h
            stage[h, 4 * c + j, offset : offset + 64, :] = grad[at : at + 64, :]


def stage_inner(stage, offset, c, grad):
    for j in range(4):
        for h in range(2):
            for i in range(4):
                at = 256 * h + 64 * i
                stage[h, 4 * c + j, offset : offset + 64, 128 * i : 128 * (i + 1)] = grad[
                    at : at + 64, 128 * j : 128 * (j + 1)
                ]


def send_stage(stage, kept, sent, place, sem):
    for h in range(2):
        for which, dst in enumerate((kept, sent)):

            @pl.when(place[2, h] == which)
            def _():
                @pl.loop(0, BLOCKS)
                def _(j):
                    pltpu.make_async_copy(stage.at[h, j], dst.at[place[h, j]], sem).start()


STEP = 64


def each_rows(rows, body):
    for i in range(rows // STEP):
        body(slice(i * STEP, (i + 1) * STEP))


def centred(v):
    shifted = v - jnp.mean(v, axis=-1, keepdims=True)
    rate = lax.rsqrt(jnp.mean(shifted * shifted, axis=-1, keepdims=True) + EPS)
    return shifted * rate, rate


def norm_back(v, gain, grad):
    unit, rate = centred(v)
    e = grad * gain
    back = e - jnp.mean(e, axis=-1, keepdims=True) - unit * jnp.mean(e * unit, axis=-1, keepdims=True)
    return back * rate, grad * unit


def gelu_parts(u):
    phi = 0.5 + 0.5 * lax.erf(u * (1.0 / math.sqrt(2.0)))
    bell = jnp.exp2(u * u * (-0.5 * LOG2E)) * (1.0 / math.sqrt(2.0 * math.pi))
    return u * phi, phi + u * bell


def places_of(dest):
    rows = dest.shape[1]
    return jnp.where(lax.broadcasted_iota(jnp.int32, (rows, rows), 0) == dest[...], 1.0, 0.0).astype(BF16)


def sort_kernel(section, inputs, came, cotangent, dest_e, dest_d, x_e, x_d, ct):
    s = section[0]
    place_e, place_d = places_of(dest_e), places_of(dest_d)
    for owner, dst, place in ((0, x_e, place_e), (1, x_d, place_d)):

        @pl.when(s == owner)
        def _():
            dst[...] = low(mm(place, inputs[s]))

        @pl.when(s != owner)
        def _():
            dst[...] = low(mm(place, came[...]))

    ct[...] = low(mm(place_d, cotangent[s]))


def sort_rows(section, inputs, came, cotangent, dest_e, dest_d):
    row16 = jax.ShapeDtypeStruct(came.shape, BF16)
    return pl.pallas_call(
        sort_kernel,
        in_specs=[TABLE] + [WHOLE] * 5,
        out_specs=[WHOLE] * 3,
        out_shape=[row16] * 3,
        compiler_params=pltpu.CompilerParams(vmem_limit_bytes=10 * MB),
        name="sort_rows",
    )(section, inputs, came, cotangent, dest_e, dest_d)


def fetch_front(table, own, other, w, sem):
    for which, src in enumerate((own, other)):
        half = table[2, 0] if which == 0 else 1 - table[2, 0]

        @pl.loop(0, BLOCKS)
        def _(p):
            at = pl.ds(pl.multiple_of(32 * table[which, p] + 16 * half, 16), 16)
            for i in range(3):
                pltpu.make_async_copy(
                    src.at[p, pl.ds(16 * i, 16), :], w.at[at, pl.ds(512 * i, 512)], sem
                ).start()


def front_kernel(moves, table, x, own, other, n, q, k, v, g, w, gs, prod, sems):
    for which, src in enumerate((own, other)):

        @pl.loop(0, BLOCKS)
        def _(p):
            pltpu.make_async_copy(src.at[p, pl.ds(GAIN, 16), :], gs.at[which, p], sems.at[1]).start()

    fetch_front(table, own, other, w, sems.at[0])
    wait_for(gs, sems.at[1])
    gains = jnp.sum(gs[...].astype(F32), axis=(0, 1))[0:8]
    g[...] = gains
    gain = gains[0:1]
    moves.ready(x)

    def body(rows):
        n[rows, :] = low(centred(x[rows, :].astype(F32))[0] * gain)

    each_rows(x.shape[0], body)
    moves.done(n)
    wait_for(w, sems.at[0])
    for i, out in enumerate((q, k, v)):
        prod[...] = mm(n[...], w[:, 512 * i : 512 * (i + 1)])

        def keep(rows, out=out):
            out[rows, :] = low(prod[rows, :])

        each_rows(x.shape[0], keep)
        moves.done(out)


def front(table, x, own, other):
    rows, width = x.shape
    row16 = jax.ShapeDtypeStruct((rows, width), BF16)
    gain = jax.ShapeDtypeStruct((8, width), F32)
    return call_dense(
        front_kernel, "front", 4, [table], [x], [own, other], [row16] + [Both(row16)] * 3 + [Near(gain)], [],
        [
            pltpu.VMEM((width, 3 * width), BF16),
            pltpu.VMEM((2, BLOCKS, 16, width), BF16),
            pltpu.VMEM((rows, width), F32),
            pltpu.SemaphoreType.DMA((2,)),
        ],
    )


def mid_kernel(
    moves, a_e, a_d, x_e, x_d, g_e, g_d, dest, pack,
    m_e, n_e, act, slope, end, memory, mem_k, mem_v, m_d, n_d, query, memory_out,
    w_out, w_in, w_down, w_cross, w_query, prod, spare, total, sems,
):
    enc, dec = pack.at[0], pack.at[1]
    fetch_out(enc, w_out.at[0], sems.at[0])
    fetch_ffn(enc, w_in, w_down, sems.at[pl.ds(1, 2)])
    fetch_out(dec, w_out.at[1], sems.at[3])
    fetch_cross(enc, w_cross, sems.at[4], (0, 1))
    fetch_cross(dec, w_query, sems.at[5], (0,))
    count = x_e.shape[0]

    def attended(a, x, g, m, n, section, sem):
        moves.ready(a)
        wait_for(w_out.at[section], sem)
        prod[...] = mm(a[...], w_out[section])
        moves.ready(x)
        gain = g[1:2, :]

        def body(rows):
            middle = x[rows, :].astype(F32) + prod[rows, :]
            m[rows, :] = middle
            n[rows, :] = low(centred(middle)[0] * gain)

        each_rows(count, body)
        moves.done(m, n)

    attended(a_e, x_e, g_e, m_e, n_e, 0, sems.at[0])
    wait_for(w_in, sems.at[1])
    wait_for(w_down, sems.at[2])
    total[...] = m_e[...]
    prods = (prod, spare)
    prod[...] = mm(n_e[...], w_in[:, 0:512])
    for c in range(4):
        cols = slice(512 * c, 512 * (c + 1))
        if c < 3:
            prods[(c + 1) % 2][...] = mm(n_e[...], w_in[:, 512 * (c + 1) : 512 * (c + 2)])

        def body(rows, cols=cols, hidden=prods[c % 2]):
            value, rate = gelu_parts(hidden[rows, :])
            act[rows, cols] = low(value)
            slope[rows, cols] = low(rate)

        each_rows(count, body)
        total[...] += mm(act[:, cols], w_down[cols, :])

    moves.done(act, slope)
    gain = g_e[2:3, :]

    def body(rows):
        ending = total[rows, :]
        end[rows, :] = ending
        memory[rows, :] = low(centred(ending)[0] * gain)

    each_rows(count, body)
    moves.done(end, memory)
    wait_for(w_cross, sems.at[4])
    mem_k[...] = low(mm(memory[...], w_cross[:, 0:512]))
    mem_v[...] = low(mm(memory[...], w_cross[:, 512:1024]))
    moves.done(mem_k, mem_v)
    memory_out[...] = low(mm_tn(places_of(dest), memory[...]))
    moves.done(memory_out)
    attended(a_d, x_d, g_d, m_d, n_d, 1, sems.at[3])
    wait_for(w_query, sems.at[5])
    query[...] = low(mm(n_d[...], w_query[...]))
    moves.done(query)


def mid(a_e, a_d, x_e, x_d, g_e, g_d, dest, pack):
    rows, width = x_e.shape
    row16 = jax.ShapeDtypeStruct((rows, width), BF16)
    row32 = jax.ShapeDtypeStruct((rows, width), F32)
    wide = jax.ShapeDtypeStruct((rows, 4 * width), BF16)
    return call_dense(
        mid_kernel, "mid", 8, [], [a_e, a_d, x_e, x_d, Near(g_e), Near(g_d), Near(dest)], [pack],
        [row32, row16, wide, wide, row32, row16, Both(row16), Both(row16), row32, row16, Both(row16), row16], [],
        [
            pltpu.VMEM((2, width, width), BF16),
            pltpu.VMEM((width, 4 * width), BF16),
            pltpu.VMEM((4 * width, width), BF16),
            pltpu.VMEM((width, 2 * width), BF16),
            pltpu.VMEM((width, width), BF16),
            pltpu.VMEM((rows, width), F32),
            pltpu.VMEM((rows, width), F32),
            pltpu.VMEM((rows, width), F32),
            pltpu.SemaphoreType.DMA((6,)),
        ],
    )


def tail_kernel(
    moves, place, section, crossed, m_d, ct, g_d, dest, memory, pack,
    stay, leave, second_grad, crossed_grad, gain_grad, kept, sent,
    w_out, w_in, w_down, second, n, unit_grad, out_prod, prod, act, hidden, grad, total, stage, sems,
):
    dec = pack.at[1]
    fetch_cross(dec, w_out, sems.at[0], (1,))
    fetch_ffn(dec, w_in, w_down, sems.at[pl.ds(1, 2)])
    count = m_d.shape[0]
    wait_for(w_out, sems.at[0])
    out_prod[...] = mm(crossed[...], w_out[...])
    moves.ready(m_d)
    gain = g_d[2:3, :]

    def body(rows):
        value = m_d[rows, :] + out_prod[rows, :]
        second[rows, :] = value
        total[rows, :] = value
        n[rows, :] = low(centred(value)[0] * gain)
        unit_grad[rows, :] = jnp.zeros((STEP, value.shape[1]), F32)

    each_rows(count, body)
    wait_for(w_in, sems.at[1])
    wait_for(w_down, sems.at[2])

    moves.ready(ct)

    def products(c):
        cols = slice(512 * c, 512 * (c + 1))
        prod[c % 2] = mm(n[...], w_in[:, cols])
        hidden[c % 2] = mm_nt(ct[...], w_down[cols, :])

    products(0)
    for c in range(4):
        cols = slice(512 * c, 512 * (c + 1))
        if c < 3:
            products(c + 1)

        def body(rows, c=c):
            value, rate = gelu_parts(prod[c % 2, rows, :])
            act[c % 2, rows, :] = low(value)
            grad[c % 2, rows, :] = low(hidden[c % 2, rows, :] * rate)

        each_rows(count, body)
        total[...] += mm(act[c % 2], w_down[cols, :])
        stage_down(stage, 0, c, low(mm_tn(act[c % 2], ct[...])))
        stage_inner(stage, 64, c, low(mm_tn(n[...], grad[c % 2])))
        unit_grad[...] += mm_nt(grad[c % 2], w_in[:, cols])

    gain_grad[...] = jnp.zeros_like(gain_grad)

    def back(rows):
        act[0, rows, :] = low(total[rows, :])
        part, gained = norm_back(second[rows, :], gain, unit_grad[rows, :])
        gain_grad[...] += fold(gained)
        whole = ct[rows, :].astype(F32) + part
        second_grad[rows, :] = whole
        n[rows, :] = low(whole)

    each_rows(count, back)
    moves.done(second_grad)
    stage_rows(stage, 128, low(mm_tn(crossed[...], n[...])))
    send_stage(stage, kept, sent, place, sems.at[3])
    crossed_grad[...] = low(mm_nt(n[...], w_out[...]))
    moves.ready(memory)
    for owner in range(2):

        @pl.when(section[0] == owner)
        def _():
            out, through = (leave, stay) if owner == 0 else (stay, leave)
            out[...] = low(mm_tn(places_of(dest), act[0]))
            through[...] = memory[...]

    moves.done(stay, leave)
    wait_for(stage, sems.at[3])


def tail(place, section, crossed, m_d, ct, g_d, dest, memory, pack):
    rows, width = m_d.shape
    row16 = jax.ShapeDtypeStruct((rows, width), BF16)
    row32 = jax.ShapeDtypeStruct((rows, width), F32)
    return call_dense(
        tail_kernel, "tail", 15, [place, section], [Near(crossed), m_d, ct, Near(g_d), Near(dest), memory], [pack],
        [row16, row16, row32, Near(row16), Near(jax.ShapeDtypeStruct((8, width), F32))], pack_pair(144, width),
        [
            pltpu.VMEM((width, width), BF16),
            pltpu.VMEM((width, 4 * width), BF16),
            pltpu.VMEM((4 * width, width), BF16),
            pltpu.VMEM((rows, width), F32),
            pltpu.VMEM((rows, width), BF16),
            pltpu.VMEM((rows, width), F32),
            pltpu.VMEM((rows, width), F32),
            pltpu.VMEM((2, rows, width), F32),
            pltpu.VMEM((2, rows, width), BF16),
            pltpu.VMEM((2, rows, width), F32),
            pltpu.VMEM((2, rows, width), BF16),
            pltpu.VMEM((rows, width), F32),
            pltpu.VMEM((2, BLOCKS, 144, width), BF16),
            pltpu.SemaphoreType.DMA((4,)),
        ],
    )


def mid_back_kernel(
    moves, place, dq, dk, dv, n_d, m_d, second_grad, a_d, memory, end, act, slope, n_e, m_e, a_e, g_e, g_d, pack,
    md_grad, ad_grad, me_grad, ae_grad, ge_grad, kept, sent,
    w_out, w_in, w_down, w_cross, w_query, prod, hidden, grad, total, small, stage, sems,
):
    enc, dec = pack.at[0], pack.at[1]
    fetch_cross(dec, w_query, sems.at[5], (0,))
    fetch_out(dec, w_out.at[1], sems.at[3])
    fetch_cross(enc, w_cross, sems.at[4], (0, 1))
    fetch_ffn(enc, w_in, w_down, sems.at[pl.ds(1, 2)])
    fetch_out(enc, w_out.at[0], sems.at[0])
    count = m_d.shape[0]
    ge_grad[...] = jnp.zeros_like(ge_grad)

    def through_out(a, grad, result, section, offset):
        stage_rows(stage, offset, low(mm_tn(a[...], small[...])))
        result[...] = low(mm_nt(small[...], w_out[section]))

    moves.ready(n_d)
    stage_rows(stage, 176, low(mm_tn(n_d[...], dq[...])))
    wait_for(w_query, sems.at[5])
    prod[...] = mm_nt(dq[...], w_query[...])
    moves.ready(m_d, second_grad)
    gain_d = g_d[1:2, :]

    def decoder(rows):
        part, _ = norm_back(m_d[rows, :], gain_d, prod[rows, :])
        whole = second_grad[rows, :] + part
        md_grad[rows, :] = whole
        small[rows, :] = low(whole)

    each_rows(count, decoder)
    moves.done(md_grad)
    moves.ready(a_d)
    wait_for(w_out.at[1], sems.at[3])
    through_out(a_d, md_grad, ad_grad, 1, 192)

    moves.ready(memory)
    stage_rows(stage, 0, low(mm_tn(memory[...], dk[...])))
    stage_rows(stage, 16, low(mm_tn(memory[...], dv[...])))
    wait_for(w_cross, sems.at[4])
    prod[...] = mm_nt(dk[...], w_cross[:, 0:512])
    prod[...] += mm_nt(dv[...], w_cross[:, 512:1024])
    moves.ready(end)
    gain_two = g_e[2:3, :]

    def ending(rows):
        part, _ = norm_back(end[rows, :], gain_two, prod[rows, :])
        me_grad[rows, :] = part
        small[rows, :] = low(part)
        total[rows, :] = jnp.zeros_like(part)

    each_rows(count, ending)
    wait_for(w_in, sems.at[1])
    wait_for(w_down, sems.at[2])

    hidden[0] = mm_nt(small[...], w_down[0:512, :])
    moves.ready(slope, act, n_e)
    for c in range(4):
        cols = slice(512 * c, 512 * (c + 1))
        if c < 3:
            hidden[(c + 1) % 2] = mm_nt(small[...], w_down[512 * (c + 1) : 512 * (c + 2), :])

        def body(rows, c=c, cols=cols):
            grad[c % 2, rows, :] = low(hidden[c % 2, rows, :] * slope[rows, cols].astype(F32))

        each_rows(count, body)
        stage_down(stage, 32, c, low(mm_tn(act[:, cols], small[...])))
        stage_inner(stage, 96, c, low(mm_tn(n_e[...], grad[c % 2])))
        total[...] += mm_nt(grad[c % 2], w_in[:, cols])

    moves.ready(m_e)
    gain_one = g_e[1:2, :]

    def encoder(rows):
        part, gained = norm_back(m_e[rows, :], gain_one, total[rows, :])
        ge_grad[...] += fold(gained)
        whole = me_grad[rows, :] + part
        me_grad[rows, :] = whole
        small[rows, :] = low(whole)

    each_rows(count, encoder)
    moves.done(me_grad)
    moves.ready(a_e)
    wait_for(w_out.at[0], sems.at[0])
    through_out(a_e, me_grad, ae_grad, 0, 160)
    send_stage(stage, kept, sent, place, sems.at[6])
    wait_for(stage, sems.at[6])


def mid_back(place, dq, dk, dv, n_d, m_d, second_grad, a_d, memory, end, act, slope, n_e, m_e, a_e, g_e, g_d, pack):
    rows, width = m_d.shape
    row16 = jax.ShapeDtypeStruct((rows, width), BF16)
    row32 = jax.ShapeDtypeStruct((rows, width), F32)
    return call_dense(
        mid_back_kernel, "mid_back", 19, [place],
        [Near(dq), Near(dk), Near(dv), n_d, m_d, second_grad, a_d, memory, end, act, slope, n_e, m_e, a_e, Near(g_e), Near(g_d)],
        [pack], [row32, Near(row16), row32, Near(row16), Near(jax.ShapeDtypeStruct((8, width), F32))],
        pack_pair(208, width),
        [
            pltpu.VMEM((2, width, width), BF16),
            pltpu.VMEM((width, 4 * width), BF16),
            pltpu.VMEM((4 * width, width), BF16),
            pltpu.VMEM((width, 2 * width), BF16),
            pltpu.VMEM((width, width), BF16),
            pltpu.VMEM((rows, width), F32),
            pltpu.VMEM((2, rows, width), F32),
            pltpu.VMEM((2, rows, width), BF16),
            pltpu.VMEM((rows, width), F32),
            pltpu.VMEM((rows, width), BF16),
            pltpu.VMEM((2, BLOCKS, 208, width), BF16),
            pltpu.SemaphoreType.DMA((7,)),
        ],
    )


def front_w_kernel(moves, place, qe, ke, ve, qd, kd, vd, n_e, n_d, ge_one, gd_two, ds_e, ds_d, ds_c, kept, sent, stage, sems):
    width = n_e.shape[1]
    for section, (grads, n) in enumerate((((qe, ke, ve), n_e), ((qd, kd, vd), n_d))):
        moves.ready(n)
        for i in range(3):
            grad = low(mm_tn(n[...], grads[i][...]))
            for j in range(BLOCKS):
                stage[section, j, 32 * i : 32 * i + 32, :] = grad[32 * j : 32 * j + 32, :]
    lane = lax.broadcasted_iota(jnp.int32, (8, width), 1)
    heads = jnp.zeros((8, width), F32)
    for i, ds in enumerate((ds_e, ds_d, ds_c)):
        heads = jnp.where(lane == i, jnp.sum(ds[...], axis=1, keepdims=True), heads)
    lines = [jnp.sum(g[...], axis=0, keepdims=True) for g in (ge_one, gd_two)]
    extra = low(jnp.concatenate(lines + [jnp.zeros((6, width), F32), heads], axis=0))
    for h in range(2):
        for j in range(BLOCKS):
            stage[h, j, 96:112, :] = extra
    send_stage(stage, kept, sent, place, sems.at[0])
    wait_for(stage, sems.at[0])


def front_w(place, grads_e, grads_d, n_e, n_d, ge_one, gd_two, ds):
    width = n_e.shape[1]
    near = [Near(g) for g in (*grads_e, *grads_d)]
    return call_dense(
        front_w_kernel, "front_w", 5, [place], [*near, n_e, n_d, *map(Near, (ge_one, gd_two, *ds))], [],
        [], pack_pair(112, width),
        [pltpu.VMEM((2, BLOCKS, 112, width), BF16), pltpu.SemaphoreType.DMA((1,))],
    )


def front_x_kernel(moves, table, dq, dk, dv, x, m_grad, g, dest, own, other, x_grad, w, prod, high, rest, sems):
    fetch_front(table, own, other, w, sems.at[0])
    wait_for(w, sems.at[0])
    prod[...] = mm_nt(dq[...], w[:, 0:512])
    prod[...] += mm_nt(dk[...], w[:, 512:1024])
    prod[...] += mm_nt(dv[...], w[:, 1024:1536])
    moves.ready(x, m_grad)
    gain = g[0:1, :]

    def body(rows):
        part, _ = norm_back(x[rows, :].astype(F32), gain, prod[rows, :])
        whole = m_grad[rows, :] + part
        high[rows, :] = low(whole)
        rest[rows, :] = low(whole - high[rows, :].astype(F32))

    each_rows(x.shape[0], body)
    place = places_of(dest)
    x_grad[...] = mm_tn(place, high[...])
    x_grad[...] += mm_tn(place, rest[...])
    moves.done(x_grad)


def front_x(table, grads, x, m_grad, g, dest, own, other):
    rows, width = x.shape
    return call_dense(
        front_x_kernel, "front_x", 4, [table], [*map(Near, grads), x, m_grad, Near(g), Near(dest)], [own, other],
        [jax.ShapeDtypeStruct((rows, width), F32)], [],
        [
            pltpu.VMEM((width, 3 * width), BF16),
            pltpu.VMEM((rows, width), F32),
            pltpu.VMEM((rows, width), BF16),
            pltpu.VMEM((rows, width), BF16),
            pltpu.SemaphoreType.DMA((1,)),
        ],
    )[0]


def exact(a, b, dims):
    return lax.dot_general(a, b, (dims, ((), ())), precision=lax.Precision.HIGHEST, preferred_element_type=F32)


def finish_kernel(
    place, own, came, last, w_qkv, w_cross, gains, slope, qkv, out, cross, inner, down, gain, alpha
):
    columns = gains.shape[1]
    extra = last[96:112, :]
    for i in range(3):
        qkv[:, 512 * i : 512 * (i + 1)] = last[32 * i : 32 * i + 32, :]

    def halves_to(offsets):
        at_out, at_cross, at_inner, at_down = offsets
        for h in range(2):
            for section, src in ((h, own), (1 - h, came)):

                @pl.when(place[1] == section)
                def _():
                    few = slice(16 * h, 16 * h + 16)
                    out[few, :] = src[at_out : at_out + 16, :].astype(F32)
                    for i in range(2):
                        at = at_cross[i]
                        cross[few, 512 * i : 512 * (i + 1)] = src[at : at + 16, :].astype(F32)
                    for i in range(4):
                        rows = slice(256 * h + 64 * i, 256 * h + 64 * (i + 1))
                        inner[rows, :] = src[at_inner : at_inner + 64, 128 * i : 128 * (i + 1)].astype(F32)
                    down[64 * h : 64 * h + 64, :] = src[at_down : at_down + 64, :].astype(F32)

    spot = lax.broadcasted_iota(jnp.int32, (extra.shape[1], columns), 0) - place[0] * columns
    pick = jnp.where(spot == lax.broadcasted_iota(jnp.int32, (extra.shape[1], columns), 1), 1.0, 0.0)
    split = exact(extra[0:8], pick, ((1,), (0,)))

    def reach(weight, grad):
        weighted = weight.astype(F32) * grad
        return exact(jnp.ones((8, weighted.shape[1]), F32), weighted, ((1,), (1,)))[0:1]

    @pl.when(place[1] == 0)
    def _():
        halves_to((160, (0, 16), 96, 32))
        gain[0:1, :] = reach(w_qkv[...], qkv[...]) / gains[0:1, :].astype(F32)
        gain[1:2, :] = split[0:1]
        gain[2:3, :] = reach(w_cross[...], cross[...]) / gains[2:3, :].astype(F32)

    @pl.when(place[1] == 1)
    def _():
        halves_to((160, (144, 128), 64, 0))
        gain[0:1, :] = reach(w_qkv[...], qkv[...]) / gains[0:1, :].astype(F32)
        gain[1:2, :] = reach(w_cross[:, 0:512], cross[:, 0:512]) / gains[1:2, :].astype(F32)
        gain[2:3, :] = split[1:2]

    alpha[...] = extra[8:16, 0:128].T[0:3, :] * slope[...]


def finish(place, own, came, last, w_qkv, w_cross, gains, slope):
    shapes = [(32, 1536), (32, 512), (32, 1024), (512, 128), (128, 512), (3, 32), (3, 8)]
    return pl.pallas_call(
        finish_kernel,
        in_specs=[TABLE] + [WHOLE] * 7,
        out_specs=[WHOLE] * 7,
        out_shape=[jax.ShapeDtypeStruct(shape, F32) for shape in shapes],
        name="finish",
    )(place, own, came, last, w_qkv, w_cross, gains, slope)


ORDER = ((4, 8, 1, 2), (4, 8, 2, 1))
SHIFT = np.array(
    [[functools.reduce(lambda a, b: a ^ b, [m for b, m in enumerate(order) if p >> b & 1], 0) for p in range(BLOCKS)] for order in ORDER],
    np.int32,
)
WHERE = np.argsort(SHIFT, axis=1).astype(np.int32)
SWAP = [(0, 1), (1, 0)]


def swap(value):
    return lax.ppermute(value, "section", SWAP)


def hop(value, bit):
    pairs = [
        (BLOCKS * s + i, BLOCKS * s + (i ^ ORDER[s][bit])) for s in range(2) for i in range(BLOCKS)
    ]
    return lax.ppermute(value, ("section", "dp"), pairs)


def jump(value, position):
    pairs = [
        (BLOCKS * s + i, BLOCKS * s + (i ^ int(SHIFT[s, position]))) for s in range(2) for i in range(BLOCKS)
    ]
    return lax.ppermute(value, ("section", "dp"), pairs)


def tie(value, held):
    return lax.optimization_barrier((value, held))


def behind(out, *packs):
    kept = [pack[0] for pack in packs]
    out, kept = lax.optimization_barrier((out, kept))
    for pack, value in zip(packs, kept):
        pack[0] = value
    return out


def total(terms, first, last):
    return low(sum(term[first:last].astype(F32) for term in terms))


def over_plane(blocks):
    planes = [[4 * z + i for i in range(4)] for z in range(4)]
    return lax.psum_scatter(blocks, "dp", scatter_dimension=0, axis_index_groups=planes, tiled=True)


def to_line(terms):
    return [total(terms, i, i + 1)[0] for i in (1, 2, 3)]


def along_line(sent):
    return [jump(block, i + 1) for i, block in enumerate(sent)]


def at_last(terms, came):
    return sum([term[0].astype(F32) for term in terms] + [block.astype(F32) for block in came])


def inner_of(halves):
    quarter, width = halves[0].shape
    rows = [h.reshape(quarter, 4, width // 4).transpose(1, 0, 2).reshape(4 * quarter, width // 4) for h in halves]
    return jnp.concatenate(rows, axis=0)


def spread_line(block):
    return jnp.stack([block] + [jump(block, i) for i in (1, 2, 3)])


def spread_plane(blocks, bit):
    return jnp.concatenate([blocks, hop(blocks, bit)], axis=0)


def weights_near(attn_qkv, attn_out, cross_proj, ffn_in, ffn_out, gains):
    me, section = lax.axis_index("dp"), lax.axis_index("section")
    gain_rows = jnp.pad(gains[0], ((0, 16 - gains.shape[1]), (0, 0)))
    kept, sent, second = pack_shards(
        jnp.stack([me, section]), attn_qkv[0], attn_out[0], cross_proj[0], ffn_in[0], ffn_out[0], gain_rows
    )
    came = swap(sent)
    enc, dec = jnp.where(section == 0, kept, came), jnp.where(section == 0, came, kept)
    enc = spread_line(enc)
    dec, enc = tie(dec, enc)
    enc, dec = tie(spread_plane(enc, 2), spread_line(dec))
    enc, dec = tie(spread_plane(enc, 3), spread_plane(dec, 2))
    enc = (enc, swap(enc))
    dec = spread_plane(dec, 3)
    pack = lax.all_gather(second, ("section", "dp"), axis=0, tiled=False)
    shift = jnp.asarray(SHIFT)
    table = jnp.stack([shift[section] ^ me, shift[1 - section] ^ me, jnp.full((BLOCKS,), section, jnp.int32)])
    where = jnp.asarray(WHERE)[:, jnp.arange(BLOCKS, dtype=jnp.int32) ^ me]
    halves = jnp.where(jnp.arange(BLOCKS) == section, 0, 1).astype(jnp.int32)
    number = jnp.arange(BLOCKS, dtype=jnp.int32)
    flat = jnp.broadcast_to(4 * (number & 3) + ((number ^ me) >> 2), (2, BLOCKS))
    return enc, dec, pack.reshape((2, BLOCKS) + second.shape), table, jnp.concatenate([where, halves[None]]), jnp.concatenate([flat, halves[None]]), gain_rows


def weights_far(attn_qkv, attn_out, cross_proj, ffn_in, ffn_out, gains):
    def whole(shard, axis):
        return lax.all_gather(shard[0], "dp", axis=axis, tiled=True)

    qkv, out, cross, inner, down, gain = (
        whole(w, a) for w, a in ((attn_qkv, 0), (attn_out, 0), (cross_proj, 0), (ffn_in, 1), (ffn_out, 0), (gains, 1))
    )
    width = out.shape[1]
    gain_rows = jnp.zeros((BLOCKS, 16, width), BF16).at[0, : gain.shape[0]].set(gain)
    first = jnp.stack(jax.vmap(pack_first)(qkv.reshape(BLOCKS, -1, 3 * width), gain_rows))
    second = jax.vmap(pack_second)(
        out.reshape(BLOCKS, -1, width),
        cross.reshape(BLOCKS, -1, 2 * width),
        down.reshape(BLOCKS, -1, width),
        inner.reshape(width, BLOCKS, -1).transpose(1, 0, 2),
    )
    section = lax.axis_index("section")
    first_other, second_other = swap(first), swap(second)

    def both(mine, came):
        return jnp.where(section == 0, mine, came), jnp.where(section == 0, came, mine)

    enc, dec = both(first, first_other)
    pack = jnp.stack(both(second, second_other))
    plain = jnp.arange(BLOCKS, dtype=jnp.int32)
    table = jnp.stack([plain, plain, jnp.zeros_like(plain)])
    halves = jnp.where(plain == 0, 0, 1).astype(jnp.int32)
    return (enc[0], enc[1]), (dec[0], dec[1]), pack, table, jnp.stack([plain, plain, halves]), jnp.stack([plain, plain, halves]), None


def far_shards(tail_pack, mid_pack, front_pack):
    tail_pack, mid_pack, front_pack = (jnp.stack(p) for p in (tail_pack, mid_pack, front_pack))

    def qkv_of(pack):
        return jnp.concatenate([pack[:, 32 * i : 32 * i + 32].reshape(-1, pack.shape[2]) for i in range(3)], axis=1)
    def rows(pack, start, count):
        part = pack[:, :, start : start + count]
        return part.transpose(1, 0, 2, 3).reshape(-1, part.shape[-1])

    def inner(pack, start):
        blocks = jax.vmap(lambda a, b: inner_of([a, b]))(pack[0, :, start : start + 64], pack[1, :, start : start + 64])
        return blocks.transpose(1, 0, 2).reshape(blocks.shape[1], -1)

    def side(pack, *starts):
        return jnp.concatenate([rows(pack, s, 16) for s in starts], axis=1)

    enc = (qkv_of(front_pack[0]), rows(mid_pack, 160, 16), side(mid_pack, 0, 16), inner(mid_pack, 96), rows(mid_pack, 32, 64))
    cross_d = jnp.concatenate([rows(mid_pack, 176, 16), rows(tail_pack, 128, 16)], axis=1)
    dec = (qkv_of(front_pack[1]), rows(mid_pack, 192, 16), cross_d, inner(tail_pack, 64), rows(tail_pack, 0, 64))
    section = lax.axis_index("section")
    grads = []
    for a, b, axis in zip(enc, dec, (0, 0, 0, 1, 0)):
        mine = jnp.where(section == 0, a, b).astype(F32) + swap(jnp.where(section == 0, b, a)).astype(F32)
        grads.append(lax.psum_scatter(mine, "dp", scatter_dimension=axis, tiled=True))
    extra = lax.psum(front_pack[0, 0, 96:112].astype(F32), ("section", "dp"))
    return tuple(grads), extra


def gain_grads(weights, grads, gains, extra):
    section = lax.axis_index("section")
    qkv, cross = (w[0].astype(F32) * g for w, g in zip(weights, grads))
    gain = gains[0].astype(F32)
    columns = gain.shape[1]
    start = lax.axis_index("dp") * columns
    split = lax.dynamic_slice(extra, (section, start), (1, columns))[0]
    half = cross.shape[1] // 2
    reach = jnp.sum(cross[:, :half], axis=1)
    memory = (reach + jnp.sum(cross[:, half:], axis=1)) / gain[2]
    first = jnp.sum(qkv, axis=1) / gain[0]
    enc, dec = jnp.stack([first, split, memory]), jnp.stack([first, reach / gain[1], split])
    return jnp.where(section == 0, enc, dec)


def new_places(lengths, starts, rows):
    ends = jnp.cumsum(lengths)
    places = jnp.arange(rows, dtype=jnp.int32)
    pick = (places[:, None] >= (ends - lengths)[None, :]) & (places[:, None] < ends[None, :])
    return (places + jnp.sum(jnp.where(pick, (starts - ends + lengths)[None, :], 0), axis=1))[None]


def local(
    layer_input, cotangent, lengths, attn_qkv, attn_out, cross_proj, ffn_in, ffn_out, gains, alpha_raw
):
    section = lax.axis_index("section")
    near = lax.axis_size("dp") == BLOCKS
    weights = weights_near if near else weights_far
    first_e, first_d, pack, table, place, place_b, gain_rows = weights(attn_qkv, attn_out, cross_proj, ffn_in, ffn_out, gains)
    rows, width = layer_input.shape[3:]
    inputs = layer_input[0, :, 0]
    came = swap(lax.dynamic_index_in_dim(inputs, 1 - section, 0, keepdims=False))
    first = section == 0
    source, target = lax.dynamic_index_in_dim(lengths[:, :, 0], section, 1, keepdims=False)
    large_e, large_d = source == jnp.max(source), target == jnp.max(target)
    starts_e = starts_of(source, jnp.where(large_e, 0, jnp.where(large_d, 2, 1)))
    starts_d = starts_of(target, jnp.where(large_d, 0, jnp.where(large_e, 1, 2)))
    dest_e, dest_d = new_places(source, starts_e, rows), new_places(target, starts_d, rows)
    x_e, x_d, ct = sort_rows(section[None], inputs, came, cotangent[:, 0], dest_e, dest_d)
    head_width = width // alpha_raw.shape[1]
    gate = jax.nn.sigmoid(alpha_raw)
    coef = [coefs_of(0.25 + 0.25 * gate[i], head_width) for i in range(3)]
    marks_e = marks_of(starts_e, source, starts_e, source, rows, False)
    marks_d = marks_of(starts_d, target, starts_d, target, rows, True)
    marks_c = marks_of(starts_d, target, starts_e, source, rows, False)

    def by_micro(kept, came):
        return jnp.stack([jnp.where(first, kept, came), jnp.where(first, came, kept)])[None, :, None]

    def settle(enc, dec):
        return by_micro(jnp.where(first, enc, dec), swap(jnp.where(first, dec, enc)))

    n_e, (q_now, q_e), (k_now, k_e), (v_now, v_e), g_e = front(table, x_e, *first_e)
    if near:
        q_now, first_d = tie(q_now, first_d)
        first_d = (first_d, swap(first_d))
    a_e, *stats_e = attend(q_now, k_now, v_now, marks_e, coef[0])
    n_d, (q_now, q_d), (k_now, k_d), (v_now, v_d), g_d = front(table, x_d, *first_d)
    a_d, *stats_d = attend(q_now, k_now, v_now, marks_d, coef[1])
    m_e, n1_e, act, slope, end, memory, (mk_now, mem_k), (mv_now, mem_v), m_d, n1_d, (query_now, query), memory_out = mid(
        a_e, a_d, x_e, x_d, g_e, g_d, dest_e, pack
    )
    crossed, *stats_c = attend(query_now, mk_now, mv_now, marks_c, coef[2])
    stay, leave, second_grad, crossed_grad, gd_two, kept, sent = tail(
        place, section[None], crossed, m_d, ct, g_d, dest_d, memory_out, pack
    )
    pack_a = (kept, sent)
    if near:
        a = [kept, swap(sent)]
    arrived = swap(leave)
    query_grad, mk_grad, mv_grad, ds_c = attend_back(query, mem_k, mem_v, crossed_grad, stats_c, marks_c, coef[2])
    if near:
        query_grad = behind(query_grad, a)
        query_grad, (sent_a, arrived) = tie(query_grad, (total(a, 8, 16), arrived))
        a.append(hop(sent_a, 3))
    md_grad, ad_grad, me_grad, ae_grad, ge_one, kept, sent = mid_back(
        place, query_grad, mk_grad, mv_grad, n1_d, m_d, second_grad, a_d, memory, end, act, slope, n1_e, m_e, a_e, g_e, g_d, pack
    )
    pack_b = (kept, sent)
    if near:
        ad_grad = behind(ad_grad, a)
        (ad_grad, sent), sent_a = tie((ad_grad, sent), total(a, 4, 8))
        a.append(hop(sent_a, 2))
        b = [kept, swap(sent)]
    *grads_d, ds_d = attend_back(q_d, k_d, v_d, ad_grad, stats_d, marks_d, coef[1])
    if near:
        grads_d[0] = behind(grads_d[0], a, b)
        ae_grad, (sent_a, sent_b, grads_d[0]) = tie(ae_grad, (to_line(a), total(b, 8, 16), grads_d[0]))
        b.append(hop(sent_b, 3))
        came_a = along_line(sent_a)
    *grads_e, ds_e = attend_back(q_e, k_e, v_e, ae_grad, stats_e, marks_e, coef[0])
    if near:
        grads_e[0] = behind(grads_e[0], a, b)
        (grads_e[0], md_grad), (sent_b, done_a) = tie((grads_e[0], md_grad), (total(b, 4, 8), at_last(a, came_a)))
        b.append(hop(sent_b, 2))
    kept, sent = front_w(place, grads_e, grads_d, n_e, n_d, ge_one, gd_two, (ds_e, ds_d, ds_c))
    if near:
        sent = behind(sent, b)
        (sent, md_grad), sent_b = tie((sent, md_grad), to_line(b))
        c = [kept, swap(sent)]
        came_b = along_line(sent_b)
    xd_grad = front_x(table, grads_d, x_d, md_grad, g_d, dest_d, *first_d)
    if near:
        xd_grad = behind(xd_grad, c)
        (me_grad, xd_grad), sent_c = tie((me_grad, xd_grad), total(c, 8, 16))
        c.append(hop(sent_c, 3))
    xe_grad = front_x(table, grads_e, x_e, me_grad, g_e, dest_e, *first_e)
    if near:
        outputs = by_micro(stay, arrived)
        xe_grad, outputs = behind((xe_grad, outputs), b, c)
        sent_c, (xe_grad, done_b) = tie(total(c, 4, 8), (xe_grad, at_last(b, came_b)))
        c.append(hop(sent_c, 2))
        input_grad = settle(xe_grad, xd_grad)
        enc, dec = low(done_b[0:176]), low(jnp.concatenate([done_a, done_b[176:208]], axis=0))
        parts = (jnp.where(first, enc, dec), swap(jnp.where(first, dec, enc)))
        (parts, input_grad) = behind((parts, input_grad), c)
        *grads, alpha_grad = finish(
            jnp.stack([lax.axis_index("dp"), section]), *parts, at_last(c, along_line(to_line(c))),
            attn_qkv[0], cross_proj[0], gain_rows, 0.25 * gate * (1.0 - gate),
        )
    else:
        input_grad, outputs = settle(xe_grad, xd_grad), by_micro(stay, arrived)
        grads, extra = far_shards(pack_a, pack_b, (kept, sent))
        grads += (gain_grads((attn_qkv, cross_proj), (grads[0], grads[2]), gains, extra),)
        alpha_grad = extra[8:16, 0:3].T * 0.25 * gate * (1.0 - gate)
    return (outputs, input_grad) + tuple(g[None] for g in grads) + (alpha_grad,)


def solution(mesh):
    return jax.shard_map(
        local,
        mesh=mesh,
        in_specs=(
            P("section", None, "dp", None, None),
            P(None, "dp", None, None),
            P(None, None, "dp", None),
            P("section", "dp", None),
            P("section", "dp", None),
            P("section", "dp", None),
            P("section", None, "dp"),
            P("section", "dp", None),
            P("section", None, "dp"),
            P(),
        ),
        out_specs=(
            P("section", None, "dp", None, None),
            P("section", None, "dp", None, None),
            P("section", "dp", None),
            P("section", "dp", None),
            P("section", "dp", None),
            P("section", None, "dp"),
            P("section", "dp", None),
            P("section", None, "dp"),
            P(),
        ),
        check_vma=False,
    )
```

```python
import functools
import math

import jax
import jax.numpy as jnp
import numpy as np
from jax import lax
from jax.experimental import pallas as pl
from jax.experimental.pallas import tpu as pltpu
from jax.sharding import PartitionSpec as P

SHARP = 0.0625
NEG = -1e9
EPS = 1e-5
TINY = 1e-37
LOG2E = 1.4426950408889634
PART = 256
CHUNK = 128
TILE = 128
BLOCKS = 16
MB = 1 << 20
COST = 1000
LIMIT = 52 * MB
F32, BF16 = jnp.float32, jnp.bfloat16
WHOLE = pl.BlockSpec(memory_space=pltpu.VMEM)
TABLE = pl.BlockSpec(memory_space=pltpu.SMEM)
AWAY = pl.BlockSpec(memory_space=pl.ANY)


def mm(a, b):
    return jnp.dot(a, b, preferred_element_type=F32)


def mm_nt(a, b):
    return lax.dot_general(a, b, (((1,), (1,)), ((), ())), preferred_element_type=F32)


def mm_tn(a, b):
    return lax.dot_general(a, b, (((0,), (0,)), ((), ())), preferred_element_type=F32)


def low(v):
    return v.astype(BF16)


class Moves:
    def __init__(self, pairs_in, pairs_out, sems):
        self.copies = {}
        for i, (src, dst) in enumerate(pairs_in):
            self.copies[id(dst)] = pltpu.make_async_copy(src, dst, sems.at[i])
            self.copies[id(dst)].start()
        self.outs = {
            id(src): pltpu.make_async_copy(src, dst, sems.at[len(pairs_in) + i])
            for i, (src, dst) in enumerate(pairs_out)
        }
        self.left = []

    def ready(self, *refs):
        for ref in refs:
            copy = self.copies.pop(id(ref), None)
            if copy is not None:
                copy.wait()

    def done(self, *refs):
        for ref in refs:
            copy = self.outs.pop(id(ref), None)
            if copy is not None:
                copy.start()
                self.left.append(copy)

    def finish(self):
        assert not self.copies and not self.outs
        for copy in self.left:
            copy.wait()


class Near:
    def __init__(self, array):
        self.array = array


class Both(Near):
    pass


def call_dense(body, name, us, tables, ins, far, outs, far_outs, scratch):
    near_in = [isinstance(a, Near) for a in ins]
    near_out = [isinstance(a, Near) for a in outs]
    away_out = [not isinstance(a, Near) or isinstance(a, Both) for a in outs]
    ins = [a.array if isinstance(a, Near) else a for a in ins]
    outs = [a.array if isinstance(a, Near) else a for a in outs]
    bufs_in = [a for a, near in zip(ins, near_in) if not near]
    bufs_out = [a for a, near in zip(outs, near_out) if not near]
    lone = [a for a, near in zip(outs, near_out) if near]
    sent = [a for a, away in zip(outs, away_out) if away]
    counts = [len(g) for g in (tables, ins, far, lone, sent, far_outs, bufs_in, bufs_out)]

    def kernel(*refs):
        groups, at = [], 0
        for count in counts:
            groups.append(list(refs[at : at + count]))
            at += count
        table_refs, in_refs, far_refs, lone_refs, sent_refs, far_out_refs, in_bufs, out_bufs = groups
        in_local = [ref if near else in_bufs.pop(0) for ref, near in zip(in_refs, near_in)]
        out_local = [lone_refs.pop(0) if near else out_bufs.pop(0) for near in near_out]
        pairs_in = [(ref, buf) for ref, buf, near in zip(in_refs, in_local, near_in) if not near]
        pairs_out = [(buf, sent_refs.pop(0)) for buf, away in zip(out_local, away_out) if away]
        moves = Moves(pairs_in, pairs_out, refs[at])
        body(moves, *table_refs, *in_local, *far_refs, *out_local, *far_out_refs, *refs[at + 1 :])
        moves.finish()

    got = pl.pallas_call(
        kernel,
        in_specs=[TABLE] * len(tables) + [WHOLE if near else AWAY for near in near_in] + [AWAY] * len(far),
        out_specs=[WHOLE] * len(lone) + [AWAY] * (len(sent) + len(far_outs)),
        out_shape=[*lone, *sent, *far_outs],
        scratch_shapes=[pltpu.VMEM(a.shape, a.dtype) for a in (*bufs_in, *bufs_out)]
        + [pltpu.SemaphoreType.DMA((max(1, len(bufs_in) + len(sent)),)), *scratch],
        compiler_params=pltpu.CompilerParams(vmem_limit_bytes=LIMIT),
        cost_estimate=pl.CostEstimate(flops=us * COST, transcendentals=0, bytes_accessed=us * COST // 400),
        name=name,
    )(*tables, *ins, *far)
    lone_got, sent_got = list(got[: len(lone)]), list(got[len(lone) : len(lone) + len(sent)])
    result = []
    for near, away in zip(near_out, away_out):
        pair = (lone_got.pop(0) if near else None, sent_got.pop(0) if away else None)
        result.append(pair if near and away else pair[0] if near else pair[1])
    return result + list(got[len(lone) + len(sent) :])


def fold(block):
    return jnp.sum(block.reshape(block.shape[0] // 8, 8, block.shape[1]), axis=0)


def fold_max(block):
    return jnp.max(block.reshape(block.shape[0] // 8, 8, block.shape[1]), axis=0)


def rows_of(parts, op):
    return jnp.concatenate([op(part, axis=0, keepdims=True) for part in parts], axis=0)


def per_head(coef, which, heads):
    place = lax.broadcasted_iota(jnp.int32, (heads, TILE), 0)
    out = jnp.zeros((heads, TILE), F32)
    for h in range(heads):
        out = jnp.where(place == h, coef[which, h], out)
    return out


def bias_of(lo, hi, start):
    place = lax.broadcasted_iota(jnp.int32, (CHUNK, TILE), 0) + start
    return jnp.where(jnp.logical_and(place >= lo, place < hi), 0.0, NEG)


def pair_of(h, width):
    return slice(h // 2 * 2 * width, (h // 2 + 1) * 2 * width)


def split_pairs(dst, turned, heads, width):
    for h in range(heads):
        block = turned[pair_of(h, width), :]
        mine = lax.broadcasted_iota(jnp.int32, block.shape, 0) // width == h % 2
        dst[h] = jnp.where(mine, block, jnp.zeros_like(block))


def fold(block):
    return jnp.sum(block.reshape(block.shape[0] // 8, 8, block.shape[1]), axis=0)


def fold_max(block):
    return jnp.max(block.reshape(block.shape[0] // 8, 8, block.shape[1]), axis=0)


def rows_of(parts, op):
    return jnp.concatenate([op(part, axis=0, keepdims=True) for part in parts], axis=0)


def per_head(coef, which, heads):
    place = lax.broadcasted_iota(jnp.int32, (heads, TILE), 0)
    out = jnp.zeros((heads, TILE), F32)
    for h in range(heads):
        out = jnp.where(place == h, coef[which, h], out)
    return out


def bias_of(lo, hi, start):
    place = lax.broadcasted_iota(jnp.int32, (CHUNK, TILE), 0) + start
    return jnp.where(jnp.logical_and(place >= lo, place < hi), 0.0, NEG)


def pair_of(h, width):
    return slice(h // 2 * 2 * width, (h // 2 + 1) * 2 * width)


def chunk_at(c):
    return pl.ds(pl.multiple_of(c * CHUNK, CHUNK), CHUNK)


def split_pairs(dst, turned, heads, width):
    for h in range(heads):
        block = turned[pair_of(h, width), :]
        mine = lax.broadcasted_iota(jnp.int32, block.shape, 0) // width == h % 2
        dst[h] = jnp.where(mine, block, jnp.zeros_like(block))


def clear_outside(first, last, keys, refs, cols):
    def blank(c, carry):
        for ref in refs:
            for h in range(ref.shape[0]):
                ref[h, chunk_at(c), cols] = jnp.zeros((CHUNK, TILE), BF16)
        return carry

    lax.fori_loop(0, first, blank, 0)
    lax.fori_loop(last, keys // CHUNK, blank, 0)


def meets(first, last, half):
    per = PART // CHUNK
    return jnp.logical_and(first < (half + 1) * per, last > half * per)


def attend_kernel(
    span, coef, lo_ref, hi_ref, q_ref, k_ref, v_ref, o_ref, tau_ref, top_ref, inv_ref, v_t, zs, ps, qz, o_t
):
    heads, keys = zs.shape[0], zs.shape[1]
    width = q_ref.shape[1] // heads
    tile = pl.program_id(0)

    @pl.when(tile == 0)
    def _():
        v_t[...] = v_ref[...].T

    split_pairs(qz, q_ref[...].T, heads, width)
    lo, hi = lo_ref[...], hi_ref[...]
    first, last = span[0, tile], span[1, tile]

    def scores(c, tops):
        here = chunk_at(c)
        bias = bias_of(lo, hi, c * CHUNK)
        out = []
        for h in range(heads):
            z = mm(k_ref[here, pair_of(h, width)], qz[h]) * coef[0, h] + bias
            zs[h, here, :] = z
            out.append(jnp.maximum(tops[h], fold_max(z)))
        return tuple(out)

    tops = lax.fori_loop(
        first, last, scores, tuple(jnp.full((8, TILE), -3e38, F32) for _ in range(heads))
    )
    peak = rows_of(tops, jnp.max)
    shrink, exponent = per_head(coef, 1, heads), per_head(coef, 4, heads)
    least = peak - 1.0
    most = peak - jnp.exp2(-shrink * jnp.log2((hi - lo).astype(F32)))
    close = 4e-6 + 5e-7 * jnp.abs(peak)
    zero = tuple(jnp.zeros((8, TILE), F32) for _ in range(3 * heads))

    def search(state):
        turn, tau, _ = state

        def body(c, sums):
            here = chunk_at(c)
            out = []
            for h in range(heads):
                u = jnp.maximum(zs[h, here, :] - tau[h : h + 1, :], TINY)
                curve = jnp.exp2(jnp.log2(u) * coef[3, h])
                slope = curve * u
                out += [sums[3 * h] + fold(slope * u), sums[3 * h + 1] + fold(slope), sums[3 * h + 2] + fold(curve)]
            return tuple(out)

        sums = lax.fori_loop(first, last, body, zero)
        mass, slope, curve = (rows_of(sums[i::3], jnp.sum) for i in range(3))
        bend = jnp.clip(1.0 - (exponent - 1.0) * curve * mass / (exponent * slope * slope), 0.0, 1.0)
        bend = jnp.where(turn < 5, bend, shrink)
        log_mass = jnp.log(mass)
        x = bend * log_mass
        rise = jnp.where(
            jnp.abs(x) < 0.1,
            log_mass * (1.0 - x * (0.5 - x * (1.0 / 6.0))),
            (1.0 - jnp.exp(-x)) / jnp.maximum(bend, 1e-6),
        )
        new = jnp.clip(tau + mass / (exponent * slope) * rise, least, most)
        return turn + 1, new, jnp.max(jnp.abs(new - tau))

    def finish(state):
        turn, tau, _, _, _ = state
        turn, tau, _ = lax.while_loop(
            lambda s: jnp.logical_and(s[2] > 6e-3, s[0] < 40), search, (turn, tau, jnp.float32(1.0))
        )

        def final(c, sums):
            here = chunk_at(c)
            out = []
            for h in range(heads):
                z = zs[h, here, :]
                u = jnp.maximum(z - tau[h : h + 1, :], TINY)
                slope = jnp.exp2(jnp.log2(u) * coef[2, h])
                p = slope * u
                ps[h, here, :] = low(p)
                soft = jnp.exp2((z - peak[h : h + 1, :]) * (LOG2E / SHARP))
                out += [sums[3 * h] + fold(p), sums[3 * h + 1] + fold(slope), sums[3 * h + 2] + fold(soft)]
            return tuple(out)

        sums = lax.fori_loop(first, last, final, zero)
        mass, slope, soft = (rows_of(sums[i::3], jnp.sum) for i in range(3))
        off = (mass - 1.0) / (exponent * slope)
        open_ = jnp.max(jnp.where(jnp.abs(off) > close, 1.0, 0.0))
        return turn, jnp.where(open_ > 0.0, jnp.clip(tau + off, least, most), tau), open_, mass, soft

    blank = jnp.ones((heads, TILE), F32)
    _, tau, _, mass, soft = lax.while_loop(
        lambda s: jnp.logical_and(s[2] > 0.0, s[0] < 40), finish, (0, least, jnp.float32(1.0), blank, blank)
    )
    inv = 1.0 / mass
    tau_ref[...] = tau
    top_ref[...] = peak + SHARP * jnp.log(soft)
    inv_ref[...] = inv
    clear_outside(first, last, keys, (ps,), slice(None))
    o_t[...] = jnp.zeros_like(o_t)
    for half in range(keys // PART):
        cols = slice(half * PART, (half + 1) * PART)

        @pl.when(meets(first, last, half))
        def _():
            for h in range(heads):
                rows = slice(h * width, (h + 1) * width)
                o_t[rows, :] += mm(v_t[rows, cols], ps[h, cols, :])

    for h in range(0, heads, 2):
        got = [o_t[i * width : (i + 1) * width, :] * inv[i : i + 1, :] for i in (h, h + 1)]
        o_ref[:, pair_of(h, width)] = low(jnp.concatenate(got, axis=0).T)


def attend(q, k, v, marks, coef):
    lo, hi, span = marks
    rows, width = q.shape
    keys, heads = k.shape[0], coef.shape[1]
    line = pl.BlockSpec((1, TILE), lambda t, *_: (0, t))
    tile = pl.BlockSpec((TILE, width), lambda t, *_: (t, 0))
    stat = pl.BlockSpec((heads, TILE), lambda t, *_: (0, t))
    full = pl.BlockSpec((keys, width), lambda t, *_: (0, 0))
    return pl.pallas_call(
        attend_kernel,
        grid_spec=pltpu.PrefetchScalarGridSpec(
            num_scalar_prefetch=2,
            grid=(rows // TILE,),
            in_specs=[line, line, tile, full, full],
            out_specs=[tile, stat, stat, stat],
            scratch_shapes=[
                pltpu.VMEM((width, keys), BF16),
                pltpu.VMEM((heads, keys, TILE), F32),
                pltpu.VMEM((heads, keys, TILE), BF16),
                pltpu.VMEM((heads, 2 * width // heads, TILE), BF16),
                pltpu.VMEM((width, TILE), F32),
            ],
        ),
        out_shape=[jax.ShapeDtypeStruct((rows, width), BF16)]
        + [jax.ShapeDtypeStruct((heads, rows), F32)] * 3,
        compiler_params=pltpu.CompilerParams(vmem_limit_bytes=24 * MB),
        cost_estimate=pl.CostEstimate(flops=14 * COST, transcendentals=0, bytes_accessed=14 * COST // 400),
        name="attend",
    )(span, coef, lo, hi, q, k, v)


def attend_back_kernel(
    span, coef, lo_ref, hi_ref, q_ref, go_ref, tau_ref, top_ref, inv_ref, q_all, go_all, k_ref, v_ref,
    dq_ref, dk_ref, dv_ref, ds_ref, k_t, zs, gs, ls, qz, gz, g_all, p_all, dq_t, dk_sum, dv_sum,
):
    heads, keys = zs.shape[0], zs.shape[1]
    width = q_ref.shape[1] // heads
    scale = 1.0 / math.sqrt(width)
    tile = pl.program_id(0)
    at = pl.ds(pl.multiple_of(tile * TILE, TILE), TILE)

    @pl.when(tile == 0)
    def _():
        k_t[...] = k_ref[...].T
        ds_ref[...] = jnp.zeros_like(ds_ref)

    split_pairs(qz, q_ref[...].T, heads, width)
    split_pairs(gz, go_ref[...].T, heads, width)
    lo, hi = lo_ref[...], hi_ref[...]
    tau, top, inv = tau_ref[...], top_ref[...], inv_ref[...]
    first, last = span[0, tile], span[1, tile]
    kinds = 5
    zero = tuple(jnp.zeros((8, TILE), F32) for _ in range(kinds * heads))

    def gather(c, sums):
        here = chunk_at(c)
        bias = bias_of(lo, hi, c * CHUNK)
        out = []
        for h in range(heads):
            z = mm(k_ref[here, pair_of(h, width)], qz[h]) * coef[0, h] + bias
            g = mm(v_ref[here, pair_of(h, width)], gz[h])
            u = jnp.maximum(z - tau[h : h + 1, :], TINY)
            log_u = jnp.log2(u)
            slope = jnp.exp2(log_u * coef[2, h])
            p = slope * u
            p_log = p * log_u
            zs[h, here, :] = z
            gs[h, here, :] = g
            ls[h, here, :] = slope
            new = (g * p, g * slope, slope, g * p_log, p_log)
            out += [sums[kinds * h + i] + fold(new[i]) for i in range(kinds)]
        return tuple(out)

    sums = lax.fori_loop(first, last, gather, zero)
    gp, gl, ll, gpl, pl_sum = (rows_of(sums[i::kinds], jnp.sum) for i in range(kinds))
    shrink = per_head(coef, 1, heads)
    inv_k = per_head(coef, 4, heads) * inv
    mean = gp * inv
    drop = inv_k * (gl - mean * ll)
    grad_k = inv * (gpl - mean * pl_sum) * (1.0 / LOG2E)
    clear_outside(first, last, keys, (g_all, p_all), at)

    def final(c, sums):
        here = chunk_at(c)
        out = []
        for h in range(heads):
            one = slice(h, h + 1)
            z, slope = zs[h, here, :], ls[h, here, :]
            p = slope * jnp.maximum(z - tau[one], TINY)
            r = (gs[h, here, :] - mean[one]) * slope * inv_k[one]
            g_z = r - drop[one] * jnp.exp2((z - top[one]) * (LOG2E / SHARP))
            g_all[h, here, at] = low(g_z * coef[1, h])
            p_all[h, here, at] = low(p * inv[one])
            out.append(sums[h] + fold(g_z * z))
        return tuple(out)

    sums = lax.fori_loop(first, last, final, zero[:heads])
    ds_ref[...] += rows_of(sums, jnp.sum) / shrink - grad_k / (shrink * shrink)
    dq_t[...] = jnp.zeros_like(dq_t)
    for half in range(keys // PART):
        cols = slice(half * PART, (half + 1) * PART)

        @pl.when(meets(first, last, half))
        def _():
            for h in range(heads):
                rows = slice(h * width, (h + 1) * width)
                dq_t[rows, :] += mm(k_t[rows, cols], g_all[h, cols, at])

    for h in range(0, heads, 2):
        dq_ref[:, pair_of(h, width)] = low(dq_t[pair_of(h, width), :].T * scale)

    @pl.when(tile == pl.num_programs(0) - 1)
    def _():
        dk_sum[...] = jnp.zeros_like(dk_sum)
        dv_sum[...] = jnp.zeros_like(dv_sum)
        tiles = PART // TILE
        lane = lax.broadcasted_iota(jnp.int32, (PART, 2 * width), 1) // width
        blank_rows = jnp.zeros((PART, 2 * width), BF16)
        for q_half in range(q_all.shape[0] // PART):
            rows = slice(q_half * PART, (q_half + 1) * PART)
            for half in range(keys // PART):
                cols = slice(half * PART, (half + 1) * PART)
                reach = [
                    meets(span[0, t], span[1, t], half) for t in range(q_half * tiles, (q_half + 1) * tiles)
                ]

                @pl.when(functools.reduce(jnp.logical_or, reach))
                def _():
                    for h in range(0, heads, 2):
                        pair = pair_of(h, width)
                        for i in (h, h + 1):
                            mine = lane == i % 2
                            dk_sum[cols, pair] += mm(g_all[i, cols, rows], jnp.where(mine, q_all[rows, pair], blank_rows))
                            dv_sum[cols, pair] += mm(p_all[i, cols, rows], jnp.where(mine, go_all[rows, pair], blank_rows))

        dk_ref[...] = low(dk_sum[...] * scale)
        dv_ref[...] = low(dv_sum[...])


def attend_back(q, k, v, go, stats, marks, coef):
    lo, hi, span = marks
    rows, width = q.shape
    keys, heads = k.shape[0], coef.shape[1]
    line = pl.BlockSpec((1, TILE), lambda t, *_: (0, t))
    tile = pl.BlockSpec((TILE, width), lambda t, *_: (t, 0))
    stat = pl.BlockSpec((heads, TILE), lambda t, *_: (0, t))
    q_full = pl.BlockSpec((rows, width), lambda t, *_: (0, 0))
    k_full = pl.BlockSpec((keys, width), lambda t, *_: (0, 0))
    return pl.pallas_call(
        attend_back_kernel,
        grid_spec=pltpu.PrefetchScalarGridSpec(
            num_scalar_prefetch=2,
            grid=(rows // TILE,),
            in_specs=[line, line, tile, tile, stat, stat, stat, q_full, q_full, k_full, k_full],
            out_specs=[tile, k_full, k_full, pl.BlockSpec((heads, TILE), lambda t, *_: (0, 0))],
            scratch_shapes=[pltpu.VMEM((width, keys), BF16)]
            + [pltpu.VMEM((heads, keys, TILE), F32)] * 3
            + [pltpu.VMEM((heads, 2 * width // heads, TILE), BF16)] * 2
            + [pltpu.VMEM((heads, keys, rows), BF16)] * 2
            + [pltpu.VMEM((width, TILE), F32)]
            + [pltpu.VMEM((keys, width), F32)] * 2,
        ),
        out_shape=[
            jax.ShapeDtypeStruct((rows, width), BF16),
            jax.ShapeDtypeStruct((keys, width), BF16),
            jax.ShapeDtypeStruct((keys, width), BF16),
            jax.ShapeDtypeStruct((heads, TILE), F32),
        ],
        compiler_params=pltpu.CompilerParams(vmem_limit_bytes=36 * MB),
        cost_estimate=pl.CostEstimate(flops=14 * COST, transcendentals=0, bytes_accessed=14 * COST // 400),
        name="attend_back",
    )(span, coef, lo, hi, q, go, *stats, q, go, k, v)


def starts_of(lengths, rank):
    number = jnp.arange(lengths.shape[0])
    before = rank[None, :] < rank[:, None]
    before |= (rank[None, :] == rank[:, None]) & (number[None, :] < number[:, None])
    return jnp.sum(jnp.where(before, lengths[None, :], 0), axis=1)


def marks_of(q_starts, q_lengths, k_starts, k_lengths, rows, causal):
    places = jnp.arange(rows, dtype=jnp.int32)
    pick = (places[:, None] >= q_starts[None, :]) & (places[:, None] < (q_starts + q_lengths)[None, :])
    lo = jnp.sum(jnp.where(pick, k_starts[None, :], 0), axis=1)
    hi = jnp.sum(jnp.where(pick, (k_starts + k_lengths)[None, :], 0), axis=1)
    if causal:
        hi = jnp.minimum(hi, places + 1)
    first = jnp.min(lo.reshape(-1, TILE), axis=1) // CHUNK
    last = (jnp.max(hi.reshape(-1, TILE), axis=1) + CHUNK - 1) // CHUNK
    return (lo[None], hi[None], jnp.stack([first, last]))


def coefs_of(shrink, width):
    exponent = 1.0 / shrink
    return jnp.stack([shrink / math.sqrt(width), shrink, exponent - 1.0, exponent - 2.0, exponent])


GAIN, FIRST, MID, TAIL = 48, 64, 208, 144
HALF = 240


def inner_rows(inner, h):
    return [inner[256 * h + 64 * i : 256 * h + 64 * (i + 1)] for i in range(4)]


def pack_halves(section, qkv, out, cross, inner, down, gain_rows):
    width = out.shape[1]
    for h in range(2):
        few, many = slice(16 * h, 16 * h + 16), slice(64 * h, 64 * h + 64)
        parts = [(16 * i, 0, qkv[few, width * i : width * (i + 1)]) for i in range(3)]
        parts.append((GAIN, 0, gain_rows if h == 0 else jnp.zeros_like(gain_rows)))
        quarters = [(128 * i, part) for i, part in enumerate(inner_rows(inner, h))]
        if section == 0:
            parts += [(FIRST, 0, cross[few, :width]), (FIRST + 16, 0, cross[few, width:])]
            parts += [(FIRST + 32, 0, down[many]), (FIRST + 160, 0, out[few])]
            parts += [(FIRST + 96, at, part) for at, part in quarters]
        else:
            parts += [(FIRST, 0, out[few]), (FIRST + 16, 0, cross[few, :width])]
            parts += [(FIRST + 32, 0, down[many]), (FIRST + 160, 0, cross[few, width:])]
            parts += [(FIRST + 96, at, part) for at, part in quarters]
        yield h, parts


def pack_plain(section, qkv, out, cross, inner, down, gain_rows):
    packs = []
    for _, parts in pack_halves(section, qkv, out, cross, inner, down, gain_rows):
        pack = jnp.zeros((HALF, out.shape[1]), BF16)
        for row, col, value in parts:
            pack = lax.dynamic_update_slice(pack, value, (row, col))
        packs.append(pack)
    return jnp.stack(packs)


def pack_kernel(me, qkv, out, cross, inner, down, gains, kept, sent):
    width = out.shape[1]
    columns = gains.shape[1]
    spot = lax.broadcasted_iota(jnp.int32, (columns, width), 1) - me[0] * columns
    here = spot == lax.broadcasted_iota(jnp.int32, (columns, width), 0)
    spread = low(mm(gains[...], jnp.where(here, 1.0, 0.0).astype(BF16)))
    spread = jnp.concatenate([spread, jnp.zeros((16 - gains.shape[0], width), BF16)], axis=0)
    for section in range(2):

        @pl.when(me[1] == section)
        def _():
            shards = (qkv[...], out[...], cross[...], inner[...], down[...], spread)
            for h, parts in pack_halves(section, *shards):
                dst = kept if h == section else sent
                for row, col, value in parts:
                    dst[row : row + value.shape[0], col : col + value.shape[1]] = value


def pack_shards(me, qkv, out, cross, inner, down, gains):
    half = jax.ShapeDtypeStruct((HALF, out.shape[1]), BF16)
    return pl.pallas_call(
        pack_kernel,
        in_specs=[TABLE] + [WHOLE] * 6,
        out_specs=[WHOLE] * 2,
        out_shape=[half, half],
        name="pack_shards",
    )(me, qkv, out, cross, inner, down, gains)


def rows_at(block, rows):
    return pl.ds(pl.multiple_of(block * rows, rows), rows)


def start_copy(src, dst, sem):
    pltpu.make_async_copy(src, dst, sem).start()


def wait_for(ref, sem):
    pltpu.make_async_copy(ref, ref, sem).wait()


def each_half(table, own, other, body):
    for which, pieces in enumerate((own, other)):
        half = table[2, 0] if which == 0 else 1 - table[2, 0]
        first = 0
        for src in pieces:

            @pl.loop(0, src.shape[0])
            def _(p, src=src, first=first):
                body(src.at[p], table[which, first + p], half)

            first += src.shape[0]


def fetch_few(table, own, other, row, dst, sem):
    def body(src, j, half):
        start_copy(src.at[pl.ds(row, 16), :], dst.at[j, pl.ds(pl.multiple_of(16 * half, 16), 16), :], sem)

    each_half(table, own, other, body)


def fetch_ffn(table, own, other, row, inner, down, sems):
    def body(src, j, half):
        start_copy(src.at[pl.ds(row, 64), :], down.at[j, pl.ds(pl.multiple_of(64 * half, 64), 64), :], sems.at[1])
        for i in range(4):
            rows = pl.ds(pl.multiple_of(256 * half + 64 * i, 64), 64)
            start_copy(src.at[pl.ds(row + 64, 64), pl.ds(128 * i, 128)], inner.at[j, rows, :], sems.at[0])

    each_half(table, own, other, body)


def joined(blocks):
    value = blocks[...]
    return value.reshape(-1, value.shape[2])


def inner_cols(inner, c):
    return jnp.concatenate([inner[4 * c + i] for i in range(4)], axis=1)


def down_rows(down, c):
    return joined(down[4 * c : 4 * c + 4])


def pack_pair(rows, width):
    return [jax.ShapeDtypeStruct((BLOCKS, rows, width), BF16)] * 2


def stage_rows(stage, offset, grad):
    for j in range(BLOCKS):
        for h in range(2):
            stage[h, j, offset : offset + 16, :] = grad[32 * j + 16 * h : 32 * j + 16 * h + 16, :]


def stage_down(stage, offset, c, grad):
    for j in range(4):
        for h in range(2):
            at = 128 * j + 64 * h
            stage[h, 4 * c + j, offset : offset + 64, :] = grad[at : at + 64, :]


def stage_inner(stage, offset, c, grad):
    for j in range(4):
        for h in range(2):
            for i in range(4):
                at = 256 * h + 64 * i
                stage[h, 4 * c + j, offset : offset + 64, 128 * i : 128 * (i + 1)] = grad[
                    at : at + 64, 128 * j : 128 * (j + 1)
                ]


def send_stage(stage, kept, sent, place, sem):
    for h in range(2):
        for which, dst in enumerate((kept, sent)):

            @pl.when(place[2, h] == which)
            def _():
                @pl.loop(0, BLOCKS)
                def _(j):
                    pltpu.make_async_copy(stage.at[h, j], dst.at[place[h, j]], sem).start()


STEP = 64


def each_rows(rows, body):
    for i in range(rows // STEP):
        body(slice(i * STEP, (i + 1) * STEP))


def centred(v):
    shifted = v - jnp.mean(v, axis=-1, keepdims=True)
    rate = lax.rsqrt(jnp.mean(shifted * shifted, axis=-1, keepdims=True) + EPS)
    return shifted * rate, rate


def norm_back(v, gain, grad):
    unit, rate = centred(v)
    e = grad * gain
    back = e - jnp.mean(e, axis=-1, keepdims=True) - unit * jnp.mean(e * unit, axis=-1, keepdims=True)
    return back * rate, grad * unit


def gelu_parts(u):
    phi = 0.5 + 0.5 * lax.erf(u * (1.0 / math.sqrt(2.0)))
    bell = jnp.exp2(u * u * (-0.5 * LOG2E)) * (1.0 / math.sqrt(2.0 * math.pi))
    return u * phi, phi + u * bell


def places_of(dest):
    rows = dest.shape[1]
    return jnp.where(lax.broadcasted_iota(jnp.int32, (rows, rows), 0) == dest[...], 1.0, 0.0).astype(BF16)


def sort_kernel(section, inputs, came, cotangent, dest_e, dest_d, x_e, x_d, ct):
    s = section[0]
    place_e, place_d = places_of(dest_e), places_of(dest_d)
    for owner, dst, place in ((0, x_e, place_e), (1, x_d, place_d)):

        @pl.when(s == owner)
        def _():
            dst[...] = low(mm(place, inputs[s]))

        @pl.when(s != owner)
        def _():
            dst[...] = low(mm(place, came[...]))

    ct[...] = low(mm(place_d, cotangent[s]))


def sort_rows(section, inputs, came, cotangent, dest_e, dest_d):
    row16 = jax.ShapeDtypeStruct(came.shape, BF16)
    return pl.pallas_call(
        sort_kernel,
        in_specs=[TABLE] + [WHOLE] * 5,
        out_specs=[WHOLE] * 3,
        out_shape=[row16] * 3,
        compiler_params=pltpu.CompilerParams(vmem_limit_bytes=10 * MB),
        name="sort_rows",
    )(section, inputs, came, cotangent, dest_e, dest_d)


def fetch_front(table, own, other, w, sem):
    def body(src, j, half):
        at = pl.ds(pl.multiple_of(32 * j + 16 * half, 16), 16)
        for i in range(3):
            start_copy(src.at[pl.ds(16 * i, 16), :], w.at[at, pl.ds(512 * i, 512)], sem)

    each_half(table, [own], [other], body)


def front_kernel(moves, table, x, own, other, n, q, k, v, g, w, gs, prod, sems):
    for which, src in enumerate((own, other)):

        @pl.loop(0, BLOCKS)
        def _(p):
            pltpu.make_async_copy(src.at[p, pl.ds(GAIN, 16), :], gs.at[which, p], sems.at[1]).start()

    fetch_front(table, own, other, w, sems.at[0])
    wait_for(gs, sems.at[1])
    gains = jnp.sum(gs[...].astype(F32), axis=(0, 1))[0:8]
    g[...] = gains
    gain = gains[0:1]
    moves.ready(x)

    def body(rows):
        n[rows, :] = low(centred(x[rows, :].astype(F32))[0] * gain)

    each_rows(x.shape[0], body)
    moves.done(n)
    wait_for(w, sems.at[0])
    for i, out in enumerate((q, k, v)):
        prod[...] = mm(n[...], w[:, 512 * i : 512 * (i + 1)])

        def keep(rows, out=out):
            out[rows, :] = low(prod[rows, :])

        each_rows(x.shape[0], keep)
        moves.done(out)


def front(table, x, own, other):
    rows, width = x.shape
    row16 = jax.ShapeDtypeStruct((rows, width), BF16)
    gain = jax.ShapeDtypeStruct((8, width), F32)
    return call_dense(
        front_kernel, "front", 4, [table], [x], [own, other], [row16] + [Both(row16)] * 3 + [Near(gain)], [],
        [
            pltpu.VMEM((width, 3 * width), BF16),
            pltpu.VMEM((2, BLOCKS, 16, width), BF16),
            pltpu.VMEM((rows, width), F32),
            pltpu.SemaphoreType.DMA((2,)),
        ],
    )


def mid_kernel(
    pieces, moves, table, a_e, a_d, x_e, x_d, g_e, g_d, dest, *refs
):
    mid_body(moves, table, a_e, a_d, x_e, x_d, g_e, g_d, dest, refs[:pieces], refs[pieces : 2 * pieces], *refs[2 * pieces :])


def mid_body(
    moves, table, a_e, a_d, x_e, x_d, g_e, g_d, dest, own, other,
    m_e, n_e, act, slope, end, memory, mem_k, mem_v, m_d, n_d, query, memory_out,
    w_out, w_in, w_down, w_cross, w_query, prod, spare, total, sems,
):
    fetch_few(table, own, other, 160, w_out.at[0], sems.at[0])
    fetch_ffn(table, own, other, 32, w_in, w_down, sems.at[pl.ds(1, 2)])
    fetch_few(table, own, other, 176, w_out.at[1], sems.at[3])
    for i in range(2):
        fetch_few(table, own, other, 16 * i, w_cross.at[i], sems.at[4])
    fetch_few(table, own, other, 192, w_query, sems.at[5])
    count = x_e.shape[0]

    def attended(a, x, g, m, n, section, sem):
        moves.ready(a)
        wait_for(w_out.at[section], sem)
        prod[...] = mm(a[...], joined(w_out[section]))
        moves.ready(x)
        gain = g[1:2, :]

        def body(rows):
            middle = x[rows, :].astype(F32) + prod[rows, :]
            m[rows, :] = middle
            n[rows, :] = low(centred(middle)[0] * gain)

        each_rows(count, body)
        moves.done(m, n)

    attended(a_e, x_e, g_e, m_e, n_e, 0, sems.at[0])
    wait_for(w_in, sems.at[1])
    wait_for(w_down, sems.at[2])
    total[...] = m_e[...]
    prods = (prod, spare)
    prod[...] = mm(n_e[...], inner_cols(w_in, 0))
    for c in range(4):
        cols = slice(512 * c, 512 * (c + 1))
        if c < 3:
            prods[(c + 1) % 2][...] = mm(n_e[...], inner_cols(w_in, c + 1))

        def body(rows, cols=cols, hidden=prods[c % 2]):
            value, rate = gelu_parts(hidden[rows, :])
            act[rows, cols] = low(value)
            slope[rows, cols] = low(rate)

        each_rows(count, body)
        total[...] += mm(act[:, cols], down_rows(w_down, c))

    moves.done(act, slope)
    gain = g_e[2:3, :]

    def body(rows):
        ending = total[rows, :]
        end[rows, :] = ending
        memory[rows, :] = low(centred(ending)[0] * gain)

    each_rows(count, body)
    moves.done(end, memory)
    wait_for(w_cross, sems.at[4])
    mem_k[...] = low(mm(memory[...], joined(w_cross[0])))
    mem_v[...] = low(mm(memory[...], joined(w_cross[1])))
    moves.done(mem_k, mem_v)
    memory_out[...] = low(mm_tn(places_of(dest), memory[...]))
    moves.done(memory_out)
    attended(a_d, x_d, g_d, m_d, n_d, 1, sems.at[3])
    wait_for(w_query, sems.at[5])
    query[...] = low(mm(n_d[...], joined(w_query)))
    moves.done(query)


def mid(table, a_e, a_d, x_e, x_d, g_e, g_d, dest, own, other):
    rows, width = x_e.shape
    row16 = jax.ShapeDtypeStruct((rows, width), BF16)
    row32 = jax.ShapeDtypeStruct((rows, width), F32)
    wide = jax.ShapeDtypeStruct((rows, 4 * width), BF16)
    return call_dense(
        functools.partial(mid_kernel, len(own)), "mid", 8, [table],
        [a_e, a_d, x_e, x_d, Near(g_e), Near(g_d), Near(dest)], [*own, *other],
        [row32, row16, wide, wide, row32, row16, Both(row16), Both(row16), row32, row16, Both(row16), row16], [],
        [
            pltpu.VMEM((2, BLOCKS, 32, width), BF16),
            pltpu.VMEM((BLOCKS, width, 128), BF16),
            pltpu.VMEM((BLOCKS, 128, width), BF16),
            pltpu.VMEM((2, BLOCKS, 32, width), BF16),
            pltpu.VMEM((BLOCKS, 32, width), BF16),
            pltpu.VMEM((rows, width), F32),
            pltpu.VMEM((rows, width), F32),
            pltpu.VMEM((rows, width), F32),
            pltpu.SemaphoreType.DMA((6,)),
        ],
    )


def tail_kernel(
    pieces, moves, place, section, table, crossed, m_d, ct, g_d, dest, memory, *refs
):
    own, other = refs[:pieces], refs[pieces : 2 * pieces]
    tail_body(moves, place, section, table, crossed, m_d, ct, g_d, dest, memory, own, other, *refs[2 * pieces :])


def tail_body(
    moves, place, section, table, crossed, m_d, ct, g_d, dest, memory, own, other,
    stay, leave, second_grad, crossed_grad, gain_grad, kept, sent,
    w_out, w_in, w_down, second, n, unit_grad, out_prod, prod, act, hidden, grad, total, stage, sems,
):
    fetch_few(table, own, other, 128, w_out, sems.at[0])
    fetch_ffn(table, own, other, 0, w_in, w_down, sems.at[pl.ds(1, 2)])
    count = m_d.shape[0]
    wait_for(w_out, sems.at[0])
    out_prod[...] = mm(crossed[...], joined(w_out))
    moves.ready(m_d)
    gain = g_d[2:3, :]

    def body(rows):
        value = m_d[rows, :] + out_prod[rows, :]
        second[rows, :] = value
        total[rows, :] = value
        n[rows, :] = low(centred(value)[0] * gain)
        unit_grad[rows, :] = jnp.zeros((STEP, value.shape[1]), F32)

    each_rows(count, body)
    wait_for(w_in, sems.at[1])
    wait_for(w_down, sems.at[2])

    moves.ready(ct)

    def products(c):
        cols = slice(512 * c, 512 * (c + 1))
        prod[c % 2] = mm(n[...], inner_cols(w_in, c))
        hidden[c % 2] = mm_nt(ct[...], down_rows(w_down, c))

    products(0)
    for c in range(4):
        cols = slice(512 * c, 512 * (c + 1))
        if c < 3:
            products(c + 1)

        def body(rows, c=c):
            value, rate = gelu_parts(prod[c % 2, rows, :])
            act[c % 2, rows, :] = low(value)
            grad[c % 2, rows, :] = low(hidden[c % 2, rows, :] * rate)

        each_rows(count, body)
        total[...] += mm(act[c % 2], down_rows(w_down, c))
        stage_down(stage, 0, c, low(mm_tn(act[c % 2], ct[...])))
        stage_inner(stage, 64, c, low(mm_tn(n[...], grad[c % 2])))
        unit_grad[...] += mm_nt(grad[c % 2], inner_cols(w_in, c))

    gain_grad[...] = jnp.zeros_like(gain_grad)

    def back(rows):
        act[0, rows, :] = low(total[rows, :])
        part, gained = norm_back(second[rows, :], gain, unit_grad[rows, :])
        gain_grad[...] += fold(gained)
        whole = ct[rows, :].astype(F32) + part
        second_grad[rows, :] = whole
        n[rows, :] = low(whole)

    each_rows(count, back)
    moves.done(second_grad)
    stage_rows(stage, 128, low(mm_tn(crossed[...], n[...])))
    send_stage(stage, kept, sent, place, sems.at[3])
    crossed_grad[...] = low(mm_nt(n[...], joined(w_out)))
    moves.ready(memory)
    for owner in range(2):

        @pl.when(section[0] == owner)
        def _():
            out, through = (leave, stay) if owner == 0 else (stay, leave)
            out[...] = low(mm_tn(places_of(dest), act[0]))
            through[...] = memory[...]

    moves.done(stay, leave)
    wait_for(stage, sems.at[3])


def tail(place, section, table, crossed, m_d, ct, g_d, dest, memory, own, other):
    rows, width = m_d.shape
    row16 = jax.ShapeDtypeStruct((rows, width), BF16)
    row32 = jax.ShapeDtypeStruct((rows, width), F32)
    return call_dense(
        functools.partial(tail_kernel, len(own)), "tail", 15, [place, section, table],
        [Near(crossed), m_d, ct, Near(g_d), Near(dest), memory], [*own, *other],
        [row16, row16, row32, Near(row16), Near(jax.ShapeDtypeStruct((8, width), F32))], pack_pair(144, width),
        [
            pltpu.VMEM((BLOCKS, 32, width), BF16),
            pltpu.VMEM((BLOCKS, width, 128), BF16),
            pltpu.VMEM((BLOCKS, 128, width), BF16),
            pltpu.VMEM((rows, width), F32),
            pltpu.VMEM((rows, width), BF16),
            pltpu.VMEM((rows, width), F32),
            pltpu.VMEM((rows, width), F32),
            pltpu.VMEM((2, rows, width), F32),
            pltpu.VMEM((2, rows, width), BF16),
            pltpu.VMEM((2, rows, width), F32),
            pltpu.VMEM((2, rows, width), BF16),
            pltpu.VMEM((rows, width), F32),
            pltpu.VMEM((2, BLOCKS, 144, width), BF16),
            pltpu.SemaphoreType.DMA((4,)),
        ],
    )


def mid_back_kernel(pieces, moves, place, table, *refs):
    ins, refs = refs[:16], refs[16:]
    mid_back_body(moves, place, table, *ins, refs[:pieces], refs[pieces : 2 * pieces], *refs[2 * pieces :])


def mid_back_body(
    moves, place, table, dq, dk, dv, n_d, m_d, second_grad, a_d, memory, end, act, slope, n_e, m_e, a_e, g_e, g_d, own, other,
    md_grad, ad_grad, me_grad, ae_grad, ge_grad, kept, sent,
    w_out, w_in, w_down, w_cross, w_query, prod, hidden, grad, total, small, stage, sems,
):
    fetch_few(table, own, other, 192, w_query, sems.at[5])
    fetch_few(table, own, other, 176, w_out.at[1], sems.at[3])
    for i in range(2):
        fetch_few(table, own, other, 16 * i, w_cross.at[i], sems.at[4])
    fetch_ffn(table, own, other, 32, w_in, w_down, sems.at[pl.ds(1, 2)])
    fetch_few(table, own, other, 160, w_out.at[0], sems.at[0])
    count = m_d.shape[0]
    ge_grad[...] = jnp.zeros_like(ge_grad)

    def through_out(a, grad, result, section, offset):
        stage_rows(stage, offset, low(mm_tn(a[...], small[...])))
        result[...] = low(mm_nt(small[...], joined(w_out[section])))

    moves.ready(n_d)
    stage_rows(stage, 176, low(mm_tn(n_d[...], dq[...])))
    wait_for(w_query, sems.at[5])
    prod[...] = mm_nt(dq[...], joined(w_query))
    moves.ready(m_d, second_grad)
    gain_d = g_d[1:2, :]

    def decoder(rows):
        part, _ = norm_back(m_d[rows, :], gain_d, prod[rows, :])
        whole = second_grad[rows, :] + part
        md_grad[rows, :] = whole
        small[rows, :] = low(whole)

    each_rows(count, decoder)
    moves.done(md_grad)
    moves.ready(a_d)
    wait_for(w_out.at[1], sems.at[3])
    through_out(a_d, md_grad, ad_grad, 1, 192)

    moves.ready(memory)
    stage_rows(stage, 0, low(mm_tn(memory[...], dk[...])))
    stage_rows(stage, 16, low(mm_tn(memory[...], dv[...])))
    wait_for(w_cross, sems.at[4])
    prod[...] = mm_nt(dk[...], joined(w_cross[0]))
    prod[...] += mm_nt(dv[...], joined(w_cross[1]))
    moves.ready(end)
    gain_two = g_e[2:3, :]

    def ending(rows):
        part, _ = norm_back(end[rows, :], gain_two, prod[rows, :])
        me_grad[rows, :] = part
        small[rows, :] = low(part)
        total[rows, :] = jnp.zeros_like(part)

    each_rows(count, ending)
    wait_for(w_in, sems.at[1])
    wait_for(w_down, sems.at[2])

    hidden[0] = mm_nt(small[...], down_rows(w_down, 0))
    moves.ready(slope, act, n_e)
    for c in range(4):
        cols = slice(512 * c, 512 * (c + 1))
        if c < 3:
            hidden[(c + 1) % 2] = mm_nt(small[...], down_rows(w_down, c + 1))

        def body(rows, c=c, cols=cols):
            grad[c % 2, rows, :] = low(hidden[c % 2, rows, :] * slope[rows, cols].astype(F32))

        each_rows(count, body)
        stage_down(stage, 32, c, low(mm_tn(act[:, cols], small[...])))
        stage_inner(stage, 96, c, low(mm_tn(n_e[...], grad[c % 2])))
        total[...] += mm_nt(grad[c % 2], inner_cols(w_in, c))

    moves.ready(m_e)
    gain_one = g_e[1:2, :]

    def encoder(rows):
        part, gained = norm_back(m_e[rows, :], gain_one, total[rows, :])
        ge_grad[...] += fold(gained)
        whole = me_grad[rows, :] + part
        me_grad[rows, :] = whole
        small[rows, :] = low(whole)

    each_rows(count, encoder)
    moves.done(me_grad)
    moves.ready(a_e)
    wait_for(w_out.at[0], sems.at[0])
    through_out(a_e, me_grad, ae_grad, 0, 160)
    send_stage(stage, kept, sent, place, sems.at[6])
    wait_for(stage, sems.at[6])


def mid_back(place, table, dq, dk, dv, n_d, m_d, second_grad, a_d, memory, end, act, slope, n_e, m_e, a_e, g_e, g_d, own, other):
    rows, width = m_d.shape
    row16 = jax.ShapeDtypeStruct((rows, width), BF16)
    row32 = jax.ShapeDtypeStruct((rows, width), F32)
    return call_dense(
        functools.partial(mid_back_kernel, len(own)), "mid_back", 19, [place, table],
        [Near(dq), Near(dk), Near(dv), n_d, m_d, second_grad, a_d, memory, end, act, slope, n_e, m_e, a_e, Near(g_e), Near(g_d)],
        [*own, *other], [row32, Near(row16), row32, Near(row16), Near(jax.ShapeDtypeStruct((8, width), F32))],
        pack_pair(208, width),
        [
            pltpu.VMEM((2, BLOCKS, 32, width), BF16),
            pltpu.VMEM((BLOCKS, width, 128), BF16),
            pltpu.VMEM((BLOCKS, 128, width), BF16),
            pltpu.VMEM((2, BLOCKS, 32, width), BF16),
            pltpu.VMEM((BLOCKS, 32, width), BF16),
            pltpu.VMEM((rows, width), F32),
            pltpu.VMEM((2, rows, width), F32),
            pltpu.VMEM((2, rows, width), BF16),
            pltpu.VMEM((rows, width), F32),
            pltpu.VMEM((rows, width), BF16),
            pltpu.VMEM((2, BLOCKS, 208, width), BF16),
            pltpu.SemaphoreType.DMA((7,)),
        ],
    )


def front_w_kernel(moves, place, qe, ke, ve, qd, kd, vd, n_e, n_d, ge_one, gd_two, ds_e, ds_d, ds_c, kept, sent, stage, sems):
    width = n_e.shape[1]
    for section, (grads, n) in enumerate((((qe, ke, ve), n_e), ((qd, kd, vd), n_d))):
        moves.ready(n)
        for i in range(3):
            grad = low(mm_tn(n[...], grads[i][...]))
            for j in range(BLOCKS):
                stage[section, j, 32 * i : 32 * i + 32, :] = grad[32 * j : 32 * j + 32, :]
    lane = lax.broadcasted_iota(jnp.int32, (8, width), 1)
    heads = jnp.zeros((8, width), F32)
    for i, ds in enumerate((ds_e, ds_d, ds_c)):
        heads = jnp.where(lane == i, jnp.sum(ds[...], axis=1, keepdims=True), heads)
    lines = [jnp.sum(g[...], axis=0, keepdims=True) for g in (ge_one, gd_two)]
    extra = low(jnp.concatenate(lines + [jnp.zeros((6, width), F32), heads], axis=0))
    for h in range(2):
        for j in range(BLOCKS):
            stage[h, j, 96:112, :] = extra
    send_stage(stage, kept, sent, place, sems.at[0])
    wait_for(stage, sems.at[0])


def front_w(place, grads_e, grads_d, n_e, n_d, ge_one, gd_two, ds):
    width = n_e.shape[1]
    near = [Near(g) for g in (*grads_e, *grads_d)]
    return call_dense(
        front_w_kernel, "front_w", 5, [place], [*near, n_e, n_d, *map(Near, (ge_one, gd_two, *ds))], [],
        [], pack_pair(112, width),
        [pltpu.VMEM((2, BLOCKS, 112, width), BF16), pltpu.SemaphoreType.DMA((1,))],
    )


def front_x_kernel(moves, table, dq, dk, dv, x, m_grad, g, dest, own, other, x_grad, w, prod, high, rest, sems):
    fetch_front(table, own, other, w, sems.at[0])
    wait_for(w, sems.at[0])
    prod[...] = mm_nt(dq[...], w[:, 0:512])
    prod[...] += mm_nt(dk[...], w[:, 512:1024])
    prod[...] += mm_nt(dv[...], w[:, 1024:1536])
    moves.ready(x, m_grad)
    gain = g[0:1, :]

    def body(rows):
        part, _ = norm_back(x[rows, :].astype(F32), gain, prod[rows, :])
        whole = m_grad[rows, :] + part
        high[rows, :] = low(whole)
        rest[rows, :] = low(whole - high[rows, :].astype(F32))

    each_rows(x.shape[0], body)
    place = places_of(dest)
    x_grad[...] = mm_tn(place, high[...])
    x_grad[...] += mm_tn(place, rest[...])
    moves.done(x_grad)


def front_x(table, grads, x, m_grad, g, dest, own, other):
    rows, width = x.shape
    return call_dense(
        front_x_kernel, "front_x", 4, [table], [*map(Near, grads), x, m_grad, Near(g), Near(dest)], [own, other],
        [jax.ShapeDtypeStruct((rows, width), F32)], [],
        [
            pltpu.VMEM((width, 3 * width), BF16),
            pltpu.VMEM((rows, width), F32),
            pltpu.VMEM((rows, width), BF16),
            pltpu.VMEM((rows, width), BF16),
            pltpu.SemaphoreType.DMA((1,)),
        ],
    )[0]


def exact(a, b, dims):
    return lax.dot_general(a, b, (dims, ((), ())), precision=lax.Precision.HIGHEST, preferred_element_type=F32)


def finish_kernel(
    moves, place, own, came, last, w_qkv, w_cross, gains, slope, qkv, out, cross, inner, down, gain, alpha
):
    columns = gains.shape[1]
    moves.ready(w_qkv, w_cross, gains, slope)
    extra = last[96:112, :]
    for i in range(3):
        qkv[:, 512 * i : 512 * (i + 1)] = last[32 * i : 32 * i + 32, :]

    def halves_to(offsets):
        at_out, at_cross, at_inner, at_down = offsets
        for h in range(2):
            for section, src in ((h, own), (1 - h, came)):

                @pl.when(place[1] == section)
                def _():
                    few = slice(16 * h, 16 * h + 16)
                    out[few, :] = src[at_out : at_out + 16, :].astype(F32)
                    for i in range(2):
                        at = at_cross[i]
                        cross[few, 512 * i : 512 * (i + 1)] = src[at : at + 16, :].astype(F32)
                    for i in range(4):
                        rows = slice(256 * h + 64 * i, 256 * h + 64 * (i + 1))
                        inner[rows, :] = src[at_inner : at_inner + 64, 128 * i : 128 * (i + 1)].astype(F32)
                    down[64 * h : 64 * h + 64, :] = src[at_down : at_down + 64, :].astype(F32)

    spot = lax.broadcasted_iota(jnp.int32, (extra.shape[1], columns), 0) - place[0] * columns
    pick = jnp.where(spot == lax.broadcasted_iota(jnp.int32, (extra.shape[1], columns), 1), 1.0, 0.0)
    split = exact(extra[0:8], pick, ((1,), (0,)))

    def reach(weight, grad):
        weighted = weight.astype(F32) * grad
        return exact(jnp.ones((8, weighted.shape[1]), F32), weighted, ((1,), (1,)))[0:1]

    @pl.when(place[1] == 0)
    def _():
        halves_to((160, (0, 16), 96, 32))
        gain[0:1, :] = reach(w_qkv[...], qkv[...]) / gains[0:1, :].astype(F32)
        gain[1:2, :] = split[0:1]
        gain[2:3, :] = reach(w_cross[...], cross[...]) / gains[2:3, :].astype(F32)

    @pl.when(place[1] == 1)
    def _():
        halves_to((160, (144, 128), 64, 0))
        gain[0:1, :] = reach(w_qkv[...], qkv[...]) / gains[0:1, :].astype(F32)
        gain[1:2, :] = reach(w_cross[:, 0:512], cross[:, 0:512]) / gains[1:2, :].astype(F32)
        gain[2:3, :] = split[1:2]

    alpha[...] = extra[8:16, 0:128].T[0:3, :] * slope[...]
    moves.done(qkv, out, cross, inner, down, gain, alpha)


def finish(place, own, came, last, w_qkv, w_cross, gains, slope):
    shapes = [(32, 1536), (32, 512), (32, 1024), (512, 128), (128, 512), (3, 32), (3, 8)]
    return call_dense(
        finish_kernel, "finish", 2, [place], [Near(own), Near(came), Near(last), w_qkv, w_cross, gains, slope], [],
        [jax.ShapeDtypeStruct(shape, F32) for shape in shapes], [], [],
    )


ORDER = ((4, 8, 1, 2), (4, 8, 2, 1))
SHIFT = np.array(
    [[functools.reduce(lambda a, b: a ^ b, [m for b, m in enumerate(order) if p >> b & 1], 0) for p in range(BLOCKS)] for order in ORDER],
    np.int32,
)
WHERE = np.argsort(SHIFT, axis=1).astype(np.int32)
SWAP = [(0, 1), (1, 0)]


def swap(value):
    return lax.ppermute(value, "section", SWAP)


def hop(value, bit):
    pairs = [
        (BLOCKS * s + i, BLOCKS * s + (i ^ ORDER[s][bit])) for s in range(2) for i in range(BLOCKS)
    ]
    return lax.ppermute(value, ("section", "dp"), pairs)


def jump(value, position):
    pairs = [
        (BLOCKS * s + i, BLOCKS * s + (i ^ int(SHIFT[s, position]))) for s in range(2) for i in range(BLOCKS)
    ]
    return lax.ppermute(value, ("section", "dp"), pairs)


def tie(value, held):
    return lax.optimization_barrier((value, held))


def behind(out, *packs):
    kept = [pack[0] for pack in packs]
    out, kept = lax.optimization_barrier((out, kept))
    for pack, value in zip(packs, kept):
        pack[0] = value
    return out


def total(terms, first, last):
    return low(sum(term[first:last].astype(F32) for term in terms))


def to_line(terms):
    return [total(terms, i, i + 1)[0] for i in (1, 2, 3)]


def along_line(sent):
    return [jump(block, i + 1) for i, block in enumerate(sent)]


def at_last(terms, came):
    return sum([term[0].astype(F32) for term in terms] + [block.astype(F32) for block in came])


def inner_of(halves):
    quarter, width = halves[0].shape
    rows = [h.reshape(quarter, 4, width // 4).transpose(1, 0, 2).reshape(4 * quarter, width // 4) for h in halves]
    return jnp.concatenate(rows, axis=0)


def spread_line(block):
    return jnp.stack([block] + [jump(block, i) for i in (1, 2, 3)])


def spread_plane(blocks, bit):
    return jnp.concatenate([blocks, hop(blocks, bit)], axis=0)


def weights_near(attn_qkv, attn_out, cross_proj, ffn_in, ffn_out, gains, later):
    me, section = lax.axis_index("dp"), lax.axis_index("section")
    kept, sent = pack_shards(
        jnp.stack([me, section]), attn_qkv[0], attn_out[0], cross_proj[0], ffn_in[0], ffn_out[0], gains[0]
    )
    came = swap(sent)
    enc, dec = jnp.where(section == 0, kept, came), jnp.where(section == 0, came, kept)
    mid_pack = jnp.concatenate([enc[FIRST:], dec[FIRST : FIRST + 32]], axis=0)
    tail_pack = dec[FIRST + 32 :]
    enc, dec = enc[:FIRST], dec[:FIRST]
    enc = spread_line(enc)
    (dec, mid_pack, later), enc = tie((dec, mid_pack, later), enc)
    came = [jump(mid_pack, i) for i in (1, 2, 3)]
    enc, dec = tie(spread_plane(enc, 2), spread_line(dec))
    (enc, tail_pack), (dec, mid_pack) = tie(
        (spread_plane(enc, 3), tail_pack), (spread_plane(dec, 2), jnp.stack([mid_pack] + came))
    )
    enc = (enc, swap(enc))
    dec = (dec, hop(dec, 3))
    mid_pack = (mid_pack, hop(mid_pack, 2))
    tail_pack = (tail_pack, [jump(tail_pack, i) for i in (1, 2, 3)])
    shift = jnp.asarray(SHIFT)
    table = jnp.stack([shift[section] ^ me, shift[1 - section] ^ me, jnp.full((BLOCKS,), section, jnp.int32)])
    where = jnp.asarray(WHERE)[:, jnp.arange(BLOCKS, dtype=jnp.int32) ^ me]
    halves = jnp.where(jnp.arange(BLOCKS) == section, 0, 1).astype(jnp.int32)
    return later, enc, dec, mid_pack, tail_pack, table, jnp.concatenate([where, halves[None]])


def weights_far(attn_qkv, attn_out, cross_proj, ffn_in, ffn_out, gains, later):
    def whole(shard, axis):
        return lax.all_gather(shard[0], "dp", axis=axis, tiled=True)

    qkv, out, cross, inner, down, gain = (
        whole(w, a) for w, a in ((attn_qkv, 0), (attn_out, 0), (cross_proj, 0), (ffn_in, 1), (ffn_out, 0), (gains, 1))
    )
    width = out.shape[1]
    gain_rows = jnp.zeros((BLOCKS, 16, width), BF16).at[0, : gain.shape[0]].set(gain)
    section = lax.axis_index("section")
    shards = (
        qkv.reshape(BLOCKS, -1, 3 * width),
        out.reshape(BLOCKS, -1, width),
        cross.reshape(BLOCKS, -1, 2 * width),
        inner.reshape(width, BLOCKS, -1).transpose(1, 0, 2),
        down.reshape(BLOCKS, -1, width),
        gain_rows,
    )
    pack = lax.cond(
        section == 0,
        lambda *args: jax.vmap(functools.partial(pack_plain, 0), out_axes=1)(*args),
        lambda *args: jax.vmap(functools.partial(pack_plain, 1), out_axes=1)(*args),
        *shards,
    )
    came = swap(pack)
    enc, dec = jnp.where(section == 0, pack, came), jnp.where(section == 0, came, pack)
    mid_pack = jnp.concatenate([enc[:, :, FIRST:], dec[:, :, FIRST : FIRST + 32]], axis=2)
    tail_pack = dec[:, :, FIRST + 32 :]
    enc, dec = enc[:, :, :FIRST], dec[:, :, :FIRST]
    plain = jnp.arange(BLOCKS, dtype=jnp.int32)
    table = jnp.stack([plain, plain, jnp.zeros_like(plain)])
    halves = jnp.where(plain == 0, 0, 1).astype(jnp.int32)
    return later, (enc[0], enc[1]), (dec[0], dec[1]), ([mid_pack[0]], [mid_pack[1]]), ([tail_pack[0]], [tail_pack[1]]), table, jnp.stack([plain, plain, halves])


def far_shards(tail_pack, mid_pack, front_pack):
    tail_pack, mid_pack, front_pack = (jnp.stack(p) for p in (tail_pack, mid_pack, front_pack))

    def qkv_of(pack):
        return jnp.concatenate([pack[:, 32 * i : 32 * i + 32].reshape(-1, pack.shape[2]) for i in range(3)], axis=1)
    def rows(pack, start, count):
        part = pack[:, :, start : start + count]
        return part.transpose(1, 0, 2, 3).reshape(-1, part.shape[-1])

    def inner(pack, start):
        blocks = jax.vmap(lambda a, b: inner_of([a, b]))(pack[0, :, start : start + 64], pack[1, :, start : start + 64])
        return blocks.transpose(1, 0, 2).reshape(blocks.shape[1], -1)

    def side(pack, *starts):
        return jnp.concatenate([rows(pack, s, 16) for s in starts], axis=1)

    enc = (qkv_of(front_pack[0]), rows(mid_pack, 160, 16), side(mid_pack, 0, 16), inner(mid_pack, 96), rows(mid_pack, 32, 64))
    cross_d = jnp.concatenate([rows(mid_pack, 176, 16), rows(tail_pack, 128, 16)], axis=1)
    dec = (qkv_of(front_pack[1]), rows(mid_pack, 192, 16), cross_d, inner(tail_pack, 64), rows(tail_pack, 0, 64))
    section = lax.axis_index("section")
    grads = []
    for a, b, axis in zip(enc, dec, (0, 0, 0, 1, 0)):
        mine = jnp.where(section == 0, a, b).astype(F32) + swap(jnp.where(section == 0, b, a)).astype(F32)
        grads.append(lax.psum_scatter(mine, "dp", scatter_dimension=axis, tiled=True))
    extra = lax.psum(front_pack[0, 0, 96:112].astype(F32), ("section", "dp"))
    return tuple(grads), extra


def gain_grads(weights, grads, gains, extra):
    section = lax.axis_index("section")
    qkv, cross = (w[0].astype(F32) * g for w, g in zip(weights, grads))
    gain = gains[0].astype(F32)
    columns = gain.shape[1]
    start = lax.axis_index("dp") * columns
    split = lax.dynamic_slice(extra, (section, start), (1, columns))[0]
    half = cross.shape[1] // 2
    reach = jnp.sum(cross[:, :half], axis=1)
    memory = (reach + jnp.sum(cross[:, half:], axis=1)) / gain[2]
    first = jnp.sum(qkv, axis=1) / gain[0]
    enc, dec = jnp.stack([first, split, memory]), jnp.stack([first, reach / gain[1], split])
    return jnp.where(section == 0, enc, dec)


def new_places(lengths, starts, rows):
    ends = jnp.cumsum(lengths)
    places = jnp.arange(rows, dtype=jnp.int32)
    pick = (places[:, None] >= (ends - lengths)[None, :]) & (places[:, None] < ends[None, :])
    return (places + jnp.sum(jnp.where(pick, (starts - ends + lengths)[None, :], 0), axis=1))[None]


def local(
    layer_input, cotangent, lengths, attn_qkv, attn_out, cross_proj, ffn_in, ffn_out, gains, alpha_raw
):
    section = lax.axis_index("section")
    near = lax.axis_size("dp") == BLOCKS
    weights = weights_near if near else weights_far
    later = (layer_input, cotangent, lengths, alpha_raw)
    later, first_e, first_d, mid_pack, tail_pack, table, place = weights(
        attn_qkv, attn_out, cross_proj, ffn_in, ffn_out, gains, later
    )
    layer_input, cotangent, lengths, alpha_raw = later
    rows, width = layer_input.shape[3:]
    inputs = layer_input[0, :, 0]
    came = swap(lax.dynamic_index_in_dim(inputs, 1 - section, 0, keepdims=False))
    first = section == 0
    source, target = lax.dynamic_index_in_dim(lengths[:, :, 0], section, 1, keepdims=False)
    large_e, large_d = source == jnp.max(source), target == jnp.max(target)
    starts_e = starts_of(source, jnp.where(large_e, 0, jnp.where(large_d, 2, 1)))
    starts_d = starts_of(target, jnp.where(large_d, 0, jnp.where(large_e, 1, 2)))
    dest_e, dest_d = new_places(source, starts_e, rows), new_places(target, starts_d, rows)
    x_e, x_d, ct = sort_rows(section[None], inputs, came, cotangent[:, 0], dest_e, dest_d)
    head_width = width // alpha_raw.shape[1]
    gate = jax.nn.sigmoid(alpha_raw)
    coef = [coefs_of(0.25 + 0.25 * gate[i], head_width) for i in range(3)]
    marks_e = marks_of(starts_e, source, starts_e, source, rows, False)
    marks_d = marks_of(starts_d, target, starts_d, target, rows, True)
    marks_c = marks_of(starts_d, target, starts_e, source, rows, False)

    def by_micro(kept, came):
        return jnp.stack([jnp.where(first, kept, came), jnp.where(first, came, kept)])[None, :, None]

    def settle(enc, dec):
        return by_micro(jnp.where(first, enc, dec), swap(jnp.where(first, dec, enc)))

    n_e, (q_now, q_e), (k_now, k_e), (v_now, v_e), g_e = front(table, x_e, *first_e)
    if near:
        (dec, dec_came), (mid_0, mid_1), (block, came) = first_d, mid_pack, tail_pack
        (dec, mid_1, block), q_now = tie((dec, mid_1, block), q_now)
        (q_now, mid_0, mid_1), (dec, tail_0) = tie(
            (q_now, mid_0, mid_1), (jnp.concatenate([dec, dec_came], axis=0), jnp.stack([block] + came))
        )
        mid_2, mid_3, other_0, other_1 = hop(mid_0, 3), hop(mid_1, 3), swap(mid_0), swap(mid_1)
        first_d = (dec, swap(dec))
    a_e, *stats_e = attend(q_now, k_now, v_now, marks_e, coef[0])
    if near:
        (mid_2, mid_3, other_0, other_1, first_d), a_e = tie((mid_2, mid_3, other_0, other_1, first_d), a_e)
        (x_d, tail_0, mid_2, mid_3), (other_0, other_1, first_d) = tie(
            (x_d, tail_0, mid_2, mid_3), (other_0, other_1, first_d)
        )
        tail_1, other_tail_0 = hop(tail_0, 2), swap(tail_0)
        other_2, other_3 = swap(mid_2), swap(mid_3)
    n_d, (q_now, q_d), (k_now, k_d), (v_now, v_d), g_d = front(table, x_d, *first_d)
    a_d, *stats_d = attend(q_now, k_now, v_now, marks_d, coef[1])
    if near:
        (tail_1, other_tail_0, other_2, other_3), a_d = tie((tail_1, other_tail_0, other_2, other_3), a_d)
        (a_d, tail_0, tail_1), (other_tail_0, other_2, other_3) = tie(
            (a_d, tail_0, tail_1), (other_tail_0, other_2, other_3)
        )
        mid_pack = ([mid_0, mid_1, mid_2, mid_3], [other_0, other_1, other_2, other_3])
        tail_2, tail_3, other_tail_1 = hop(tail_0, 3), hop(tail_1, 3), swap(tail_1)
    m_e, n1_e, act, slope, end, memory, (mk_now, mem_k), (mv_now, mem_v), m_d, n1_d, (query_now, query), memory_out = mid(
        table, a_e, a_d, x_e, x_d, g_e, g_d, dest_e, *mid_pack
    )
    crossed, *stats_c = attend(query_now, mk_now, mv_now, marks_c, coef[2])
    if near:
        (tail_2, tail_3, other_tail_1), crossed = tie((tail_2, tail_3, other_tail_1), crossed)
        tail_pack = ([tail_0, tail_1, tail_2, tail_3], [other_tail_0, other_tail_1, swap(tail_2), swap(tail_3)])
    stay, leave, second_grad, crossed_grad, gd_two, kept, sent = tail(
        place, section[None], table, crossed, m_d, ct, g_d, dest_d, memory_out, *tail_pack
    )
    pack_a = (kept, sent)
    if near:
        a = [kept, swap(sent)]
    arrived = swap(leave)
    query_grad, mk_grad, mv_grad, ds_c = attend_back(query, mem_k, mem_v, crossed_grad, stats_c, marks_c, coef[2])
    if near:
        query_grad = behind(query_grad, a)
        query_grad, (sent_a, arrived) = tie(query_grad, (total(a, 8, 16), arrived))
        a.append(hop(sent_a, 3))
    md_grad, ad_grad, me_grad, ae_grad, ge_one, kept, sent = mid_back(
        place, table, query_grad, mk_grad, mv_grad, n1_d, m_d, second_grad, a_d, memory, end, act, slope, n1_e, m_e, a_e, g_e, g_d,
        *mid_pack
    )
    pack_b = (kept, sent)
    if near:
        ad_grad = behind(ad_grad, a)
        (ad_grad, sent), sent_a = tie((ad_grad, sent), total(a, 4, 8))
        a.append(hop(sent_a, 2))
        b = [kept, swap(sent)]
    *grads_d, ds_d = attend_back(q_d, k_d, v_d, ad_grad, stats_d, marks_d, coef[1])
    if near:
        grads_d[0] = behind(grads_d[0], a, b)
        ae_grad, (sent_a, sent_b, grads_d[0]) = tie(ae_grad, (total(a, 2, 4), total(b, 8, 16), grads_d[0]))
        a.append(hop(sent_a, 1))
        b.append(hop(sent_b, 3))
    *grads_e, ds_e = attend_back(q_e, k_e, v_e, ae_grad, stats_e, marks_e, coef[0])
    if near:
        grads_e[0] = behind(grads_e[0], a, b)
        (grads_e[0], md_grad), (sent_a, sent_b) = tie((grads_e[0], md_grad), (total(a, 1, 2), total(b, 4, 8)))
        a.append(hop(sent_a, 0))
        b.append(hop(sent_b, 2))
    kept, sent = front_w(place, grads_e, grads_d, n_e, n_d, ge_one, gd_two, (ds_e, ds_d, ds_c))
    if near:
        sent = behind(sent, a, b)
        sent, (sent_b, done_a) = tie(sent, (to_line(b), at_last(a, [])))
        c = [kept, swap(sent)]
        came_b = along_line(sent_b)
        (md_grad, me_grad), sent_c = tie((md_grad, me_grad), total(c, 8, 16))
        c.append(hop(sent_c, 3))
    xd_grad = front_x(table, grads_d, x_d, md_grad, g_d, dest_d, *first_d)
    xe_grad = front_x(table, grads_e, x_e, me_grad, g_e, dest_e, *first_e)
    if near:
        outputs = by_micro(stay, arrived)
        xd_grad, xe_grad, outputs = behind((xd_grad, xe_grad, outputs), b, c)
        sent_c, (xe_grad, done_b) = tie(total(c, 4, 8), (xe_grad, at_last(b, came_b)))
        c.append(hop(sent_c, 2))
        input_grad = settle(xe_grad, xd_grad)
        enc, dec = low(done_b[0:176]), low(jnp.concatenate([done_a, done_b[176:208]], axis=0))
        parts = (jnp.where(first, enc, dec), swap(jnp.where(first, dec, enc)))
        (parts, input_grad) = behind((parts, input_grad), c)
        *grads, alpha_grad = finish(
            jnp.stack([lax.axis_index("dp"), section]), *parts, at_last(c, along_line(to_line(c))),
            attn_qkv[0], cross_proj[0], gains[0], 0.25 * gate * (1.0 - gate),
        )
    else:
        input_grad, outputs = settle(xe_grad, xd_grad), by_micro(stay, arrived)
        grads, extra = far_shards(pack_a, pack_b, (kept, sent))
        grads += (gain_grads((attn_qkv, cross_proj), (grads[0], grads[2]), gains, extra),)
        alpha_grad = extra[8:16, 0:3].T * 0.25 * gate * (1.0 - gate)
    return (outputs, input_grad) + tuple(g[None] for g in grads) + (alpha_grad,)


def solution(mesh):
    return jax.shard_map(
        local,
        mesh=mesh,
        in_specs=(
            P("section", None, "dp", None, None),
            P(None, "dp", None, None),
            P(None, None, "dp", None),
            P("section", "dp", None),
            P("section", "dp", None),
            P("section", "dp", None),
            P("section", None, "dp"),
            P("section", "dp", None),
            P("section", None, "dp"),
            P(),
        ),
        out_specs=(
            P("section", None, "dp", None, None),
            P("section", None, "dp", None, None),
            P("section", "dp", None),
            P("section", "dp", None),
            P("section", "dp", None),
            P("section", None, "dp"),
            P("section", "dp", None),
            P("section", None, "dp"),
            P(),
        ),
        check_vma=False,
    )
```

```python
import functools
import math

import jax
import jax.numpy as jnp
import numpy as np
from jax import lax
from jax.experimental import pallas as pl
from jax.experimental.pallas import tpu as pltpu
from jax.sharding import PartitionSpec as P

SHARP = 0.0625
NEG = -1e9
EPS = 1e-5
TINY = 1e-37
LOG2E = 1.4426950408889634
PART = 256
CHUNK = 128
TILE = 128
BLOCKS = 16
MB = 1 << 20
COST = 1000
LIMIT = 52 * MB
F32, BF16 = jnp.float32, jnp.bfloat16
WHOLE = pl.BlockSpec(memory_space=pltpu.VMEM)
TABLE = pl.BlockSpec(memory_space=pltpu.SMEM)
AWAY = pl.BlockSpec(memory_space=pl.ANY)


def mm(a, b):
    return jnp.dot(a, b, preferred_element_type=F32)


def mm_nt(a, b):
    return lax.dot_general(a, b, (((1,), (1,)), ((), ())), preferred_element_type=F32)


def mm_tn(a, b):
    return lax.dot_general(a, b, (((0,), (0,)), ((), ())), preferred_element_type=F32)


def low(v):
    return v.astype(BF16)


class Moves:
    def __init__(self, pairs_in, pairs_out, sems):
        self.copies = {}
        for i, (src, dst) in enumerate(pairs_in):
            self.copies[id(dst)] = pltpu.make_async_copy(src, dst, sems.at[i])
            self.copies[id(dst)].start()
        self.outs = {
            id(src): pltpu.make_async_copy(src, dst, sems.at[len(pairs_in) + i])
            for i, (src, dst) in enumerate(pairs_out)
        }
        self.left = []

    def ready(self, *refs):
        for ref in refs:
            copy = self.copies.pop(id(ref), None)
            if copy is not None:
                copy.wait()

    def done(self, *refs):
        for ref in refs:
            copy = self.outs.pop(id(ref), None)
            if copy is not None:
                copy.start()
                self.left.append(copy)

    def finish(self):
        assert not self.copies and not self.outs
        for copy in self.left:
            copy.wait()


class Near:
    def __init__(self, array):
        self.array = array


class Both(Near):
    pass


def call_dense(body, name, us, tables, ins, far, outs, far_outs, scratch):
    near_in = [isinstance(a, Near) for a in ins]
    near_out = [isinstance(a, Near) for a in outs]
    away_out = [not isinstance(a, Near) or isinstance(a, Both) for a in outs]
    ins = [a.array if isinstance(a, Near) else a for a in ins]
    outs = [a.array if isinstance(a, Near) else a for a in outs]
    bufs_in = [a for a, near in zip(ins, near_in) if not near]
    bufs_out = [a for a, near in zip(outs, near_out) if not near]
    lone = [a for a, near in zip(outs, near_out) if near]
    sent = [a for a, away in zip(outs, away_out) if away]
    counts = [len(g) for g in (tables, ins, far, lone, sent, far_outs, bufs_in, bufs_out)]

    def kernel(*refs):
        groups, at = [], 0
        for count in counts:
            groups.append(list(refs[at : at + count]))
            at += count
        table_refs, in_refs, far_refs, lone_refs, sent_refs, far_out_refs, in_bufs, out_bufs = groups
        in_local = [ref if near else in_bufs.pop(0) for ref, near in zip(in_refs, near_in)]
        out_local = [lone_refs.pop(0) if near else out_bufs.pop(0) for near in near_out]
        pairs_in = [(ref, buf) for ref, buf, near in zip(in_refs, in_local, near_in) if not near]
        pairs_out = [(buf, sent_refs.pop(0)) for buf, away in zip(out_local, away_out) if away]
        moves = Moves(pairs_in, pairs_out, refs[at])
        body(moves, *table_refs, *in_local, *far_refs, *out_local, *far_out_refs, *refs[at + 1 :])
        moves.finish()

    got = pl.pallas_call(
        kernel,
        in_specs=[TABLE] * len(tables) + [WHOLE if near else AWAY for near in near_in] + [AWAY] * len(far),
        out_specs=[WHOLE] * len(lone) + [AWAY] * (len(sent) + len(far_outs)),
        out_shape=[*lone, *sent, *far_outs],
        scratch_shapes=[pltpu.VMEM(a.shape, a.dtype) for a in (*bufs_in, *bufs_out)]
        + [pltpu.SemaphoreType.DMA((max(1, len(bufs_in) + len(sent)),)), *scratch],
        compiler_params=pltpu.CompilerParams(vmem_limit_bytes=LIMIT),
        cost_estimate=pl.CostEstimate(flops=us * COST, transcendentals=0, bytes_accessed=us * COST // 400),
        name=name,
    )(*tables, *ins, *far)
    lone_got, sent_got = list(got[: len(lone)]), list(got[len(lone) : len(lone) + len(sent)])
    result = []
    for near, away in zip(near_out, away_out):
        pair = (lone_got.pop(0) if near else None, sent_got.pop(0) if away else None)
        result.append(pair if near and away else pair[0] if near else pair[1])
    return result + list(got[len(lone) + len(sent) :])


def fold(block):
    return jnp.sum(block.reshape(block.shape[0] // 8, 8, block.shape[1]), axis=0)


def fold_max(block):
    return jnp.max(block.reshape(block.shape[0] // 8, 8, block.shape[1]), axis=0)


def rows_of(parts, op):
    return jnp.concatenate([op(part, axis=0, keepdims=True) for part in parts], axis=0)


def per_head(coef, which, heads):
    place = lax.broadcasted_iota(jnp.int32, (heads, TILE), 0)
    out = jnp.zeros((heads, TILE), F32)
    for h in range(heads):
        out = jnp.where(place == h, coef[which, h], out)
    return out


def bias_of(lo, hi, start):
    place = lax.broadcasted_iota(jnp.int32, (CHUNK, TILE), 0) + start
    return jnp.where(jnp.logical_and(place >= lo, place < hi), 0.0, NEG)


def pair_of(h, width):
    return slice(h // 2 * 2 * width, (h // 2 + 1) * 2 * width)


def split_pairs(dst, turned, heads, width):
    for h in range(heads):
        block = turned[pair_of(h, width), :]
        mine = lax.broadcasted_iota(jnp.int32, block.shape, 0) // width == h % 2
        dst[h] = jnp.where(mine, block, jnp.zeros_like(block))


def fold(block):
    return jnp.sum(block.reshape(block.shape[0] // 8, 8, block.shape[1]), axis=0)


def fold_max(block):
    return jnp.max(block.reshape(block.shape[0] // 8, 8, block.shape[1]), axis=0)


def rows_of(parts, op):
    return jnp.concatenate([op(part, axis=0, keepdims=True) for part in parts], axis=0)


def per_head(coef, which, heads):
    place = lax.broadcasted_iota(jnp.int32, (heads, TILE), 0)
    out = jnp.zeros((heads, TILE), F32)
    for h in range(heads):
        out = jnp.where(place == h, coef[which, h], out)
    return out


def bias_of(lo, hi, start):
    place = lax.broadcasted_iota(jnp.int32, (CHUNK, TILE), 0) + start
    return jnp.where(jnp.logical_and(place >= lo, place < hi), 0.0, NEG)


def pair_of(h, width):
    return slice(h // 2 * 2 * width, (h // 2 + 1) * 2 * width)


def chunk_at(c):
    return pl.ds(pl.multiple_of(c * CHUNK, CHUNK), CHUNK)


def split_pairs(dst, turned, heads, width):
    for h in range(heads):
        block = turned[pair_of(h, width), :]
        mine = lax.broadcasted_iota(jnp.int32, block.shape, 0) // width == h % 2
        dst[h] = jnp.where(mine, block, jnp.zeros_like(block))


def clear_outside(first, last, keys, refs, cols):
    def blank(c, carry):
        for ref in refs:
            for h in range(ref.shape[0]):
                ref[h, chunk_at(c), cols] = jnp.zeros((CHUNK, TILE), BF16)
        return carry

    lax.fori_loop(0, first, blank, 0)
    lax.fori_loop(last, keys // CHUNK, blank, 0)


def meets(first, last, half):
    per = PART // CHUNK
    return jnp.logical_and(first < (half + 1) * per, last > half * per)


def attend_kernel(
    span, coef, lo_ref, hi_ref, q_ref, k_ref, v_ref, o_ref, tau_ref, top_ref, inv_ref, v_t, zs, ps, qz, o_t
):
    heads, keys = zs.shape[0], zs.shape[1]
    width = q_ref.shape[1] // heads
    tile = pl.program_id(0)

    @pl.when(tile == 0)
    def _():
        v_t[...] = v_ref[...].T

    split_pairs(qz, q_ref[...].T, heads, width)
    lo, hi = lo_ref[...], hi_ref[...]
    first, last = span[0, tile], span[1, tile]

    def scores(c, tops):
        here = chunk_at(c)
        bias = bias_of(lo, hi, c * CHUNK)
        out = []
        for h in range(heads):
            z = mm(k_ref[here, pair_of(h, width)], qz[h]) * coef[0, h] + bias
            zs[h, here, :] = z
            out.append(jnp.maximum(tops[h], fold_max(z)))
        return tuple(out)

    tops = lax.fori_loop(
        first, last, scores, tuple(jnp.full((8, TILE), -3e38, F32) for _ in range(heads))
    )
    peak = rows_of(tops, jnp.max)
    shrink, exponent = per_head(coef, 1, heads), per_head(coef, 4, heads)
    least = peak - 1.0
    most = peak - jnp.exp2(-shrink * jnp.log2((hi - lo).astype(F32)))
    close = 4e-6 + 5e-7 * jnp.abs(peak)
    zero = tuple(jnp.zeros((8, TILE), F32) for _ in range(3 * heads))

    def search(state):
        turn, tau, _ = state

        def body(c, sums):
            here = chunk_at(c)
            out = []
            for h in range(heads):
                u = jnp.maximum(zs[h, here, :] - tau[h : h + 1, :], TINY)
                curve = jnp.exp2(jnp.log2(u) * coef[3, h])
                slope = curve * u
                out += [sums[3 * h] + fold(slope * u), sums[3 * h + 1] + fold(slope), sums[3 * h + 2] + fold(curve)]
            return tuple(out)

        sums = lax.fori_loop(first, last, body, zero)
        mass, slope, curve = (rows_of(sums[i::3], jnp.sum) for i in range(3))
        bend = jnp.clip(1.0 - (exponent - 1.0) * curve * mass / (exponent * slope * slope), 0.0, 1.0)
        bend = jnp.where(turn < 5, bend, shrink)
        log_mass = jnp.log(mass)
        x = bend * log_mass
        rise = jnp.where(
            jnp.abs(x) < 0.1,
            log_mass * (1.0 - x * (0.5 - x * (1.0 / 6.0))),
            (1.0 - jnp.exp(-x)) / jnp.maximum(bend, 1e-6),
        )
        new = jnp.clip(tau + mass / (exponent * slope) * rise, least, most)
        return turn + 1, new, jnp.max(jnp.abs(new - tau))

    def finish(state):
        turn, tau, _, _, _ = state
        turn, tau, _ = lax.while_loop(
            lambda s: jnp.logical_and(s[2] > 6e-3, s[0] < 40), search, (turn, tau, jnp.float32(1.0))
        )

        def final(c, sums):
            here = chunk_at(c)
            out = []
            for h in range(heads):
                z = zs[h, here, :]
                u = jnp.maximum(z - tau[h : h + 1, :], TINY)
                slope = jnp.exp2(jnp.log2(u) * coef[2, h])
                p = slope * u
                ps[h, here, :] = low(p)
                soft = jnp.exp2((z - peak[h : h + 1, :]) * (LOG2E / SHARP))
                out += [sums[3 * h] + fold(p), sums[3 * h + 1] + fold(slope), sums[3 * h + 2] + fold(soft)]
            return tuple(out)

        sums = lax.fori_loop(first, last, final, zero)
        mass, slope, soft = (rows_of(sums[i::3], jnp.sum) for i in range(3))
        off = (mass - 1.0) / (exponent * slope)
        open_ = jnp.max(jnp.where(jnp.abs(off) > close, 1.0, 0.0))
        return turn, jnp.where(open_ > 0.0, jnp.clip(tau + off, least, most), tau), open_, mass, soft

    blank = jnp.ones((heads, TILE), F32)
    _, tau, _, mass, soft = lax.while_loop(
        lambda s: jnp.logical_and(s[2] > 0.0, s[0] < 40), finish, (0, least, jnp.float32(1.0), blank, blank)
    )
    inv = 1.0 / mass
    tau_ref[...] = tau
    top_ref[...] = peak + SHARP * jnp.log(soft)
    inv_ref[...] = inv
    clear_outside(first, last, keys, (ps,), slice(None))
    o_t[...] = jnp.zeros_like(o_t)
    for half in range(keys // PART):
        cols = slice(half * PART, (half + 1) * PART)

        @pl.when(meets(first, last, half))
        def _():
            for h in range(heads):
                rows = slice(h * width, (h + 1) * width)
                o_t[rows, :] += mm(v_t[rows, cols], ps[h, cols, :])

    for h in range(0, heads, 2):
        got = [o_t[i * width : (i + 1) * width, :] * inv[i : i + 1, :] for i in (h, h + 1)]
        o_ref[:, pair_of(h, width)] = low(jnp.concatenate(got, axis=0).T)


def attend(q, k, v, marks, coef):
    lo, hi, span = marks
    rows, width = q.shape
    keys, heads = k.shape[0], coef.shape[1]
    line = pl.BlockSpec((1, TILE), lambda t, *_: (0, t))
    tile = pl.BlockSpec((TILE, width), lambda t, *_: (t, 0))
    stat = pl.BlockSpec((heads, TILE), lambda t, *_: (0, t))
    full = pl.BlockSpec((keys, width), lambda t, *_: (0, 0))
    return pl.pallas_call(
        attend_kernel,
        grid_spec=pltpu.PrefetchScalarGridSpec(
            num_scalar_prefetch=2,
            grid=(rows // TILE,),
            in_specs=[line, line, tile, full, full],
            out_specs=[tile, stat, stat, stat],
            scratch_shapes=[
                pltpu.VMEM((width, keys), BF16),
                pltpu.VMEM((heads, keys, TILE), F32),
                pltpu.VMEM((heads, keys, TILE), BF16),
                pltpu.VMEM((heads, 2 * width // heads, TILE), BF16),
                pltpu.VMEM((width, TILE), F32),
            ],
        ),
        out_shape=[jax.ShapeDtypeStruct((rows, width), BF16)]
        + [jax.ShapeDtypeStruct((heads, rows), F32)] * 3,
        compiler_params=pltpu.CompilerParams(vmem_limit_bytes=24 * MB),
        cost_estimate=pl.CostEstimate(flops=14 * COST, transcendentals=0, bytes_accessed=14 * COST // 400),
        name="attend",
    )(span, coef, lo, hi, q, k, v)


def attend_back_kernel(
    span, coef, lo_ref, hi_ref, q_ref, go_ref, tau_ref, top_ref, inv_ref, q_all, go_all, k_ref, v_ref,
    dq_ref, dk_ref, dv_ref, ds_ref, k_t, zs, gs, ls, qz, gz, g_all, p_all, dq_t, dk_sum, dv_sum,
):
    heads, keys = zs.shape[0], zs.shape[1]
    width = q_ref.shape[1] // heads
    scale = 1.0 / math.sqrt(width)
    tile = pl.program_id(0)
    at = pl.ds(pl.multiple_of(tile * TILE, TILE), TILE)

    @pl.when(tile == 0)
    def _():
        k_t[...] = k_ref[...].T
        ds_ref[...] = jnp.zeros_like(ds_ref)

    split_pairs(qz, q_ref[...].T, heads, width)
    split_pairs(gz, go_ref[...].T, heads, width)
    lo, hi = lo_ref[...], hi_ref[...]
    tau, top, inv = tau_ref[...], top_ref[...], inv_ref[...]
    first, last = span[0, tile], span[1, tile]
    kinds = 5
    zero = tuple(jnp.zeros((8, TILE), F32) for _ in range(kinds * heads))

    def gather(c, sums):
        here = chunk_at(c)
        bias = bias_of(lo, hi, c * CHUNK)
        out = []
        for h in range(heads):
            z = mm(k_ref[here, pair_of(h, width)], qz[h]) * coef[0, h] + bias
            g = mm(v_ref[here, pair_of(h, width)], gz[h])
            u = jnp.maximum(z - tau[h : h + 1, :], TINY)
            log_u = jnp.log2(u)
            slope = jnp.exp2(log_u * coef[2, h])
            p = slope * u
            p_log = p * log_u
            zs[h, here, :] = z
            gs[h, here, :] = g
            ls[h, here, :] = slope
            new = (g * p, g * slope, slope, g * p_log, p_log)
            out += [sums[kinds * h + i] + fold(new[i]) for i in range(kinds)]
        return tuple(out)

    sums = lax.fori_loop(first, last, gather, zero)
    gp, gl, ll, gpl, pl_sum = (rows_of(sums[i::kinds], jnp.sum) for i in range(kinds))
    shrink = per_head(coef, 1, heads)
    inv_k = per_head(coef, 4, heads) * inv
    mean = gp * inv
    drop = inv_k * (gl - mean * ll)
    grad_k = inv * (gpl - mean * pl_sum) * (1.0 / LOG2E)
    clear_outside(first, last, keys, (g_all, p_all), at)

    def final(c, sums):
        here = chunk_at(c)
        out = []
        for h in range(heads):
            one = slice(h, h + 1)
            z, slope = zs[h, here, :], ls[h, here, :]
            p = slope * jnp.maximum(z - tau[one], TINY)
            r = (gs[h, here, :] - mean[one]) * slope * inv_k[one]
            g_z = r - drop[one] * jnp.exp2((z - top[one]) * (LOG2E / SHARP))
            g_all[h, here, at] = low(g_z * coef[1, h])
            p_all[h, here, at] = low(p * inv[one])
            out.append(sums[h] + fold(g_z * z))
        return tuple(out)

    sums = lax.fori_loop(first, last, final, zero[:heads])
    ds_ref[...] += rows_of(sums, jnp.sum) / shrink - grad_k / (shrink * shrink)
    dq_t[...] = jnp.zeros_like(dq_t)
    for half in range(keys // PART):
        cols = slice(half * PART, (half + 1) * PART)

        @pl.when(meets(first, last, half))
        def _():
            for h in range(heads):
                rows = slice(h * width, (h + 1) * width)
                dq_t[rows, :] += mm(k_t[rows, cols], g_all[h, cols, at])

    for h in range(0, heads, 2):
        dq_ref[:, pair_of(h, width)] = low(dq_t[pair_of(h, width), :].T * scale)

    @pl.when(tile == pl.num_programs(0) - 1)
    def _():
        dk_sum[...] = jnp.zeros_like(dk_sum)
        dv_sum[...] = jnp.zeros_like(dv_sum)
        tiles = PART // TILE
        lane = lax.broadcasted_iota(jnp.int32, (PART, 2 * width), 1) // width
        blank_rows = jnp.zeros((PART, 2 * width), BF16)
        for q_half in range(q_all.shape[0] // PART):
            rows = slice(q_half * PART, (q_half + 1) * PART)
            for half in range(keys // PART):
                cols = slice(half * PART, (half + 1) * PART)
                reach = [
                    meets(span[0, t], span[1, t], half) for t in range(q_half * tiles, (q_half + 1) * tiles)
                ]

                @pl.when(functools.reduce(jnp.logical_or, reach))
                def _():
                    for h in range(0, heads, 2):
                        pair = pair_of(h, width)
                        for i in (h, h + 1):
                            mine = lane == i % 2
                            dk_sum[cols, pair] += mm(g_all[i, cols, rows], jnp.where(mine, q_all[rows, pair], blank_rows))
                            dv_sum[cols, pair] += mm(p_all[i, cols, rows], jnp.where(mine, go_all[rows, pair], blank_rows))

        dk_ref[...] = low(dk_sum[...] * scale)
        dv_ref[...] = low(dv_sum[...])


def attend_back(q, k, v, go, stats, marks, coef):
    lo, hi, span = marks
    rows, width = q.shape
    keys, heads = k.shape[0], coef.shape[1]
    line = pl.BlockSpec((1, TILE), lambda t, *_: (0, t))
    tile = pl.BlockSpec((TILE, width), lambda t, *_: (t, 0))
    stat = pl.BlockSpec((heads, TILE), lambda t, *_: (0, t))
    q_full = pl.BlockSpec((rows, width), lambda t, *_: (0, 0))
    k_full = pl.BlockSpec((keys, width), lambda t, *_: (0, 0))
    return pl.pallas_call(
        attend_back_kernel,
        grid_spec=pltpu.PrefetchScalarGridSpec(
            num_scalar_prefetch=2,
            grid=(rows // TILE,),
            in_specs=[line, line, tile, tile, stat, stat, stat, q_full, q_full, k_full, k_full],
            out_specs=[tile, k_full, k_full, pl.BlockSpec((heads, TILE), lambda t, *_: (0, 0))],
            scratch_shapes=[pltpu.VMEM((width, keys), BF16)]
            + [pltpu.VMEM((heads, keys, TILE), F32)] * 3
            + [pltpu.VMEM((heads, 2 * width // heads, TILE), BF16)] * 2
            + [pltpu.VMEM((heads, keys, rows), BF16)] * 2
            + [pltpu.VMEM((width, TILE), F32)]
            + [pltpu.VMEM((keys, width), F32)] * 2,
        ),
        out_shape=[
            jax.ShapeDtypeStruct((rows, width), BF16),
            jax.ShapeDtypeStruct((keys, width), BF16),
            jax.ShapeDtypeStruct((keys, width), BF16),
            jax.ShapeDtypeStruct((heads, TILE), F32),
        ],
        compiler_params=pltpu.CompilerParams(vmem_limit_bytes=36 * MB),
        cost_estimate=pl.CostEstimate(flops=14 * COST, transcendentals=0, bytes_accessed=14 * COST // 400),
        name="attend_back",
    )(span, coef, lo, hi, q, go, *stats, q, go, k, v)


def starts_of(lengths, rank):
    number = jnp.arange(lengths.shape[0])
    before = rank[None, :] < rank[:, None]
    before |= (rank[None, :] == rank[:, None]) & (number[None, :] < number[:, None])
    return jnp.sum(jnp.where(before, lengths[None, :], 0), axis=1)


def marks_of(q_starts, q_lengths, k_starts, k_lengths, rows, causal):
    places = jnp.arange(rows, dtype=jnp.int32)
    pick = (places[:, None] >= q_starts[None, :]) & (places[:, None] < (q_starts + q_lengths)[None, :])
    lo = jnp.sum(jnp.where(pick, k_starts[None, :], 0), axis=1)
    hi = jnp.sum(jnp.where(pick, (k_starts + k_lengths)[None, :], 0), axis=1)
    if causal:
        hi = jnp.minimum(hi, places + 1)
    first = jnp.min(lo.reshape(-1, TILE), axis=1) // CHUNK
    last = (jnp.max(hi.reshape(-1, TILE), axis=1) + CHUNK - 1) // CHUNK
    return (lo[None], hi[None], jnp.stack([first, last]))


def coefs_of(shrink, width):
    exponent = 1.0 / shrink
    return jnp.stack([shrink / math.sqrt(width), shrink, exponent - 1.0, exponent - 2.0, exponent])


GAIN, FIRST, MID, TAIL = 48, 64, 208, 144
HALF = 240


def inner_rows(inner, h):
    return [inner[256 * h + 64 * i : 256 * h + 64 * (i + 1)] for i in range(4)]


def pack_halves(section, qkv, out, cross, inner, down, gain_rows):
    width = out.shape[1]
    for h in range(2):
        few, many = slice(16 * h, 16 * h + 16), slice(64 * h, 64 * h + 64)
        parts = [(16 * i, 0, qkv[few, width * i : width * (i + 1)]) for i in range(3)]
        parts.append((GAIN, 0, gain_rows if h == 0 else jnp.zeros_like(gain_rows)))
        quarters = [(128 * i, part) for i, part in enumerate(inner_rows(inner, h))]
        if section == 0:
            parts += [(FIRST, 0, cross[few, :width]), (FIRST + 16, 0, cross[few, width:])]
            parts += [(FIRST + 32, 0, down[many]), (FIRST + 160, 0, out[few])]
            parts += [(FIRST + 96, at, part) for at, part in quarters]
        else:
            parts += [(FIRST, 0, out[few]), (FIRST + 16, 0, cross[few, :width])]
            parts += [(FIRST + 32, 0, down[many]), (FIRST + 160, 0, cross[few, width:])]
            parts += [(FIRST + 96, at, part) for at, part in quarters]
        yield h, parts


def pack_plain(section, qkv, out, cross, inner, down, gain_rows):
    packs = []
    for _, parts in pack_halves(section, qkv, out, cross, inner, down, gain_rows):
        pack = jnp.zeros((HALF, out.shape[1]), BF16)
        for row, col, value in parts:
            pack = lax.dynamic_update_slice(pack, value, (row, col))
        packs.append(pack)
    return jnp.stack(packs)


def pack_kernel(me, qkv, out, cross, inner, down, gains, kept, sent):
    width = out.shape[1]
    columns = gains.shape[1]
    spot = lax.broadcasted_iota(jnp.int32, (columns, width), 1) - me[0] * columns
    here = spot == lax.broadcasted_iota(jnp.int32, (columns, width), 0)
    spread = low(mm(gains[...], jnp.where(here, 1.0, 0.0).astype(BF16)))
    spread = jnp.concatenate([spread, jnp.zeros((16 - gains.shape[0], width), BF16)], axis=0)
    for section in range(2):

        @pl.when(me[1] == section)
        def _():
            shards = (qkv[...], out[...], cross[...], inner[...], down[...], spread)
            for h, parts in pack_halves(section, *shards):
                dst = kept if h == section else sent
                for row, col, value in parts:
                    dst[row : row + value.shape[0], col : col + value.shape[1]] = value


def pack_shards(me, qkv, out, cross, inner, down, gains):
    half = jax.ShapeDtypeStruct((HALF, out.shape[1]), BF16)
    return pl.pallas_call(
        pack_kernel,
        in_specs=[TABLE] + [WHOLE] * 6,
        out_specs=[WHOLE] * 2,
        out_shape=[half, half],
        name="pack_shards",
    )(me, qkv, out, cross, inner, down, gains)


def rows_at(block, rows):
    return pl.ds(pl.multiple_of(block * rows, rows), rows)


def start_copy(src, dst, sem):
    pltpu.make_async_copy(src, dst, sem).start()


def wait_for(ref, sem):
    pltpu.make_async_copy(ref, ref, sem).wait()


def each_half(table, own, other, body):
    for which, pieces in enumerate((own, other)):
        half = table[2, 0] if which == 0 else 1 - table[2, 0]
        first = 0
        for src in pieces:

            @pl.loop(0, src.shape[0])
            def _(p, src=src, first=first):
                body(src.at[p], table[which, first + p], half)

            first += src.shape[0]


def fetch_few(table, own, other, row, dst, sem):
    def body(src, j, half):
        start_copy(src.at[pl.ds(row, 16), :], dst.at[j, pl.ds(pl.multiple_of(16 * half, 16), 16), :], sem)

    each_half(table, own, other, body)


def fetch_ffn(table, own, other, row, inner, down, sems):
    def body(src, j, half):
        start_copy(src.at[pl.ds(row, 64), :], down.at[j, pl.ds(pl.multiple_of(64 * half, 64), 64), :], sems.at[1])
        for i in range(4):
            rows = pl.ds(pl.multiple_of(256 * half + 64 * i, 64), 64)
            start_copy(src.at[pl.ds(row + 64, 64), pl.ds(128 * i, 128)], inner.at[j, rows, :], sems.at[0])

    each_half(table, own, other, body)


def joined(blocks):
    value = blocks[...]
    return value.reshape(-1, value.shape[2])


def inner_cols(inner, c):
    return jnp.concatenate([inner[4 * c + i] for i in range(4)], axis=1)


def down_rows(down, c):
    return joined(down[4 * c : 4 * c + 4])


def pack_pair(rows, width):
    return [jax.ShapeDtypeStruct((BLOCKS, rows, width), BF16)] * 2


def stage_rows(stage, offset, grad):
    for j in range(BLOCKS):
        for h in range(2):
            stage[h, j, offset : offset + 16, :] = grad[32 * j + 16 * h : 32 * j + 16 * h + 16, :]


def stage_down(stage, offset, c, grad):
    for j in range(4):
        for h in range(2):
            at = 128 * j + 64 * h
            stage[h, 4 * c + j, offset : offset + 64, :] = grad[at : at + 64, :]


def stage_inner(stage, offset, c, grad):
    for j in range(4):
        for h in range(2):
            for i in range(4):
                at = 256 * h + 64 * i
                stage[h, 4 * c + j, offset : offset + 64, 128 * i : 128 * (i + 1)] = grad[
                    at : at + 64, 128 * j : 128 * (j + 1)
                ]


def send_stage(stage, kept, sent, place, sem):
    for h in range(2):
        for which, dst in enumerate((kept, sent)):

            @pl.when(place[2, h] == which)
            def _():
                @pl.loop(0, BLOCKS)
                def _(j):
                    pltpu.make_async_copy(stage.at[h, j], dst.at[place[h, j]], sem).start()


STEP = 64


def each_rows(rows, body):
    for i in range(rows // STEP):
        body(slice(i * STEP, (i + 1) * STEP))


def centred(v):
    shifted = v - jnp.mean(v, axis=-1, keepdims=True)
    rate = lax.rsqrt(jnp.mean(shifted * shifted, axis=-1, keepdims=True) + EPS)
    return shifted * rate, rate


def norm_back(v, gain, grad):
    unit, rate = centred(v)
    e = grad * gain
    back = e - jnp.mean(e, axis=-1, keepdims=True) - unit * jnp.mean(e * unit, axis=-1, keepdims=True)
    return back * rate, grad * unit


def gelu_parts(u):
    phi = 0.5 + 0.5 * lax.erf(u * (1.0 / math.sqrt(2.0)))
    bell = jnp.exp2(u * u * (-0.5 * LOG2E)) * (1.0 / math.sqrt(2.0 * math.pi))
    return u * phi, phi + u * bell


def places_of(dest):
    rows = dest.shape[1]
    return jnp.where(lax.broadcasted_iota(jnp.int32, (rows, rows), 0) == dest[...], 1.0, 0.0).astype(BF16)


def sort_kernel(moves, section, inputs, came, cotangent, dest_e, dest_d, x_e, x_d, ct):
    s = section[0]
    moves.ready(dest_e, dest_d, inputs, came, cotangent)
    place_e, place_d = places_of(dest_e), places_of(dest_d)
    for owner, dst, place in ((0, x_e, place_e), (1, x_d, place_d)):

        @pl.when(s == owner)
        def _():
            dst[...] = low(mm(place, inputs[s]))

        @pl.when(s != owner)
        def _():
            dst[...] = low(mm(place, came[...]))

    moves.done(x_e, x_d)
    ct[...] = low(mm(place_d, cotangent[s]))
    moves.done(ct)


def sort_rows(section, inputs, came, cotangent, dest_e, dest_d):
    row16 = jax.ShapeDtypeStruct(came.shape, BF16)
    return call_dense(
        sort_kernel, "sort_rows", 2, [section], [inputs, came, cotangent, Near(dest_e), Near(dest_d)], [], [row16] * 3, [], []
    )


def fetch_front(table, own, other, w, sem):
    def body(src, j, half):
        at = pl.ds(pl.multiple_of(32 * j + 16 * half, 16), 16)
        for i in range(3):
            start_copy(src.at[pl.ds(16 * i, 16), :], w.at[at, pl.ds(512 * i, 512)], sem)

    each_half(table, [own], [other], body)


def front_kernel(moves, table, x, own, other, n, q, k, v, g, w, gs, prod, sems):
    for which, src in enumerate((own, other)):

        @pl.loop(0, BLOCKS)
        def _(p):
            pltpu.make_async_copy(src.at[p, pl.ds(GAIN, 16), :], gs.at[which, p], sems.at[1]).start()

    fetch_front(table, own, other, w, sems.at[0])
    wait_for(gs, sems.at[1])
    gains = jnp.sum(gs[...].astype(F32), axis=(0, 1))[0:8]
    g[...] = gains
    gain = gains[0:1]
    moves.ready(x)

    def body(rows):
        n[rows, :] = low(centred(x[rows, :].astype(F32))[0] * gain)

    each_rows(x.shape[0], body)
    moves.done(n)
    wait_for(w, sems.at[0])
    for i, out in enumerate((q, k, v)):
        prod[...] = mm(n[...], w[:, 512 * i : 512 * (i + 1)])

        def keep(rows, out=out):
            out[rows, :] = low(prod[rows, :])

        each_rows(x.shape[0], keep)
        moves.done(out)


def front(table, x, own, other):
    rows, width = x.shape
    row16 = jax.ShapeDtypeStruct((rows, width), BF16)
    gain = jax.ShapeDtypeStruct((8, width), F32)
    return call_dense(
        front_kernel, "front", 4, [table], [x], [own, other], [row16] + [Both(row16)] * 3 + [Near(gain)], [],
        [
            pltpu.VMEM((width, 3 * width), BF16),
            pltpu.VMEM((2, BLOCKS, 16, width), BF16),
            pltpu.VMEM((rows, width), F32),
            pltpu.SemaphoreType.DMA((2,)),
        ],
    )


def mid_kernel(
    pieces, moves, table, a_e, a_d, x_e, x_d, g_e, g_d, dest, *refs
):
    mid_body(moves, table, a_e, a_d, x_e, x_d, g_e, g_d, dest, refs[:pieces], refs[pieces : 2 * pieces], *refs[2 * pieces :])


def mid_body(
    moves, table, a_e, a_d, x_e, x_d, g_e, g_d, dest, own, other,
    m_e, n_e, act, slope, end, memory, mem_k, mem_v, m_d, n_d, query, memory_out,
    w_out, w_in, w_down, w_cross, w_query, prod, spare, total, sems,
):
    fetch_few(table, own, other, 160, w_out.at[0], sems.at[0])
    fetch_ffn(table, own, other, 32, w_in, w_down, sems.at[pl.ds(1, 2)])
    fetch_few(table, own, other, 176, w_out.at[1], sems.at[3])
    for i in range(2):
        fetch_few(table, own, other, 16 * i, w_cross.at[i], sems.at[4])
    fetch_few(table, own, other, 192, w_query, sems.at[5])
    count = x_e.shape[0]

    def attended(a, x, g, m, n, section, sem):
        moves.ready(a)
        wait_for(w_out.at[section], sem)
        prod[...] = mm(a[...], joined(w_out[section]))
        moves.ready(x)
        gain = g[1:2, :]

        def body(rows):
            middle = x[rows, :].astype(F32) + prod[rows, :]
            m[rows, :] = middle
            n[rows, :] = low(centred(middle)[0] * gain)

        each_rows(count, body)
        moves.done(m, n)

    attended(a_e, x_e, g_e, m_e, n_e, 0, sems.at[0])
    wait_for(w_in, sems.at[1])
    wait_for(w_down, sems.at[2])
    total[...] = m_e[...]
    prods = (prod, spare)
    prod[...] = mm(n_e[...], inner_cols(w_in, 0))
    for c in range(4):
        cols = slice(512 * c, 512 * (c + 1))
        if c < 3:
            prods[(c + 1) % 2][...] = mm(n_e[...], inner_cols(w_in, c + 1))

        def body(rows, cols=cols, hidden=prods[c % 2]):
            value, rate = gelu_parts(hidden[rows, :])
            act[rows, cols] = low(value)
            slope[rows, cols] = low(rate)

        each_rows(count, body)
        total[...] += mm(act[:, cols], down_rows(w_down, c))

    moves.done(act, slope)
    gain = g_e[2:3, :]

    def body(rows):
        ending = total[rows, :]
        end[rows, :] = ending
        memory[rows, :] = low(centred(ending)[0] * gain)

    each_rows(count, body)
    moves.done(end, memory)
    wait_for(w_cross, sems.at[4])
    mem_k[...] = low(mm(memory[...], joined(w_cross[0])))
    mem_v[...] = low(mm(memory[...], joined(w_cross[1])))
    moves.done(mem_k, mem_v)
    memory_out[...] = low(mm_tn(places_of(dest), memory[...]))
    moves.done(memory_out)
    attended(a_d, x_d, g_d, m_d, n_d, 1, sems.at[3])
    wait_for(w_query, sems.at[5])
    query[...] = low(mm(n_d[...], joined(w_query)))
    moves.done(query)


def mid(table, a_e, a_d, x_e, x_d, g_e, g_d, dest, own, other):
    rows, width = x_e.shape
    row16 = jax.ShapeDtypeStruct((rows, width), BF16)
    row32 = jax.ShapeDtypeStruct((rows, width), F32)
    wide = jax.ShapeDtypeStruct((rows, 4 * width), BF16)
    return call_dense(
        functools.partial(mid_kernel, len(own)), "mid", 8, [table],
        [a_e, a_d, x_e, x_d, Near(g_e), Near(g_d), Near(dest)], [*own, *other],
        [row32, row16, wide, wide, row32, row16, Both(row16), Both(row16), row32, row16, Both(row16), row16], [],
        [
            pltpu.VMEM((2, BLOCKS, 32, width), BF16),
            pltpu.VMEM((BLOCKS, width, 128), BF16),
            pltpu.VMEM((BLOCKS, 128, width), BF16),
            pltpu.VMEM((2, BLOCKS, 32, width), BF16),
            pltpu.VMEM((BLOCKS, 32, width), BF16),
            pltpu.VMEM((rows, width), F32),
            pltpu.VMEM((rows, width), F32),
            pltpu.VMEM((rows, width), F32),
            pltpu.SemaphoreType.DMA((6,)),
        ],
    )


def tail_kernel(
    pieces, moves, place, section, table, crossed, m_d, ct, g_d, dest, memory, *refs
):
    own, other = refs[:pieces], refs[pieces : 2 * pieces]
    tail_body(moves, place, section, table, crossed, m_d, ct, g_d, dest, memory, own, other, *refs[2 * pieces :])


def tail_body(
    moves, place, section, table, crossed, m_d, ct, g_d, dest, memory, own, other,
    stay, leave, second_grad, crossed_grad, gain_grad, kept, sent,
    w_out, w_in, w_down, second, n, unit_grad, out_prod, prod, act, hidden, grad, total, stage, sems,
):
    fetch_few(table, own, other, 128, w_out, sems.at[0])
    fetch_ffn(table, own, other, 0, w_in, w_down, sems.at[pl.ds(1, 2)])
    count = m_d.shape[0]
    wait_for(w_out, sems.at[0])
    out_prod[...] = mm(crossed[...], joined(w_out))
    moves.ready(m_d)
    gain = g_d[2:3, :]

    def body(rows):
        value = m_d[rows, :] + out_prod[rows, :]
        second[rows, :] = value
        total[rows, :] = value
        n[rows, :] = low(centred(value)[0] * gain)
        unit_grad[rows, :] = jnp.zeros((STEP, value.shape[1]), F32)

    each_rows(count, body)
    wait_for(w_in, sems.at[1])
    wait_for(w_down, sems.at[2])

    moves.ready(ct)

    def products(c):
        cols = slice(512 * c, 512 * (c + 1))
        prod[c % 2] = mm(n[...], inner_cols(w_in, c))
        hidden[c % 2] = mm_nt(ct[...], down_rows(w_down, c))

    products(0)
    for c in range(4):
        cols = slice(512 * c, 512 * (c + 1))
        if c < 3:
            products(c + 1)

        def body(rows, c=c):
            value, rate = gelu_parts(prod[c % 2, rows, :])
            act[c % 2, rows, :] = low(value)
            grad[c % 2, rows, :] = low(hidden[c % 2, rows, :] * rate)

        each_rows(count, body)
        total[...] += mm(act[c % 2], down_rows(w_down, c))
        stage_down(stage, 0, c, low(mm_tn(act[c % 2], ct[...])))
        stage_inner(stage, 64, c, low(mm_tn(n[...], grad[c % 2])))
        unit_grad[...] += mm_nt(grad[c % 2], inner_cols(w_in, c))

    gain_grad[...] = jnp.zeros_like(gain_grad)

    def back(rows):
        act[0, rows, :] = low(total[rows, :])
        part, gained = norm_back(second[rows, :], gain, unit_grad[rows, :])
        gain_grad[...] += fold(gained)
        whole = ct[rows, :].astype(F32) + part
        second_grad[rows, :] = whole
        n[rows, :] = low(whole)

    each_rows(count, back)
    moves.done(second_grad)
    stage_rows(stage, 128, low(mm_tn(crossed[...], n[...])))
    send_stage(stage, kept, sent, place, sems.at[3])
    crossed_grad[...] = low(mm_nt(n[...], joined(w_out)))
    moves.ready(memory)
    for owner in range(2):

        @pl.when(section[0] == owner)
        def _():
            out, through = (leave, stay) if owner == 0 else (stay, leave)
            out[...] = low(mm_tn(places_of(dest), act[0]))
            through[...] = memory[...]

    moves.done(stay, leave)
    wait_for(stage, sems.at[3])


def tail(place, section, table, crossed, m_d, ct, g_d, dest, memory, own, other):
    rows, width = m_d.shape
    row16 = jax.ShapeDtypeStruct((rows, width), BF16)
    row32 = jax.ShapeDtypeStruct((rows, width), F32)
    return call_dense(
        functools.partial(tail_kernel, len(own)), "tail", 15, [place, section, table],
        [Near(crossed), m_d, ct, Near(g_d), Near(dest), memory], [*own, *other],
        [row16, row16, row32, Near(row16), Near(jax.ShapeDtypeStruct((8, width), F32))], pack_pair(144, width),
        [
            pltpu.VMEM((BLOCKS, 32, width), BF16),
            pltpu.VMEM((BLOCKS, width, 128), BF16),
            pltpu.VMEM((BLOCKS, 128, width), BF16),
            pltpu.VMEM((rows, width), F32),
            pltpu.VMEM((rows, width), BF16),
            pltpu.VMEM((rows, width), F32),
            pltpu.VMEM((rows, width), F32),
            pltpu.VMEM((2, rows, width), F32),
            pltpu.VMEM((2, rows, width), BF16),
            pltpu.VMEM((2, rows, width), F32),
            pltpu.VMEM((2, rows, width), BF16),
            pltpu.VMEM((rows, width), F32),
            pltpu.VMEM((2, BLOCKS, 144, width), BF16),
            pltpu.SemaphoreType.DMA((4,)),
        ],
    )


def mid_back_kernel(pieces, moves, place, table, *refs):
    ins, refs = refs[:16], refs[16:]
    mid_back_body(moves, place, table, *ins, refs[:pieces], refs[pieces : 2 * pieces], *refs[2 * pieces :])


def mid_back_body(
    moves, place, table, dq, dk, dv, n_d, m_d, second_grad, a_d, memory, end, act, slope, n_e, m_e, a_e, g_e, g_d, own, other,
    md_grad, ad_grad, me_grad, ae_grad, ge_grad, kept, sent,
    w_out, w_in, w_down, w_cross, w_query, prod, hidden, grad, total, small, stage, sems,
):
    fetch_few(table, own, other, 192, w_query, sems.at[5])
    fetch_few(table, own, other, 176, w_out.at[1], sems.at[3])
    for i in range(2):
        fetch_few(table, own, other, 16 * i, w_cross.at[i], sems.at[4])
    fetch_ffn(table, own, other, 32, w_in, w_down, sems.at[pl.ds(1, 2)])
    fetch_few(table, own, other, 160, w_out.at[0], sems.at[0])
    count = m_d.shape[0]
    ge_grad[...] = jnp.zeros_like(ge_grad)

    def through_out(a, grad, result, section, offset):
        stage_rows(stage, offset, low(mm_tn(a[...], small[...])))
        result[...] = low(mm_nt(small[...], joined(w_out[section])))

    moves.ready(n_d)
    stage_rows(stage, 176, low(mm_tn(n_d[...], dq[...])))
    wait_for(w_query, sems.at[5])
    prod[...] = mm_nt(dq[...], joined(w_query))
    moves.ready(m_d, second_grad)
    gain_d = g_d[1:2, :]

    def decoder(rows):
        part, _ = norm_back(m_d[rows, :], gain_d, prod[rows, :])
        whole = second_grad[rows, :] + part
        md_grad[rows, :] = whole
        small[rows, :] = low(whole)

    each_rows(count, decoder)
    moves.done(md_grad)
    moves.ready(a_d)
    wait_for(w_out.at[1], sems.at[3])
    through_out(a_d, md_grad, ad_grad, 1, 192)

    moves.ready(memory)
    stage_rows(stage, 0, low(mm_tn(memory[...], dk[...])))
    stage_rows(stage, 16, low(mm_tn(memory[...], dv[...])))
    wait_for(w_cross, sems.at[4])
    prod[...] = mm_nt(dk[...], joined(w_cross[0]))
    prod[...] += mm_nt(dv[...], joined(w_cross[1]))
    moves.ready(end)
    gain_two = g_e[2:3, :]

    def ending(rows):
        part, _ = norm_back(end[rows, :], gain_two, prod[rows, :])
        me_grad[rows, :] = part
        small[rows, :] = low(part)
        total[rows, :] = jnp.zeros_like(part)

    each_rows(count, ending)
    wait_for(w_in, sems.at[1])
    wait_for(w_down, sems.at[2])

    hidden[0] = mm_nt(small[...], down_rows(w_down, 0))
    moves.ready(slope, act, n_e)
    for c in range(4):
        cols = slice(512 * c, 512 * (c + 1))
        if c < 3:
            hidden[(c + 1) % 2] = mm_nt(small[...], down_rows(w_down, c + 1))

        def body(rows, c=c, cols=cols):
            grad[c % 2, rows, :] = low(hidden[c % 2, rows, :] * slope[rows, cols].astype(F32))

        each_rows(count, body)
        stage_down(stage, 32, c, low(mm_tn(act[:, cols], small[...])))
        stage_inner(stage, 96, c, low(mm_tn(n_e[...], grad[c % 2])))
        total[...] += mm_nt(grad[c % 2], inner_cols(w_in, c))

    moves.ready(m_e)
    gain_one = g_e[1:2, :]

    def encoder(rows):
        part, gained = norm_back(m_e[rows, :], gain_one, total[rows, :])
        ge_grad[...] += fold(gained)
        whole = me_grad[rows, :] + part
        me_grad[rows, :] = whole
        small[rows, :] = low(whole)

    each_rows(count, encoder)
    moves.done(me_grad)
    moves.ready(a_e)
    wait_for(w_out.at[0], sems.at[0])
    through_out(a_e, me_grad, ae_grad, 0, 160)
    send_stage(stage, kept, sent, place, sems.at[6])
    wait_for(stage, sems.at[6])


def mid_back(place, table, dq, dk, dv, n_d, m_d, second_grad, a_d, memory, end, act, slope, n_e, m_e, a_e, g_e, g_d, own, other):
    rows, width = m_d.shape
    row16 = jax.ShapeDtypeStruct((rows, width), BF16)
    row32 = jax.ShapeDtypeStruct((rows, width), F32)
    return call_dense(
        functools.partial(mid_back_kernel, len(own)), "mid_back", 19, [place, table],
        [Near(dq), Near(dk), Near(dv), n_d, m_d, second_grad, a_d, memory, end, act, slope, n_e, m_e, a_e, Near(g_e), Near(g_d)],
        [*own, *other], [row32, Near(row16), row32, Near(row16), Near(jax.ShapeDtypeStruct((8, width), F32))],
        pack_pair(208, width),
        [
            pltpu.VMEM((2, BLOCKS, 32, width), BF16),
            pltpu.VMEM((BLOCKS, width, 128), BF16),
            pltpu.VMEM((BLOCKS, 128, width), BF16),
            pltpu.VMEM((2, BLOCKS, 32, width), BF16),
            pltpu.VMEM((BLOCKS, 32, width), BF16),
            pltpu.VMEM((rows, width), F32),
            pltpu.VMEM((2, rows, width), F32),
            pltpu.VMEM((2, rows, width), BF16),
            pltpu.VMEM((rows, width), F32),
            pltpu.VMEM((rows, width), BF16),
            pltpu.VMEM((2, BLOCKS, 208, width), BF16),
            pltpu.SemaphoreType.DMA((7,)),
        ],
    )


def front_w_kernel(moves, place, qe, ke, ve, qd, kd, vd, n_e, n_d, ge_one, gd_two, ds_e, ds_d, ds_c, kept, sent, stage, sems):
    width = n_e.shape[1]
    for section, (grads, n) in enumerate((((qe, ke, ve), n_e), ((qd, kd, vd), n_d))):
        moves.ready(n)
        for i in range(3):
            grad = low(mm_tn(n[...], grads[i][...]))
            for j in range(BLOCKS):
                stage[section, j, 32 * i : 32 * i + 32, :] = grad[32 * j : 32 * j + 32, :]
    lane = lax.broadcasted_iota(jnp.int32, (8, width), 1)
    heads = jnp.zeros((8, width), F32)
    for i, ds in enumerate((ds_e, ds_d, ds_c)):
        heads = jnp.where(lane == i, jnp.sum(ds[...], axis=1, keepdims=True), heads)
    lines = [jnp.sum(g[...], axis=0, keepdims=True) for g in (ge_one, gd_two)]
    extra = low(jnp.concatenate(lines + [jnp.zeros((6, width), F32), heads], axis=0))
    for h in range(2):
        for j in range(BLOCKS):
            stage[h, j, 96:112, :] = extra
    send_stage(stage, kept, sent, place, sems.at[0])
    wait_for(stage, sems.at[0])


def front_w(place, grads_e, grads_d, n_e, n_d, ge_one, gd_two, ds):
    width = n_e.shape[1]
    near = [Near(g) for g in (*grads_e, *grads_d)]
    return call_dense(
        front_w_kernel, "front_w", 5, [place], [*near, n_e, n_d, *map(Near, (ge_one, gd_two, *ds))], [],
        [], pack_pair(112, width),
        [pltpu.VMEM((2, BLOCKS, 112, width), BF16), pltpu.SemaphoreType.DMA((1,))],
    )


def front_x_kernel(moves, table, *refs):
    ins, far, outs, (w, prod, high, rest, sems) = refs[:14], refs[14:18], refs[18:20], refs[20:]
    for i in range(2):
        fetch_front(table, far[2 * i], far[2 * i + 1], w.at[i], sems.at[i])
    for i in range(2):
        dq, dk, dv, x, m_grad, g, dest = (*ins[3 * i : 3 * i + 3], *ins[6 + 4 * i : 10 + 4 * i])
        wait_for(w.at[i], sems.at[i])
        prod[i] = mm_nt(dq[...], w[i, :, 0:512])
        prod[i] += mm_nt(dk[...], w[i, :, 512:1024])
        prod[i] += mm_nt(dv[...], w[i, :, 1024:1536])
        moves.ready(x, m_grad)
        gain = g[0:1, :]

        def body(rows, i=i, x=x, m_grad=m_grad, gain=gain):
            part, _ = norm_back(x[rows, :].astype(F32), gain, prod[i, rows, :])
            whole = m_grad[rows, :] + part
            high[i, rows, :] = low(whole)
            rest[i, rows, :] = low(whole - high[i, rows, :].astype(F32))

        each_rows(x.shape[0], body)
        place = places_of(dest)
        outs[i][...] = mm_tn(place, high[i])
        outs[i][...] += mm_tn(place, rest[i])
        moves.done(outs[i])


def front_x(table, grads, xs, m_grads, gs, dests, firsts):
    rows, width = xs[0].shape
    rest = [a for x, m, g, d in zip(xs, m_grads, gs, dests) for a in (x, m, Near(g), Near(d))]
    return call_dense(
        front_x_kernel, "front_x", 9, [table], [*(Near(g) for pair in grads for g in pair), *rest],
        [pack for pair in firsts for pack in pair], [jax.ShapeDtypeStruct((rows, width), F32)] * 2, [],
        [
            pltpu.VMEM((2, width, 3 * width), BF16),
            pltpu.VMEM((2, rows, width), F32),
            pltpu.VMEM((2, rows, width), BF16),
            pltpu.VMEM((2, rows, width), BF16),
            pltpu.SemaphoreType.DMA((2,)),
        ],
    )


def exact(a, b, dims):
    return lax.dot_general(a, b, (dims, ((), ())), precision=lax.Precision.HIGHEST, preferred_element_type=F32)


def finish_kernel(
    moves, place, own, came, last, w_qkv, w_cross, gains, slope, qkv, out, cross, inner, down, gain, alpha
):
    columns = gains.shape[1]
    moves.ready(w_qkv, w_cross, gains, slope)
    extra = last[96:112, :]
    for i in range(3):
        qkv[:, 512 * i : 512 * (i + 1)] = last[32 * i : 32 * i + 32, :]

    def halves_to(offsets):
        at_out, at_cross, at_inner, at_down = offsets
        for h in range(2):
            for section, src in ((h, own), (1 - h, came)):

                @pl.when(place[1] == section)
                def _():
                    few = slice(16 * h, 16 * h + 16)
                    out[few, :] = src[at_out : at_out + 16, :].astype(F32)
                    for i in range(2):
                        at = at_cross[i]
                        cross[few, 512 * i : 512 * (i + 1)] = src[at : at + 16, :].astype(F32)
                    for i in range(4):
                        rows = slice(256 * h + 64 * i, 256 * h + 64 * (i + 1))
                        inner[rows, :] = src[at_inner : at_inner + 64, 128 * i : 128 * (i + 1)].astype(F32)
                    down[64 * h : 64 * h + 64, :] = src[at_down : at_down + 64, :].astype(F32)

    spot = lax.broadcasted_iota(jnp.int32, (extra.shape[1], columns), 0) - place[0] * columns
    pick = jnp.where(spot == lax.broadcasted_iota(jnp.int32, (extra.shape[1], columns), 1), 1.0, 0.0)
    split = exact(extra[0:8], pick, ((1,), (0,)))

    def reach(weight, grad):
        weighted = weight.astype(F32) * grad
        return exact(jnp.ones((8, weighted.shape[1]), F32), weighted, ((1,), (1,)))[0:1]

    @pl.when(place[1] == 0)
    def _():
        halves_to((160, (0, 16), 96, 32))
        gain[0:1, :] = reach(w_qkv[...], qkv[...]) / gains[0:1, :].astype(F32)
        gain[1:2, :] = split[0:1]
        gain[2:3, :] = reach(w_cross[...], cross[...]) / gains[2:3, :].astype(F32)

    @pl.when(place[1] == 1)
    def _():
        halves_to((160, (144, 128), 64, 0))
        gain[0:1, :] = reach(w_qkv[...], qkv[...]) / gains[0:1, :].astype(F32)
        gain[1:2, :] = reach(w_cross[:, 0:512], cross[:, 0:512]) / gains[1:2, :].astype(F32)
        gain[2:3, :] = split[1:2]

    alpha[...] = extra[8:16, 0:128].T[0:3, :] * slope[...]
    moves.done(qkv, out, cross, inner, down, gain, alpha)


def finish(place, own, came, last, w_qkv, w_cross, gains, slope):
    shapes = [(32, 1536), (32, 512), (32, 1024), (512, 128), (128, 512), (3, 32), (3, 8)]
    return call_dense(
        finish_kernel, "finish", 2, [place], [Near(own), Near(came), Near(last), w_qkv, w_cross, gains, slope], [],
        [jax.ShapeDtypeStruct(shape, F32) for shape in shapes], [], [],
    )


ORDER = ((4, 8, 1, 2), (4, 8, 2, 1))
SHIFT = np.array(
    [[functools.reduce(lambda a, b: a ^ b, [m for b, m in enumerate(order) if p >> b & 1], 0) for p in range(BLOCKS)] for order in ORDER],
    np.int32,
)
WHERE = np.argsort(SHIFT, axis=1).astype(np.int32)
SWAP = [(0, 1), (1, 0)]


def swap(value):
    return lax.ppermute(value, "section", SWAP)


def hop(value, bit):
    pairs = [
        (BLOCKS * s + i, BLOCKS * s + (i ^ ORDER[s][bit])) for s in range(2) for i in range(BLOCKS)
    ]
    return lax.ppermute(value, ("section", "dp"), pairs)


def jump(value, position):
    pairs = [
        (BLOCKS * s + i, BLOCKS * s + (i ^ int(SHIFT[s, position]))) for s in range(2) for i in range(BLOCKS)
    ]
    return lax.ppermute(value, ("section", "dp"), pairs)


def tie(value, held):
    return lax.optimization_barrier((value, held))


def behind(out, *packs):
    kept = [pack[0] for pack in packs]
    out, kept = lax.optimization_barrier((out, kept))
    for pack, value in zip(packs, kept):
        pack[0] = value
    return out


def total(terms, first, last):
    return low(sum(term[first:last].astype(F32) for term in terms))


def to_line(terms):
    return [total(terms, i, i + 1)[0] for i in (1, 2, 3)]


def along_line(sent):
    return [jump(sent[i - 1], i) for i in (2, 3, 1)]


def at_last(terms, came):
    return sum([term[0].astype(F32) for term in terms] + [block.astype(F32) for block in came])


def inner_of(halves):
    quarter, width = halves[0].shape
    rows = [h.reshape(quarter, 4, width // 4).transpose(1, 0, 2).reshape(4 * quarter, width // 4) for h in halves]
    return jnp.concatenate(rows, axis=0)


def spread_line(block):
    return jnp.stack([block] + [jump(block, i) for i in (1, 2, 3)])


def spread_plane(blocks, bit):
    return jnp.concatenate([blocks, hop(blocks, bit)], axis=0)


def weights_near(attn_qkv, attn_out, cross_proj, ffn_in, ffn_out, gains, later):
    me, section = lax.axis_index("dp"), lax.axis_index("section")
    kept, sent = pack_shards(
        jnp.stack([me, section]), attn_qkv[0], attn_out[0], cross_proj[0], ffn_in[0], ffn_out[0], gains[0]
    )
    came = swap(sent)
    enc, dec = jnp.where(section == 0, kept, came), jnp.where(section == 0, came, kept)
    mid_pack = jnp.concatenate([enc[FIRST:], dec[FIRST : FIRST + 32]], axis=0)
    tail_pack = dec[FIRST + 32 :]
    enc, dec = enc[:FIRST], dec[:FIRST]
    enc = spread_line(enc)
    (dec, mid_pack, later), enc = tie((dec, mid_pack, later), enc)
    came = [jump(mid_pack, i) for i in (1, 2, 3)]
    enc, dec = tie(spread_plane(enc, 2), spread_line(dec))
    (enc, tail_pack), (dec, mid_pack) = tie(
        (spread_plane(enc, 3), tail_pack), (spread_plane(dec, 2), jnp.stack([mid_pack] + came))
    )
    enc = (enc, swap(enc))
    dec = (dec, hop(dec, 3))
    mid_pack = (mid_pack, hop(mid_pack, 2))
    tail_pack = (tail_pack, [jump(tail_pack, i) for i in (1, 2, 3)])
    shift = jnp.asarray(SHIFT)
    table = jnp.stack([shift[section] ^ me, shift[1 - section] ^ me, jnp.full((BLOCKS,), section, jnp.int32)])
    where = jnp.asarray(WHERE)[:, jnp.arange(BLOCKS, dtype=jnp.int32) ^ me]
    halves = jnp.where(jnp.arange(BLOCKS) == section, 0, 1).astype(jnp.int32)
    return later, enc, dec, mid_pack, tail_pack, table, jnp.concatenate([where, halves[None]])


def weights_far(attn_qkv, attn_out, cross_proj, ffn_in, ffn_out, gains, later):
    def whole(shard, axis):
        return lax.all_gather(shard[0], "dp", axis=axis, tiled=True)

    qkv, out, cross, inner, down, gain = (
        whole(w, a) for w, a in ((attn_qkv, 0), (attn_out, 0), (cross_proj, 0), (ffn_in, 1), (ffn_out, 0), (gains, 1))
    )
    width = out.shape[1]
    gain_rows = jnp.zeros((BLOCKS, 16, width), BF16).at[0, : gain.shape[0]].set(gain)
    section = lax.axis_index("section")
    shards = (
        qkv.reshape(BLOCKS, -1, 3 * width),
        out.reshape(BLOCKS, -1, width),
        cross.reshape(BLOCKS, -1, 2 * width),
        inner.reshape(width, BLOCKS, -1).transpose(1, 0, 2),
        down.reshape(BLOCKS, -1, width),
        gain_rows,
    )
    pack = lax.cond(
        section == 0,
        lambda *args: jax.vmap(functools.partial(pack_plain, 0), out_axes=1)(*args),
        lambda *args: jax.vmap(functools.partial(pack_plain, 1), out_axes=1)(*args),
        *shards,
    )
    came = swap(pack)
    enc, dec = jnp.where(section == 0, pack, came), jnp.where(section == 0, came, pack)
    mid_pack = jnp.concatenate([enc[:, :, FIRST:], dec[:, :, FIRST : FIRST + 32]], axis=2)
    tail_pack = dec[:, :, FIRST + 32 :]
    enc, dec = enc[:, :, :FIRST], dec[:, :, :FIRST]
    plain = jnp.arange(BLOCKS, dtype=jnp.int32)
    table = jnp.stack([plain, plain, jnp.zeros_like(plain)])
    halves = jnp.where(plain == 0, 0, 1).astype(jnp.int32)
    return later, (enc[0], enc[1]), (dec[0], dec[1]), ([mid_pack[0]], [mid_pack[1]]), ([tail_pack[0]], [tail_pack[1]]), table, jnp.stack([plain, plain, halves])


def far_shards(tail_pack, mid_pack, front_pack):
    tail_pack, mid_pack, front_pack = (jnp.stack(p) for p in (tail_pack, mid_pack, front_pack))

    def qkv_of(pack):
        return jnp.concatenate([pack[:, 32 * i : 32 * i + 32].reshape(-1, pack.shape[2]) for i in range(3)], axis=1)
    def rows(pack, start, count):
        part = pack[:, :, start : start + count]
        return part.transpose(1, 0, 2, 3).reshape(-1, part.shape[-1])

    def inner(pack, start):
        blocks = jax.vmap(lambda a, b: inner_of([a, b]))(pack[0, :, start : start + 64], pack[1, :, start : start + 64])
        return blocks.transpose(1, 0, 2).reshape(blocks.shape[1], -1)

    def side(pack, *starts):
        return jnp.concatenate([rows(pack, s, 16) for s in starts], axis=1)

    enc = (qkv_of(front_pack[0]), rows(mid_pack, 160, 16), side(mid_pack, 0, 16), inner(mid_pack, 96), rows(mid_pack, 32, 64))
    cross_d = jnp.concatenate([rows(mid_pack, 176, 16), rows(tail_pack, 128, 16)], axis=1)
    dec = (qkv_of(front_pack[1]), rows(mid_pack, 192, 16), cross_d, inner(tail_pack, 64), rows(tail_pack, 0, 64))
    section = lax.axis_index("section")
    grads = []
    for a, b, axis in zip(enc, dec, (0, 0, 0, 1, 0)):
        mine = jnp.where(section == 0, a, b).astype(F32) + swap(jnp.where(section == 0, b, a)).astype(F32)
        grads.append(lax.psum_scatter(mine, "dp", scatter_dimension=axis, tiled=True))
    extra = lax.psum(front_pack[0, 0, 96:112].astype(F32), ("section", "dp"))
    return tuple(grads), extra


def gain_grads(weights, grads, gains, extra):
    section = lax.axis_index("section")
    qkv, cross = (w[0].astype(F32) * g for w, g in zip(weights, grads))
    gain = gains[0].astype(F32)
    columns = gain.shape[1]
    start = lax.axis_index("dp") * columns
    split = lax.dynamic_slice(extra, (section, start), (1, columns))[0]
    half = cross.shape[1] // 2
    reach = jnp.sum(cross[:, :half], axis=1)
    memory = (reach + jnp.sum(cross[:, half:], axis=1)) / gain[2]
    first = jnp.sum(qkv, axis=1) / gain[0]
    enc, dec = jnp.stack([first, split, memory]), jnp.stack([first, reach / gain[1], split])
    return jnp.where(section == 0, enc, dec)


def new_places(lengths, starts, rows):
    ends = jnp.cumsum(lengths)
    places = jnp.arange(rows, dtype=jnp.int32)
    pick = (places[:, None] >= (ends - lengths)[None, :]) & (places[:, None] < ends[None, :])
    return (places + jnp.sum(jnp.where(pick, (starts - ends + lengths)[None, :], 0), axis=1))[None]


def local(
    layer_input, cotangent, lengths, attn_qkv, attn_out, cross_proj, ffn_in, ffn_out, gains, alpha_raw
):
    section = lax.axis_index("section")
    near = lax.axis_size("dp") == BLOCKS
    weights = weights_near if near else weights_far
    later = (layer_input, cotangent, lengths, alpha_raw)
    later, first_e, first_d, mid_pack, tail_pack, table, place = weights(
        attn_qkv, attn_out, cross_proj, ffn_in, ffn_out, gains, later
    )
    layer_input, cotangent, lengths, alpha_raw = later
    rows, width = layer_input.shape[3:]
    inputs = layer_input[0, :, 0]
    came = swap(lax.dynamic_index_in_dim(inputs, 1 - section, 0, keepdims=False))
    first = section == 0
    source, target = lax.dynamic_index_in_dim(lengths[:, :, 0], section, 1, keepdims=False)
    large_e, large_d = source == jnp.max(source), target == jnp.max(target)
    starts_e = starts_of(source, jnp.where(large_e, 0, jnp.where(large_d, 2, 1)))
    starts_d = starts_of(target, jnp.where(large_d, 0, jnp.where(large_e, 1, 2)))
    dest_e, dest_d = new_places(source, starts_e, rows), new_places(target, starts_d, rows)
    x_e, x_d, ct = sort_rows(section[None], inputs, came, cotangent[:, 0], dest_e, dest_d)
    head_width = width // alpha_raw.shape[1]
    gate = jax.nn.sigmoid(alpha_raw)
    coef = [coefs_of(0.25 + 0.25 * gate[i], head_width) for i in range(3)]
    marks_e = marks_of(starts_e, source, starts_e, source, rows, False)
    marks_d = marks_of(starts_d, target, starts_d, target, rows, True)
    marks_c = marks_of(starts_d, target, starts_e, source, rows, False)

    def by_micro(kept, came):
        return jnp.stack([jnp.where(first, kept, came), jnp.where(first, came, kept)])[None, :, None]

    def settle(enc, dec):
        return by_micro(jnp.where(first, enc, dec), swap(jnp.where(first, dec, enc)))

    n_e, (q_now, q_e), (k_now, k_e), (v_now, v_e), g_e = front(table, x_e, *first_e)
    if near:
        (dec, dec_came), (mid_0, mid_1), (block, came) = first_d, mid_pack, tail_pack
        (dec, mid_1, block), q_now = tie((dec, mid_1, block), q_now)
        (q_now, mid_0, mid_1), (dec, tail_0) = tie(
            (q_now, mid_0, mid_1), (jnp.concatenate([dec, dec_came], axis=0), jnp.stack([block] + came))
        )
        mid_2, mid_3, other_0, other_1 = hop(mid_0, 3), hop(mid_1, 3), swap(mid_0), swap(mid_1)
        first_d = (dec, swap(dec))
    a_e, *stats_e = attend(q_now, k_now, v_now, marks_e, coef[0])
    if near:
        (mid_2, mid_3, other_0, other_1, first_d), a_e = tie((mid_2, mid_3, other_0, other_1, first_d), a_e)
        (x_d, tail_0, mid_2, mid_3), (other_0, other_1, first_d) = tie(
            (x_d, tail_0, mid_2, mid_3), (other_0, other_1, first_d)
        )
        tail_1, other_tail_0 = hop(tail_0, 2), swap(tail_0)
        other_2, other_3 = swap(mid_2), swap(mid_3)
    n_d, (q_now, q_d), (k_now, k_d), (v_now, v_d), g_d = front(table, x_d, *first_d)
    a_d, *stats_d = attend(q_now, k_now, v_now, marks_d, coef[1])
    if near:
        (tail_1, other_tail_0, other_2, other_3), a_d = tie((tail_1, other_tail_0, other_2, other_3), a_d)
        (a_d, tail_0, tail_1), (other_tail_0, other_2, other_3) = tie(
            (a_d, tail_0, tail_1), (other_tail_0, other_2, other_3)
        )
        mid_pack = ([mid_0, mid_1, mid_2, mid_3], [other_0, other_1, other_2, other_3])
        tail_2, tail_3, other_tail_1 = hop(tail_0, 3), hop(tail_1, 3), swap(tail_1)
    m_e, n1_e, act, slope, end, memory, (mk_now, mem_k), (mv_now, mem_v), m_d, n1_d, (query_now, query), memory_out = mid(
        table, a_e, a_d, x_e, x_d, g_e, g_d, dest_e, *mid_pack
    )
    crossed, *stats_c = attend(query_now, mk_now, mv_now, marks_c, coef[2])
    if near:
        (tail_2, tail_3, other_tail_1), crossed = tie((tail_2, tail_3, other_tail_1), crossed)
        tail_pack = ([tail_0, tail_1, tail_2, tail_3], [other_tail_0, other_tail_1, swap(tail_2), swap(tail_3)])
    stay, leave, second_grad, crossed_grad, gd_two, kept, sent = tail(
        place, section[None], table, crossed, m_d, ct, g_d, dest_d, memory_out, *tail_pack
    )
    pack_a = (kept, sent)
    if near:
        a = [kept, swap(sent)]
    arrived = swap(leave)
    query_grad, mk_grad, mv_grad, ds_c = attend_back(query, mem_k, mem_v, crossed_grad, stats_c, marks_c, coef[2])
    if near:
        query_grad = behind(query_grad, a)
        query_grad, (sent_a, arrived) = tie(query_grad, (total(a, 8, 16), arrived))
        a.append(hop(sent_a, 3))
    md_grad, ad_grad, me_grad, ae_grad, ge_one, kept, sent = mid_back(
        place, table, query_grad, mk_grad, mv_grad, n1_d, m_d, second_grad, a_d, memory, end, act, slope, n1_e, m_e, a_e, g_e, g_d,
        *mid_pack
    )
    pack_b = (kept, sent)
    if near:
        ad_grad = behind(ad_grad, a)
        (ad_grad, sent), sent_a = tie((ad_grad, sent), total(a, 4, 8))
        a.append(hop(sent_a, 2))
        b = [kept, swap(sent)]
    *grads_d, ds_d = attend_back(q_d, k_d, v_d, ad_grad, stats_d, marks_d, coef[1])
    if near:
        grads_d[0] = behind(grads_d[0], a, b)
        ae_grad, (sent_a, sent_b, grads_d[0]) = tie(ae_grad, (total(a, 2, 4), total(b, 8, 16), grads_d[0]))
        a.append(hop(sent_a, 1))
        b.append(hop(sent_b, 3))
    *grads_e, ds_e = attend_back(q_e, k_e, v_e, ae_grad, stats_e, marks_e, coef[0])
    if near:
        grads_e[0] = behind(grads_e[0], a, b)
        (grads_e[0], md_grad), (sent_a, sent_b) = tie((grads_e[0], md_grad), (total(a, 1, 2), total(b, 4, 8)))
        a.append(hop(sent_a, 0))
        b.append(hop(sent_b, 2))
    kept, sent = front_w(place, grads_e, grads_d, n_e, n_d, ge_one, gd_two, (ds_e, ds_d, ds_c))
    if near:
        sent = behind(sent, a, b)
        sent, (sent_b, done_a) = tie(sent, (to_line(b), at_last(a, [])))
        c = [kept, swap(sent)]
        came_b = along_line(sent_b)
        (md_grad, me_grad), sent_c = tie((md_grad, me_grad), total(c, 8, 16))
        c.append(hop(sent_c, 3))
    xd_grad, xe_grad = front_x(
        table, (grads_d, grads_e), (x_d, x_e), (md_grad, me_grad), (g_d, g_e), (dest_d, dest_e), (first_d, first_e)
    )
    if near:
        xd_grad, xe_grad = behind((xd_grad, xe_grad), b, c)
        (sent_c, stay), (xe_grad, came_b) = tie((total(c, 4, 8), stay), (xe_grad, came_b))
        done_b = at_last(b, came_b)
        c.append(hop(sent_c, 2))
        input_grad, outputs = settle(xe_grad, xd_grad), by_micro(stay, arrived)
        enc, dec = low(done_b[0:176]), low(jnp.concatenate([done_a, done_b[176:208]], axis=0))
        parts = (jnp.where(first, enc, dec), swap(jnp.where(first, dec, enc)))
        parts, input_grad, outputs = behind((parts, input_grad, outputs), c)
        *grads, alpha_grad = finish(
            jnp.stack([lax.axis_index("dp"), section]), *parts, at_last(c, along_line(to_line(c))),
            attn_qkv[0], cross_proj[0], gains[0], 0.25 * gate * (1.0 - gate),
        )
    else:
        input_grad, outputs = settle(xe_grad, xd_grad), by_micro(stay, arrived)
        grads, extra = far_shards(pack_a, pack_b, (kept, sent))
        grads += (gain_grads((attn_qkv, cross_proj), (grads[0], grads[2]), gains, extra),)
        alpha_grad = extra[8:16, 0:3].T * 0.25 * gate * (1.0 - gate)
    return (outputs, input_grad) + tuple(g[None] for g in grads) + (alpha_grad,)


def solution(mesh):
    return jax.shard_map(
        local,
        mesh=mesh,
        in_specs=(
            P("section", None, "dp", None, None),
            P(None, "dp", None, None),
            P(None, None, "dp", None),
            P("section", "dp", None),
            P("section", "dp", None),
            P("section", "dp", None),
            P("section", None, "dp"),
            P("section", "dp", None),
            P("section", None, "dp"),
            P(),
        ),
        out_specs=(
            P("section", None, "dp", None, None),
            P("section", None, "dp", None, None),
            P("section", "dp", None),
            P("section", "dp", None),
            P("section", "dp", None),
            P("section", None, "dp"),
            P("section", "dp", None),
            P("section", None, "dp"),
            P(),
        ),
        check_vma=False,
    )
```
